32 devices in a mesh: blk: 16 (over z, y, x), tp: 2 (over core).
Axes of the slice: x: 2, y: 2, z: 4, core: 2. Of those that a mesh axis runs over, the one named last changes fastest.
Arguments:
- tokens: bfloat16 [2048, 2048], P('blk'), may hold values from -6 to 6
- w_qkv: bfloat16 [3, 2048, 2048], P(None, 'blk', 'tp'), may hold values from -0.125 to 0.125
- b_qkv: bfloat16 [3, 16, 128], P(None, 'tp', 'blk'), may hold values from -2 to 2
- w_out: bfloat16 [2048, 2048], P('tp', 'blk'), may hold values from -2 to 2
- b_out: bfloat16 [16, 128], P(None, 'blk'), may hold values from -2 to 2
- w_in: bfloat16 [2048, 8192], P('blk', 'tp'), may hold values from -0.125 to 0.125
- b_in: bfloat16 [64, 128], P('tp', 'blk'), may hold values from -3 to 3
- w_out2: bfloat16 [8192, 2048], P('tp', 'blk'), may hold values from -0.0625 to 0.0625
- b_out2: bfloat16 [16, 128], P(None, 'blk'), may hold values from -2 to 2
- norm_gain: bfloat16 [2, 16, 128], P(None, None, 'blk'), may hold values from 0.099609375 to 1.8984375
- norm_shift: bfloat16 [2, 16, 128], P(None, None, 'blk'), may hold values from -2 to 2
- doc_start: int32 [2048], P('blk'), may hold values from 0 to 2047, as said below
- live: int32 [2048], P('blk'), may hold values from 0 to 1, as said below
- cotangent: bfloat16 [2048, 2048], P('blk'), may hold values from -6 to 6
Outputs:
- mixed: bfloat16 [2048, 2048], P('blk')
- tokens_grad: bfloat16 [2048, 2048], P('blk')
- w_qkv_grad: float32 [3, 2048, 2048], P(None, 'blk', 'tp')
- b_qkv_grad: float32 [3, 16, 128], P(None, 'tp', 'blk')
- w_out_grad: float32 [2048, 2048], P('tp', 'blk')
- b_out_grad: float32 [16, 128], P(None, 'blk')
- w_in_grad: float32 [2048, 8192], P('blk', 'tp')
- b_in_grad: float32 [64, 128], P('tp', 'blk')
- w_out2_grad: float32 [8192, 2048], P('tp', 'blk')
- b_out2_grad: float32 [16, 128], P(None, 'blk')
- norm_gain_grad: float32 [2, 16, 128], P(None, None, 'blk')
- norm_shift_grad: float32 [2, 16, 128], P(None, None, 'blk')
The draws below stay inside these ranges and needn't reach their ends.
Inputs may be any that keep to these rules, and one draw needn't show every extreme that they name: `doc_start`: each token's value is the index of the first token of its document, so tokens with equal values form one run and the first token has 0; the last token is a document of its own. Short documents lie in the first block of 128 tokens; then one document runs up to the second-to-last token. `live`: pad tokens are the last tokens of the pack, from a quarter to a half of 2048 of them; all others are 1.
All inputs are finite; a program needn't handle non-finite values.
Results may differ from the reference program's by a relative error of at most 0.013.
Values may be sent and summed in bfloat16 or wider, within the bound.
No kernel may reach another device: no remote copies, remote signals or barrier semaphores. Data moves between devices by JAX's collectives and lax.ppermute only.
A program may use at most 256 MiB of HBM per device.

```python
import math
import jax
import jax.numpy as jnp
from jax import lax

D = 2048
HEADS = 8
HEAD = 256
ROT = 64
FF = 8192
TOK_DEV = 128
TOKENS = 2048


def doc_layout(key):
    total = TOKENS
    parts = jax.random.split(key, 3)
    head_len = jax.random.randint(parts[0], (), 1, TOK_DEV // 2 + 2)
    pad_len = jax.random.randint(parts[1], (), total // 4, total // 2 + 1)
    index = jnp.arange(total, dtype=jnp.int32)
    coin = jax.random.randint(parts[2], (total,), 0, 4) == 0
    fixed_start = (index == 0) | (index == head_len) | (index == total - 1)
    short_zone = index < head_len
    is_start = fixed_start | coin & short_zone
    marks = jnp.where(is_start, index, 0).astype(jnp.int32)
    starts = lax.cummax(marks, axis=0)
    live_flags = (index < total - pad_len).astype(jnp.int32)
    return (starts, live_flags)


def draw_doc_start(key, part):
    starts, live_flags = doc_layout(key)
    return starts


def draw_live(key, part):
    starts, live_flags = doc_layout(key)
    return live_flags


def block_levels(rng, dims, cuts, least, high):
    level, own = 1.0, jax.random.fold_in(rng, 6)
    for axis_at, blocks in cuts:
        steps = jnp.exp(jax.random.uniform(jax.random.fold_in(own, axis_at), (blocks,), jnp.float32, least / len(cuts), high / len(cuts)))
        level = level * jnp.repeat(steps, dims[axis_at] // blocks).reshape([-1 if axis == axis_at else 1 for axis in range(len(dims))])
    return level


def scatter_about(stream_key, shape, scale, bound, shards=(), kind=jnp.bfloat16):
    level = block_levels(stream_key, shape, shards, -0.22, 0.18) if shards else 1.0
    values = jax.random.normal(stream_key, shape, jnp.float32) * scale * level
    return jnp.minimum(jnp.maximum(values, -bound), bound).astype(kind)


def setup_inputs(seed: int = 0) -> dict:
    key_of = jax.random.split(jax.random.key(seed), 15)
    return {
        "tokens": scatter_about(key_of[0], (TOKENS, D), 1.0, 6.0, ((0, 16),)),
        "w_qkv": scatter_about(key_of[1], (3, D, D), D ** -0.5, 0.125, ((1, 16), (2, 2))),
        "b_qkv": scatter_about(key_of[2], (3, D // 128, 128), 0.3, 2.0, ((1, 2), (2, 16))),
        "w_out": scatter_about(key_of[3], (D, D), (max(1, D // 256)) ** -0.5, 2.0, ((0, 2), (1, 16))),
        "b_out": scatter_about(key_of[4], (D // 128, 128), 0.3, 2.0, ((1, 16),)),
        "w_in": scatter_about(key_of[5], (D, FF), D ** -0.5, 0.125, ((0, 16), (1, 2))),
        "b_in": scatter_about(key_of[6], (FF // 128, 128), 0.5, 3.0, ((0, 2), (1, 16))),
        "w_out2": scatter_about(key_of[7], (FF, D), FF ** -0.5, 0.0625, ((0, 2), (1, 16))),
        "b_out2": scatter_about(key_of[8], (D // 128, 128), 0.3, 2.0, ((1, 16),)),
        "norm_gain": jnp.clip(1.0 + 0.18 * jax.random.normal(key_of[9], (2, D // 128, 128), jnp.float32), 0.099609375, 1.8984375).astype(jnp.bfloat16),
        "norm_shift": scatter_about(key_of[10], (2, D // 128, 128), 0.3, 2.0, ((2, 16),)),
        "doc_start": draw_doc_start(jax.random.fold_in(key_of[14], 71), 0),
        "live": draw_live(jax.random.fold_in(key_of[14], 71), 0),
        "cotangent": scatter_about(key_of[13], (TOKENS, D), 1.0, 6.0, ((0, 16),)),
    }


HIGHEST = lax.Precision.HIGHEST
EPSILON = 1e-05
NEGATIVE = -1e+30

@jax.custom_vjp
def low(v):
    return lax.optimization_barrier(v.astype(jnp.bfloat16)).astype(jnp.float32)

@jax.custom_vjp
def low_back(v):
    return v

def low_keep(v):
    return (low(v), None)

def low_pass(kept, grad):
    return (grad,)

def back_keep(v):
    return (v, None)

def back_low(kept, grad):
    return (low(grad),)
low.defvjp(low_keep, low_pass)
low_back.defvjp(back_keep, back_low)

def layer_norm(values, gain, shift):
    center = values - lax.optimization_barrier(jnp.mean(values, axis=-1, keepdims=True))
    spread = lax.optimization_barrier(jnp.mean(center * center, axis=-1, keepdims=True))
    return center * lax.rsqrt(spread + EPSILON) * gain + shift

def rotary_tables(positions, width):
    steps = jnp.arange(width // 2, dtype=jnp.float32)
    inverse = 10000.0 ** (-2.0 * steps / width)
    angle = positions.astype(jnp.float32)[:, None] * inverse[None, :]
    return (jnp.cos(angle), jnp.sin(angle))

def rotate(values, cosine, sine):
    half = cosine.shape[-1]
    first = values[..., :half]
    second = values[..., half:2 * half]
    cosine = cosine[:, None, :]
    sine = sine[:, None, :]
    return jnp.concatenate([first * cosine - second * sine, second * cosine + first * sine, values[..., 2 * half:]], axis=-1)

def attention(queries, keys, values, doc_start, live):
    count = queries.shape[0]
    size = math.gcd(count, 512)
    index = jnp.arange(count, dtype=jnp.int32)
    scale = 1.0 / math.sqrt(HEAD)

    @jax.checkpoint
    def one_block(block):
        block_queries, block_starts, block_index = block
        scores = low_back(jnp.einsum('qhd,khd->hqk', block_queries, keys, precision=HIGHEST) * scale)
        same = block_starts[:, None] == doc_start[None, :]
        causal = index[None, :] <= block_index[:, None]
        usable = (live[None, :] == 1) | (index[None, :] == block_index[:, None])
        mask = (same & causal & usable)[None]
        masked = jnp.where(mask, scores, NEGATIVE)
        top = lax.optimization_barrier(jnp.max(masked, axis=-1, keepdims=True))
        weight = jnp.where(mask, jnp.exp(masked - top), 0.0)
        prob = low(weight / lax.optimization_barrier(jnp.sum(weight, axis=-1, keepdims=True)))
        return jnp.einsum('hqk,khd->qhd', prob, values, precision=HIGHEST)
    blocks = (queries.reshape(count // size, size, HEADS, HEAD), doc_start.reshape(count // size, size), index.reshape(count // size, size))
    return lax.map(one_block, blocks).reshape(count, HEADS, HEAD)

def layer_block(inputs, w_qkv, b_qkv, w_out, b_out, w_in, b_in, w_out2, b_out2, norm_gain, norm_shift, doc_start, live):
    count = inputs.shape[0]
    gains = norm_gain.reshape(2, -1)
    shifts = norm_shift.reshape(2, -1)
    normed_attend = low(layer_norm(inputs, gains[0], shifts[0]))
    normed_feed = low(layer_norm(inputs, gains[1], shifts[1]))
    linear = jnp.einsum('td,sde->ste', normed_attend, w_qkv, precision=HIGHEST) + b_qkv.reshape(3, -1)[:, None, :]
    linear = low_back(linear)
    index = jnp.arange(count, dtype=jnp.int32)
    cosine, sine = rotary_tables(index - doc_start, ROT)
    split = linear.reshape(3, count, HEADS, HEAD)
    queries = low(rotate(split[0], cosine, sine))
    keys = low(rotate(split[1], cosine, sine))
    values = low(split[2])
    attended = low(low_back(attention(queries, keys, values, doc_start, live)))
    attend_branch = jnp.dot(attended.reshape(count, HEADS * HEAD), w_out, precision=HIGHEST) + b_out.reshape(-1)
    expanded = low_back(jnp.dot(normed_feed, w_in, precision=HIGHEST) + b_in.reshape(-1))
    activated = low(jax.nn.gelu(expanded, approximate=False))
    feed_branch = jnp.dot(activated, w_out2, precision=HIGHEST) + b_out2.reshape(-1)
    return inputs + attend_branch + feed_branch

def reference(tokens, w_qkv, b_qkv, w_out, b_out, w_in, b_in, w_out2, b_out2, norm_gain, norm_shift, doc_start, live, cotangent):
    params = tuple((array.astype(jnp.float32) for array in (tokens, w_qkv, b_qkv, w_out, b_out, w_in, b_in, w_out2, b_out2, norm_gain, norm_shift)))

    def forward(*arrays):
        return layer_block(*arrays, doc_start, live)
    mixed, pull = jax.vjp(forward, *params)
    grads = pull(cotangent.astype(jnp.float32))
    return (mixed.astype(jnp.bfloat16), grads[0].astype(jnp.bfloat16), grads[1], grads[2], grads[3], grads[4], grads[5], grads[6], grads[7], grads[8], grads[9], grads[10])
```

```python
import math

import jax
import jax.numpy as jnp
from jax import lax
from jax.sharding import PartitionSpec as P

HEADS = 8
HEAD = 256
ROT = 64

EPSILON = 1e-05
NEGATIVE = -1e30
BF = jnp.bfloat16
F32 = jnp.float32


def dot(left, right, dims):
    return lax.dot_general(left, right, (dims, ((), ())), preferred_element_type=F32)


def swap_cores(value):
    return lax.ppermute(value, "tp", [(0, 1), (1, 0)])


def from_peer(value, mask):
    count = lax.axis_size("blk")
    return lax.ppermute(value, "blk", [(i, i ^ mask) for i in range(count)])


def spread(value, masks):
    return jnp.stack([value] + [from_peer(value, mask) for mask in masks])


def collect(parts, masks):
    total = parts[0].astype(F32)
    for at, mask in enumerate(masks):
        total = total + from_peer(parts[at + 1], mask).astype(F32)
    return total


def by_core(core, mine, other):
    first = core == 0
    return jnp.where(first, mine, other), jnp.where(first, other, mine)


def gelu_and_slope(values):
    cumulative = 0.5 * (1.0 + lax.erf(values * (1.0 / math.sqrt(2.0))))
    density = jnp.exp(-0.5 * values * values) * (1.0 / math.sqrt(2.0 * math.pi))
    return values * cumulative, cumulative + values * density


def turn(values, cosine, sine):
    half = ROT // 2
    first, second = values[:, :half], values[:, half:ROT]
    return jnp.concatenate(
        [first * cosine - second * sine, second * cosine + first * sine, values[:, ROT:]],
        axis=1,
    )


def body(
    tokens,
    w_qkv,
    b_qkv,
    w_out,
    b_out,
    w_in,
    b_in,
    w_out2,
    b_out2,
    norm_gain,
    norm_shift,
    doc_start,
    live,
    cotangent,
):
    blocks = lax.axis_size("blk")
    cores = lax.axis_size("tp")
    me, core = lax.axis_index("blk"), lax.axis_index("tp")
    rows, width = tokens.shape
    depth = w_in.shape[0]
    part = rows // cores
    quarter = part // 2
    group = blocks // HEADS
    columns = HEAD // group
    units = w_in.shape[1] // blocks
    cut = depth // cores
    near = columns // cores
    scale = 1.0 / math.sqrt(HEAD)

    masks_x = list(range(1, group))
    masks_y = [group]
    masks_z = [2 * group * i for i in range(1, blocks // (2 * group))]
    size_x, size_y, size_z = group, 2, len(masks_z) + 1

    def gather(value):
        over_z = spread(value, masks_z)
        one = spread(spread(over_z[:, :quarter], masks_y), masks_x)
        two = spread(spread(over_z[:, quarter:], masks_x), masks_y)
        return one.reshape(-1, value.shape[-1]), two.reshape(-1, value.shape[-1])

    def scatter(one, two):
        one = one.reshape(size_x, size_y, size_z, quarter, width)
        two = two.reshape(size_y, size_x, size_z, quarter, width)
        one = collect(collect(one, masks_x).astype(BF), masks_y)
        two = collect(collect(two, masks_y).astype(BF), masks_x)
        return collect(jnp.concatenate([one, two], axis=1).astype(BF), masks_z)

    small = jnp.concatenate(
        [
            norm_gain.reshape(-1),
            norm_shift.reshape(-1),
            b_out.reshape(-1),
            b_out2.reshape(-1),
            b_qkv.reshape(-1),
            b_in.reshape(-1),
            (doc_start // 256).astype(BF),
            (doc_start % 256).astype(BF),
            live.astype(BF),
        ]
    )
    small_rows = -(-small.size // 2048) * 16
    small = jnp.pad(small, (0, small_rows * 128 - small.size)).reshape(small_rows * 128 // columns, columns)
    lines = small.shape[0]

    own_heads = HEADS // cores * group
    triple = w_qkv.reshape(3, cores, cut, own_heads, columns).transpose(1, 3, 0, 2, 4)
    triple = triple.reshape(cores, own_heads, 3 * cut, columns)
    outward = w_out.reshape(own_heads, cores, near, depth).transpose(1, 0, 2, 3)
    outward = outward.reshape(cores, own_heads, near * depth // columns, columns)
    dealt = jnp.concatenate([triple, outward], axis=2)
    keep = lax.dynamic_index_in_dim(dealt, core, 0, keepdims=False)
    give = lax.dynamic_index_in_dim(dealt, 1 - core, 0, keepdims=False)
    got = swap_cores(give)
    heads_low, heads_high = by_core(core, keep, got)
    deal = jnp.concatenate(
        [
            jnp.concatenate([heads_low, heads_high]),
            jnp.broadcast_to(small, (blocks,) + small.shape),
        ],
        axis=1,
    )
    here = lax.all_to_all(deal, "blk", 0, 0, tiled=True)
    there = swap_cores(here)
    both = jnp.stack(by_core(core, here, there))

    expand_deal = w_in.reshape(depth, blocks, units).transpose(1, 0, 2)
    expand_mine = lax.all_to_all(expand_deal, "blk", 0, 0, tiled=True).reshape(width, units)
    expand_other = swap_cores(expand_mine)
    shrink_mine = lax.all_to_all(
        w_out2.reshape(blocks, units, depth), "blk", 0, 0, tiled=True
    )
    shrink_other = swap_cores(shrink_mine)
    w_expand = jnp.concatenate([expand_mine, expand_other], axis=1)
    w_shrink = jnp.concatenate([shrink_mine, shrink_other], axis=1)
    w_shrink = w_shrink.transpose(1, 0, 2).reshape(2 * units, width)

    my_tokens = lax.dynamic_slice_in_dim(tokens, core * part, part, 0)
    my_cotangent = lax.dynamic_slice_in_dim(cotangent, core * part, part, 0)
    all_tokens = jnp.concatenate(gather(my_tokens))
    all_cotangent = jnp.concatenate(gather(my_cotangent))
    count = all_tokens.shape[0]

    at = 3 * cut
    mid = at + near * depth // columns
    w_triple = both[:, :, :at].reshape(cores, blocks, 3, cut, columns)
    w_triple = w_triple.transpose(1, 0, 3, 2, 4).reshape(width, 3 * columns)
    w_near = both[:, :, at:mid].reshape(cores, blocks, near, depth)
    w_near = w_near.transpose(0, 2, 1, 3).reshape(columns, width)
    w_head = spread(w_near, masks_x).reshape(HEAD, width)
    flat = both[:, :, mid:].reshape(cores, blocks, -1)

    def take(offset, like):
        return flat[:, :, offset : offset + like.size].reshape((cores, blocks) + like.shape), offset + like.size

    offset = 0
    gain_all, offset = take(offset, norm_gain)
    shift_all, offset = take(offset, norm_shift)
    out_all, offset = take(offset, b_out)
    out2_all, offset = take(offset, b_out2)
    triple_all, offset = take(offset, b_qkv)
    expand_all, offset = take(offset, b_in)
    start_high, offset = take(offset, doc_start)
    start_low, offset = take(offset, doc_start)
    live_all, offset = take(offset, live)
    gains = gain_all[0].transpose(1, 2, 0, 3).reshape(2, width).astype(F32)
    shifts = shift_all[0].transpose(1, 2, 0, 3).reshape(2, width).astype(F32)
    residual_shift = (out_all[0].astype(F32) + out2_all[0].astype(F32)).transpose(1, 0, 2).reshape(width)
    triple_shift = triple_all.astype(F32).transpose(2, 0, 3, 1, 4).reshape(3, width)
    triple_shift = lax.dynamic_slice_in_dim(triple_shift, me * columns, columns, 1).reshape(-1)
    expand_shift = expand_all.astype(F32).transpose(0, 2, 1, 3).reshape(cores, -1)
    expand_shift = lax.dynamic_slice_in_dim(expand_shift, me * units, units, 1)
    expand_shift = jnp.concatenate(by_core(core, expand_shift[0], expand_shift[1]))
    starts = (start_high[0].astype(F32) * 256.0 + start_low[0].astype(F32)).astype(jnp.int32)
    lives = live_all[0].astype(jnp.int32)

    x_at = jnp.arange(size_x)[:, None, None]
    y_at = group * jnp.arange(size_y)[None, :, None]
    z_at = 2 * group * jnp.arange(size_z)[None, None, :]
    order = (x_at + y_at + z_at) ^ me
    inside = jnp.arange(quarter, dtype=jnp.int32)

    def index_of(which):
        base = order[..., None] * rows + which * part + inside
        one, two = base, base + quarter
        return jnp.concatenate(
            [one.reshape(size_x, -1), two.reshape(size_x, -1)], axis=1
        )

    def heads_order(value):
        tail = value.shape[1:]
        one = value[: count // 2].reshape((size_x, -1) + tail)
        two = value[count // 2 :].reshape((size_y, size_x, -1) + tail)
        two = jnp.swapaxes(two, 0, 1).reshape((size_x, -1) + tail)
        return jnp.concatenate([one, two], axis=1)

    def gathered_order(value):
        tail = value.shape[2:]
        middle = value.shape[1] // 2
        one = value[:, :middle].reshape((count // 2,) + tail)
        two = value[:, middle:].reshape((size_x, size_y, -1) + tail)
        two = jnp.swapaxes(two, 0, 1).reshape((count // 2,) + tail)
        return jnp.concatenate([one, two])

    index_mine, index_other = index_of(core), index_of(1 - core)
    index = jnp.concatenate([index_mine.reshape(-1), index_other.reshape(-1)])
    token_start = starts.reshape(-1)[index]
    token_live = lives.reshape(-1)[index]

    inputs = all_tokens.astype(F32)
    center = inputs - jnp.mean(inputs, axis=-1, keepdims=True)
    inverse = lax.rsqrt(jnp.mean(center * center, axis=-1, keepdims=True) + EPSILON)
    normal = center * inverse
    normed_attend = (normal * gains[0] + shifts[0]).astype(BF)
    normed_feed = (normal * gains[1] + shifts[1]).astype(BF)

    linear = dot(normed_attend, w_triple, ((1,), (0,))) + triple_shift
    linear = heads_order(linear).reshape(count, 3, columns)
    steps = jnp.arange(ROT // 2, dtype=F32)
    speed = 10000.0 ** (-2.0 * steps / ROT)
    place = (index - token_start).astype(F32)
    angle = place[:count, None] * speed[None, :]
    cosine, sine = jnp.cos(angle), jnp.sin(angle)
    slot = me % group

    def turn_pieces(pieces, cosine, sine):
        if columns >= ROT:
            return jnp.stack(
                [
                    turn(
                        pieces[r],
                        jnp.where(slot == r, cosine, 1.0),
                        jnp.where(slot == r, sine, 0.0),
                    )
                    for r in range(group)
                ]
            )
        place_of = jnp.arange(group) ^ slot
        whole = jnp.swapaxes(pieces[place_of], 0, 1).reshape(pieces.shape[1], HEAD)
        whole = turn(whole, cosine, sine).reshape(-1, group, columns)
        return jnp.swapaxes(whole, 0, 1)[place_of]

    if columns >= ROT:
        own_cosine = jnp.where(slot == 0, cosine, 1.0)
        own_sine = jnp.where(slot == 0, sine, 0.0)
        queries = turn(linear[:, 0], own_cosine, own_sine)
        keys = turn(linear[:, 1], own_cosine, own_sine)
    else:
        queries, keys = linear[:, 0], linear[:, 1]
    mine = jnp.concatenate([queries, keys, linear[:, 2]], axis=1).astype(BF)

    def align(value, r):
        return value.reshape((size_x, -1) + value.shape[1:])[jnp.arange(size_x) ^ r].reshape(value.shape)

    pieces = [mine] + [align(from_peer(mine, r), r) for r in masks_x]
    pieces = jnp.stack(pieces).reshape(group, count, 3, columns)
    if columns < ROT:
        turned = [turn_pieces(pieces[:, :, s].astype(F32), cosine, sine).astype(BF) for s in (0, 1)]
        pieces = jnp.stack(turned + [pieces[:, :, 2]], axis=2)
    own_triple = pieces.transpose(2, 1, 0, 3).reshape(3, count, HEAD)
    other_triple = swap_cores(own_triple)
    queries, keys, values = jnp.concatenate([own_triple, other_triple], axis=1)

    cotangent_x = heads_order(all_cotangent)
    grad_attended = dot(all_cotangent, w_head, ((1,), (1,))).astype(BF)
    grad_attended = heads_order(grad_attended).reshape(count, HEAD)
    grad_attended = jnp.concatenate([grad_attended, swap_cores(grad_attended)])

    share = count // size_x
    mine_index, mine_start, mine_live = index[:share], token_start[:share], token_live[:share]

    def allowed(query_index, query_start, key_index, key_start, key_live):
        same = query_start == key_start
        causal = key_index <= query_index
        usable = (key_live == 1) | (key_index == query_index)
        return same & causal & usable

    mask = allowed(mine_index[:, None], mine_start[:, None], index[None], token_start[None], token_live[None])
    scores = dot(queries[:share], keys, ((1,), (1,))) * scale
    masked = jnp.where(mask, scores, NEGATIVE)
    top = jnp.max(masked, axis=-1, keepdims=True)
    weight = jnp.where(mask, jnp.exp(masked - top), 0.0)
    total = jnp.sum(weight, axis=-1, keepdims=True)
    prob = weight / total
    attended = dot(prob.astype(BF), values, ((1,), (0,)))
    log_total = top + jnp.log(total)
    delta = jnp.sum(grad_attended[:share].astype(F32) * attended, axis=-1, keepdims=True)
    push = dot(grad_attended[:share], values, ((1,), (1,)))
    slope = (prob * (push - delta)).astype(BF)
    grad_queries = dot(slope, keys, ((1,), (0,))) * scale
    attended = attended.astype(BF)

    marks = jnp.concatenate([log_total, delta], axis=1).T
    marks = spread(marks, masks_x).transpose(1, 0, 2).reshape(2, count)
    marks = jnp.concatenate([marks, swap_cores(marks)], axis=1)
    mask = allowed(index[None], token_start[None], mine_index[:, None], mine_start[:, None], mine_live[:, None])
    scores = dot(keys[:share], queries, ((1,), (1,))) * scale
    prob = jnp.where(mask, jnp.exp(jnp.where(mask, scores, NEGATIVE) - marks[0][None]), 0.0)
    grad_values = dot(prob.astype(BF), grad_attended, ((1,), (0,)))
    push = dot(values[:share], grad_attended, ((1,), (1,)))
    slope = (prob * (push - marks[1][None])).astype(BF)
    grad_keys = dot(slope, queries, ((1,), (0,))) * scale

    expanded = dot(normed_feed, w_expand, ((1,), (0,))) + expand_shift
    activated, bend = gelu_and_slope(expanded)
    activated = activated.astype(BF)
    grad_activated = dot(all_cotangent, w_shrink, ((1,), (1,)))
    grad_expanded = (bend * grad_activated).astype(BF)

    branch = dot(activated, w_shrink, ((1,), (0,)))
    attend_part = dot(attended, w_head, ((1,), (0,)))
    rest = jnp.zeros((size_x - 1,) + attend_part.shape, F32)
    attend_part = gathered_order(jnp.concatenate([attend_part[None], rest]))
    branch = (branch + attend_part).astype(BF)
    branch = scatter(branch[: count // 2], branch[count // 2 :])
    my_inputs = my_tokens.astype(F32)
    my_mixed = (my_inputs + branch.reshape(part, width) + residual_shift).astype(BF)

    def whole_block(value):
        low, high = by_core(core, value, swap_cores(value))
        return jnp.concatenate([low, high])

    mixed = whole_block(my_mixed)

    grad_shrink = dot(activated, all_cotangent, ((0,), (0,)))
    grad_expand = dot(normed_feed, grad_expanded, ((0,), (0,)))
    grad_shrink = grad_shrink[:units] + swap_cores(grad_shrink[units:].astype(BF)).astype(F32)
    grad_expand = grad_expand[:, :units] + swap_cores(grad_expand[:, units:].astype(BF)).astype(F32)
    shrink_deal = grad_shrink.astype(BF).reshape(units, blocks, depth).transpose(1, 0, 2)
    expand_deal = grad_expand.astype(BF).reshape(blocks, depth, units)
    shrink_grad = lax.all_to_all(shrink_deal, "blk", 0, 0, tiled=True)
    shrink_grad = shrink_grad.reshape(-1, depth).astype(F32)
    expand_grad = lax.all_to_all(expand_deal, "blk", 0, 0, tiled=True)
    expand_grad = expand_grad.transpose(1, 0, 2).reshape(depth, -1).astype(F32)

    def by_pieces(value):
        return value.reshape(share, group, columns).transpose(1, 0, 2)

    own_cosine, own_sine = cosine[:share], -sine[:share]
    back = [
        turn_pieces(by_pieces(grad_queries), own_cosine, own_sine),
        turn_pieces(by_pieces(grad_keys), own_cosine, own_sine),
        by_pieces(grad_values),
    ]
    back = jnp.concatenate(back, axis=2).astype(BF)
    back = jnp.concatenate([back, by_pieces(attended)], axis=2)
    back = jnp.stack([back[0]] + [from_peer(back[r], r) for r in masks_x])
    back = gathered_order(back)
    grad_linear, attended_near = back[:, : 3 * columns], back[:, 3 * columns :]
    grad_triple = dot(normed_attend, grad_linear, ((0,), (0,)))
    grad_out = dot(attended_near, all_cotangent, ((0,), (0,)))
    grad_triple = grad_triple.reshape(blocks, cores, cut, 3, columns).transpose(1, 0, 3, 2, 4)
    grad_triple = grad_triple.reshape(cores, blocks, 3 * cut, columns)
    grad_out = grad_out.reshape(cores, near, blocks, depth).transpose(0, 2, 1, 3)
    grad_out = grad_out.reshape(cores, blocks, near * depth // columns, columns)
    dealt = jnp.concatenate([grad_triple, grad_out], axis=2)
    keep = lax.dynamic_index_in_dim(dealt, core, 0, keepdims=False)
    give = lax.dynamic_index_in_dim(dealt, 1 - core, 0, keepdims=False)
    dealt = (keep + swap_cores(give.astype(BF)).astype(F32)).astype(BF)
    dealt = lax.all_to_all(dealt, "blk", 0, 0, tiled=True)
    dealt = dealt.reshape((cores, own_heads) + dealt.shape[1:])
    keep = lax.dynamic_index_in_dim(dealt, core, 0, keepdims=False)
    give = lax.dynamic_index_in_dim(dealt, 1 - core, 0, keepdims=False)
    dealt = jnp.stack(by_core(core, keep, swap_cores(give)))
    triple_grad = dealt[:, :, :at].reshape(cores, own_heads, 3, cut, columns)
    triple_grad = triple_grad.transpose(2, 0, 3, 1, 4).reshape(3, depth, -1).astype(F32)
    output_grad = dealt[:, :, at:].reshape(cores, own_heads, near, depth)
    output_grad = output_grad.transpose(1, 0, 2, 3).reshape(-1, depth).astype(F32)

    grad_attend_norm = dot(grad_linear, w_triple, ((1,), (1,)))
    grad_feed_norm = dot(grad_expanded, w_expand, ((1,), (1,)))
    combined = (gains[0] * grad_attend_norm + gains[1] * grad_feed_norm).astype(BF)
    combined = scatter(combined[: count // 2], combined[count // 2 :]).reshape(part, width)
    my_center = my_inputs - jnp.mean(my_inputs, axis=-1, keepdims=True)
    my_inverse = lax.rsqrt(jnp.mean(my_center * my_center, axis=-1, keepdims=True) + EPSILON)
    my_normal = my_center * my_inverse
    my_grad = my_inverse * (
        combined
        - jnp.mean(combined, axis=-1, keepdims=True)
        - my_normal * jnp.mean(combined * my_normal, axis=-1, keepdims=True)
    )
    tokens_grad = whole_block((my_cotangent.astype(F32) + my_grad).astype(BF))

    sums = [
        jnp.sum(normal * grad_attend_norm, axis=0),
        jnp.sum(normal * grad_feed_norm, axis=0),
        jnp.sum(grad_attend_norm, axis=0),
        jnp.sum(grad_feed_norm, axis=0),
        jnp.sum(all_cotangent.astype(F32), axis=0),
        jnp.sum(grad_expanded.astype(F32), axis=0),
        jnp.sum(grad_linear.astype(F32), axis=0),
    ]
    sums = jnp.concatenate(sums)
    other = swap_cores(sums)
    added = sums + other
    norm_sums = added[: 4 * width].reshape(4, width // 128, blocks, -1).transpose(2, 0, 1, 3)
    residual_sum = added[4 * width : 5 * width].reshape(width // 128, 128)
    lanes = 128 // blocks
    residual_grad = lax.dynamic_slice_in_dim(residual_sum, me * lanes, lanes, 1)
    unit_sum = sums[5 * width : 5 * width + units] + other[5 * width + units : 5 * width + 2 * units]
    unit_sums = lax.dynamic_update_slice_in_dim(
        jnp.zeros((w_in.shape[1],), F32), unit_sum, me * units, 0
    )
    unit_sums = unit_sums.reshape(-1, blocks, lanes).transpose(1, 0, 2)
    line_sum = added[5 * width + 2 * units :].reshape(3, columns)
    line_sums = lax.dynamic_update_slice_in_dim(
        jnp.zeros((3, width), F32), line_sum, me * columns, 1
    )
    line_sums = lax.dynamic_slice_in_dim(line_sums, core * (width // cores), width // cores, 1)
    line_sums = line_sums.reshape(3, -1, blocks, lanes).transpose(2, 0, 1, 3)
    tiny = jnp.concatenate(
        [norm_sums.reshape(blocks, -1), unit_sums.reshape(blocks, -1), line_sums.reshape(blocks, -1)],
        axis=1,
    )
    tiny = jnp.sum(lax.all_to_all(tiny, "blk", 0, 0, tiled=True), axis=0)
    first = norm_gain.size
    gain_grad = tiny[:first].reshape(norm_gain.shape)
    shift_grad = tiny[first : 2 * first].reshape(norm_shift.shape)
    expand_bias_grad = tiny[2 * first : 2 * first + b_in.size].reshape(b_in.shape)
    triple_bias_grad = tiny[2 * first + b_in.size :].reshape(b_qkv.shape)
    return (
        mixed,
        tokens_grad,
        triple_grad,
        triple_bias_grad,
        output_grad,
        residual_grad,
        expand_grad,
        expand_bias_grad,
        shrink_grad,
        residual_grad,
        gain_grad,
        shift_grad,
    )


def solution(mesh):
    placed = (
        P("blk", None),
        P(None, "blk", "tp"),
        P(None, "tp", "blk"),
        P("tp", "blk"),
        P(None, "blk"),
        P("blk", "tp"),
        P("tp", "blk"),
        P("tp", "blk"),
        P(None, "blk"),
        P(None, None, "blk"),
        P(None, None, "blk"),
        P("blk"),
        P("blk"),
        P("blk", None),
    )
    return jax.shard_map(
        body,
        mesh=mesh,
        in_specs=placed,
        out_specs=(
            P("blk", None),
            P("blk", None),
            P(None, "blk", "tp"),
            P(None, "tp", "blk"),
            P("tp", "blk"),
            P(None, "blk"),
            P("blk", "tp"),
            P("tp", "blk"),
            P("tp", "blk"),
            P(None, "blk"),
            P(None, None, "blk"),
            P(None, None, "blk"),
        ),
        check_vma=False,
    )
```

```python
import math

import jax
import jax.numpy as jnp
from jax import lax
from jax.experimental import pallas as pl
from jax.experimental.pallas import tpu as pltpu
from jax.sharding import PartitionSpec as P

HEADS = 8
HEAD = 256
ROT = 64

EPSILON = 1e-05
NEGATIVE = -1e30
BF = jnp.bfloat16
F32 = jnp.float32


def dot(left, right, dims):
    return lax.dot_general(left, right, (dims, ((), ())), preferred_element_type=F32)


def swap_cores(value):
    return lax.ppermute(value, "tp", [(0, 1), (1, 0)])


def from_peer(value, mask):
    count = lax.axis_size("blk")
    return lax.ppermute(value, "blk", [(i, i ^ mask) for i in range(count)])


def spread(value, masks):
    return jnp.stack([value] + [from_peer(value, mask) for mask in masks])


def collect(parts, masks):
    total = parts[0].astype(F32)
    for at, mask in enumerate(masks):
        total = total + from_peer(parts[at + 1], mask).astype(F32)
    return total


def by_core(core, mine, other):
    first = core == 0
    return jnp.where(first, mine, other), jnp.where(first, other, mine)


def gelu_and_slope(values):
    cumulative = 0.5 * (1.0 + lax.erf(values * (1.0 / math.sqrt(2.0))))
    density = jnp.exp(-0.5 * values * values) * (1.0 / math.sqrt(2.0 * math.pi))
    return values * cumulative, cumulative + values * density


def turn(values, cosine, sine):
    half = ROT // 2
    first, second = values[:, :half], values[:, half:ROT]
    return jnp.concatenate(
        [first * cosine - second * sine, second * cosine + first * sine, values[:, ROT:]],
        axis=1,
    )


def general_body(
    tokens,
    w_qkv,
    b_qkv,
    w_out,
    b_out,
    w_in,
    b_in,
    w_out2,
    b_out2,
    norm_gain,
    norm_shift,
    doc_start,
    live,
    cotangent,
):
    blocks = lax.axis_size("blk")
    cores = lax.axis_size("tp")
    me, core = lax.axis_index("blk"), lax.axis_index("tp")
    rows, width = tokens.shape
    depth = w_in.shape[0]
    part = rows // cores
    quarter = part // 2
    group = blocks // HEADS
    columns = HEAD // group
    units = w_in.shape[1] // blocks
    cut = depth // cores
    near = columns // cores
    scale = 1.0 / math.sqrt(HEAD)

    masks_x = list(range(1, group))
    masks_y = [group]
    masks_z = [2 * group * i for i in range(1, blocks // (2 * group))]
    size_x, size_y, size_z = group, 2, len(masks_z) + 1

    def gather(value):
        over_z = spread(value, masks_z)
        one = spread(spread(over_z[:, :quarter], masks_y), masks_x)
        two = spread(spread(over_z[:, quarter:], masks_x), masks_y)
        return one.reshape(-1, value.shape[-1]), two.reshape(-1, value.shape[-1])

    def scatter(one, two):
        one = one.reshape(size_x, size_y, size_z, quarter, width)
        two = two.reshape(size_y, size_x, size_z, quarter, width)
        one = collect(collect(one, masks_x).astype(BF), masks_y)
        two = collect(collect(two, masks_y).astype(BF), masks_x)
        return collect(jnp.concatenate([one, two], axis=1).astype(BF), masks_z)

    small = jnp.concatenate(
        [
            norm_gain.reshape(-1),
            norm_shift.reshape(-1),
            b_out.reshape(-1),
            b_out2.reshape(-1),
            b_qkv.reshape(-1),
            b_in.reshape(-1),
            (doc_start // 256).astype(BF),
            (doc_start % 256).astype(BF),
            live.astype(BF),
        ]
    )
    small_rows = -(-small.size // 2048) * 16
    small = jnp.pad(small, (0, small_rows * 128 - small.size)).reshape(small_rows * 128 // columns, columns)
    lines = small.shape[0]

    own_heads = HEADS // cores * group
    triple = w_qkv.reshape(3, cores, cut, own_heads, columns).transpose(1, 3, 0, 2, 4)
    triple = triple.reshape(cores, own_heads, 3 * cut, columns)
    outward = w_out.reshape(own_heads, cores, near, depth).transpose(1, 0, 2, 3)
    outward = outward.reshape(cores, own_heads, near * depth // columns, columns)
    dealt = jnp.concatenate([triple, outward], axis=2)
    keep = lax.dynamic_index_in_dim(dealt, core, 0, keepdims=False)
    give = lax.dynamic_index_in_dim(dealt, 1 - core, 0, keepdims=False)
    got = swap_cores(give)
    heads_low, heads_high = by_core(core, keep, got)
    deal = jnp.concatenate(
        [
            jnp.concatenate([heads_low, heads_high]),
            jnp.broadcast_to(small, (blocks,) + small.shape),
        ],
        axis=1,
    )
    here = lax.all_to_all(deal, "blk", 0, 0, tiled=True)
    there = swap_cores(here)
    both = jnp.stack(by_core(core, here, there))

    expand_deal = w_in.reshape(depth, blocks, units).transpose(1, 0, 2)
    expand_mine = lax.all_to_all(expand_deal, "blk", 0, 0, tiled=True).reshape(width, units)
    expand_other = swap_cores(expand_mine)
    shrink_mine = lax.all_to_all(
        w_out2.reshape(blocks, units, depth), "blk", 0, 0, tiled=True
    )
    shrink_other = swap_cores(shrink_mine)
    w_expand = jnp.concatenate([expand_mine, expand_other], axis=1)
    w_shrink = jnp.concatenate([shrink_mine, shrink_other], axis=1)
    w_shrink = w_shrink.transpose(1, 0, 2).reshape(2 * units, width)

    my_tokens = lax.dynamic_slice_in_dim(tokens, core * part, part, 0)
    my_cotangent = lax.dynamic_slice_in_dim(cotangent, core * part, part, 0)
    all_tokens = jnp.concatenate(gather(my_tokens))
    all_cotangent = jnp.concatenate(gather(my_cotangent))
    count = all_tokens.shape[0]

    at = 3 * cut
    mid = at + near * depth // columns
    w_triple = both[:, :, :at].reshape(cores, blocks, 3, cut, columns)
    w_triple = w_triple.transpose(1, 0, 3, 2, 4).reshape(width, 3 * columns)
    w_near = both[:, :, at:mid].reshape(cores, blocks, near, depth)
    w_near = w_near.transpose(0, 2, 1, 3).reshape(columns, width)
    w_head = spread(w_near, masks_x).reshape(HEAD, width)
    flat = both[:, :, mid:].reshape(cores, blocks, -1)

    def take(offset, like):
        return flat[:, :, offset : offset + like.size].reshape((cores, blocks) + like.shape), offset + like.size

    offset = 0
    gain_all, offset = take(offset, norm_gain)
    shift_all, offset = take(offset, norm_shift)
    out_all, offset = take(offset, b_out)
    out2_all, offset = take(offset, b_out2)
    triple_all, offset = take(offset, b_qkv)
    expand_all, offset = take(offset, b_in)
    start_high, offset = take(offset, doc_start)
    start_low, offset = take(offset, doc_start)
    live_all, offset = take(offset, live)
    gains = gain_all[0].transpose(1, 2, 0, 3).reshape(2, width).astype(F32)
    shifts = shift_all[0].transpose(1, 2, 0, 3).reshape(2, width).astype(F32)
    residual_shift = (out_all[0].astype(F32) + out2_all[0].astype(F32)).transpose(1, 0, 2).reshape(width)
    triple_shift = triple_all.astype(F32).transpose(2, 0, 3, 1, 4).reshape(3, width)
    triple_shift = lax.dynamic_slice_in_dim(triple_shift, me * columns, columns, 1).reshape(-1)
    expand_shift = expand_all.astype(F32).transpose(0, 2, 1, 3).reshape(cores, -1)
    expand_shift = lax.dynamic_slice_in_dim(expand_shift, me * units, units, 1)
    expand_shift = jnp.concatenate(by_core(core, expand_shift[0], expand_shift[1]))
    starts = (start_high[0].astype(F32) * 256.0 + start_low[0].astype(F32)).astype(jnp.int32)
    lives = live_all[0].astype(jnp.int32)

    x_at = jnp.arange(size_x)[:, None, None]
    y_at = group * jnp.arange(size_y)[None, :, None]
    z_at = 2 * group * jnp.arange(size_z)[None, None, :]
    order = (x_at + y_at + z_at) ^ me
    inside = jnp.arange(quarter, dtype=jnp.int32)

    def index_of(which):
        base = order[..., None] * rows + which * part + inside
        one, two = base, base + quarter
        return jnp.concatenate(
            [one.reshape(size_x, -1), two.reshape(size_x, -1)], axis=1
        )

    def heads_order(value):
        tail = value.shape[1:]
        one = value[: count // 2].reshape((size_x, -1) + tail)
        two = value[count // 2 :].reshape((size_y, size_x, -1) + tail)
        two = jnp.swapaxes(two, 0, 1).reshape((size_x, -1) + tail)
        return jnp.concatenate([one, two], axis=1)

    def gathered_order(value):
        tail = value.shape[2:]
        middle = value.shape[1] // 2
        one = value[:, :middle].reshape((count // 2,) + tail)
        two = value[:, middle:].reshape((size_x, size_y, -1) + tail)
        two = jnp.swapaxes(two, 0, 1).reshape((count // 2,) + tail)
        return jnp.concatenate([one, two])

    index_mine, index_other = index_of(core), index_of(1 - core)
    index = jnp.concatenate([index_mine.reshape(-1), index_other.reshape(-1)])
    token_start = starts.reshape(-1)[index]
    token_live = lives.reshape(-1)[index]

    inputs = all_tokens.astype(F32)
    center = inputs - jnp.mean(inputs, axis=-1, keepdims=True)
    inverse = lax.rsqrt(jnp.mean(center * center, axis=-1, keepdims=True) + EPSILON)
    normal = center * inverse
    normed_attend = (normal * gains[0] + shifts[0]).astype(BF)
    normed_feed = (normal * gains[1] + shifts[1]).astype(BF)

    linear = dot(normed_attend, w_triple, ((1,), (0,))) + triple_shift
    linear = heads_order(linear).reshape(count, 3, columns)
    steps = jnp.arange(ROT // 2, dtype=F32)
    speed = 10000.0 ** (-2.0 * steps / ROT)
    place = (index - token_start).astype(F32)
    angle = place[:count, None] * speed[None, :]
    cosine, sine = jnp.cos(angle), jnp.sin(angle)
    slot = me % group

    def turn_pieces(pieces, cosine, sine):
        if columns >= ROT:
            return jnp.stack(
                [
                    turn(
                        pieces[r],
                        jnp.where(slot == r, cosine, 1.0),
                        jnp.where(slot == r, sine, 0.0),
                    )
                    for r in range(group)
                ]
            )
        place_of = jnp.arange(group) ^ slot
        whole = jnp.swapaxes(pieces[place_of], 0, 1).reshape(pieces.shape[1], HEAD)
        whole = turn(whole, cosine, sine).reshape(-1, group, columns)
        return jnp.swapaxes(whole, 0, 1)[place_of]

    if columns >= ROT:
        own_cosine = jnp.where(slot == 0, cosine, 1.0)
        own_sine = jnp.where(slot == 0, sine, 0.0)
        queries = turn(linear[:, 0], own_cosine, own_sine)
        keys = turn(linear[:, 1], own_cosine, own_sine)
    else:
        queries, keys = linear[:, 0], linear[:, 1]
    mine = jnp.concatenate([queries, keys, linear[:, 2]], axis=1).astype(BF)

    def align(value, r):
        slabs = value.reshape((size_x, -1) + value.shape[1:])
        return jnp.stack([slabs[x ^ r] for x in range(size_x)]).reshape(value.shape)

    pieces = [mine] + [align(from_peer(mine, r), r) for r in masks_x]
    pieces = jnp.stack(pieces).reshape(group, count, 3, columns)
    if columns < ROT:
        turned = [turn_pieces(pieces[:, :, s].astype(F32), cosine, sine).astype(BF) for s in (0, 1)]
        pieces = jnp.stack(turned + [pieces[:, :, 2]], axis=2)
    own_triple = pieces.transpose(2, 1, 0, 3).reshape(3, count, HEAD)
    other_triple = swap_cores(own_triple)
    queries, keys, values = jnp.concatenate([own_triple, other_triple], axis=1)

    cotangent_x = heads_order(all_cotangent)
    grad_attended = dot(all_cotangent, w_head, ((1,), (1,))).astype(BF)
    grad_attended = heads_order(grad_attended).reshape(count, HEAD)
    grad_attended = jnp.concatenate([grad_attended, swap_cores(grad_attended)])

    share = count // size_x
    mine_index, mine_start, mine_live = index[:share], token_start[:share], token_live[:share]

    def allowed(query_index, query_start, key_index, key_start, key_live):
        same = query_start == key_start
        causal = key_index <= query_index
        usable = (key_live == 1) | (key_index == query_index)
        return same & causal & usable

    mask = allowed(mine_index[:, None], mine_start[:, None], index[None], token_start[None], token_live[None])
    scores = dot(queries[:share], keys, ((1,), (1,))) * scale
    masked = jnp.where(mask, scores, NEGATIVE)
    top = jnp.max(masked, axis=-1, keepdims=True)
    weight = jnp.where(mask, jnp.exp(masked - top), 0.0)
    total = jnp.sum(weight, axis=-1, keepdims=True)
    prob = weight / total
    attended = dot(prob.astype(BF), values, ((1,), (0,)))
    log_total = top + jnp.log(total)
    delta = jnp.sum(grad_attended[:share].astype(F32) * attended, axis=-1, keepdims=True)
    push = dot(grad_attended[:share], values, ((1,), (1,)))
    slope = (prob * (push - delta)).astype(BF)
    grad_queries = dot(slope, keys, ((1,), (0,))) * scale
    attended = attended.astype(BF)

    marks = jnp.concatenate([log_total, delta], axis=1).T
    marks = spread(marks, masks_x).transpose(1, 0, 2).reshape(2, count)
    marks = jnp.concatenate([marks, swap_cores(marks)], axis=1)
    mask = allowed(index[None], token_start[None], mine_index[:, None], mine_start[:, None], mine_live[:, None])
    scores = dot(keys[:share], queries, ((1,), (1,))) * scale
    prob = jnp.where(mask, jnp.exp(jnp.where(mask, scores, NEGATIVE) - marks[0][None]), 0.0)
    grad_values = dot(prob.astype(BF), grad_attended, ((1,), (0,)))
    push = dot(values[:share], grad_attended, ((1,), (1,)))
    slope = (prob * (push - marks[1][None])).astype(BF)
    grad_keys = dot(slope, queries, ((1,), (0,))) * scale

    expanded = dot(normed_feed, w_expand, ((1,), (0,))) + expand_shift
    activated, bend = gelu_and_slope(expanded)
    activated = activated.astype(BF)
    grad_activated = dot(all_cotangent, w_shrink, ((1,), (1,)))
    grad_expanded = (bend * grad_activated).astype(BF)

    branch = dot(activated, w_shrink, ((1,), (0,)))
    attend_part = dot(attended, w_head, ((1,), (0,)))
    rest = jnp.zeros((size_x - 1,) + attend_part.shape, F32)
    attend_part = gathered_order(jnp.concatenate([attend_part[None], rest]))
    branch = (branch + attend_part).astype(BF)
    branch = scatter(branch[: count // 2], branch[count // 2 :])
    my_inputs = my_tokens.astype(F32)
    my_mixed = (my_inputs + branch.reshape(part, width) + residual_shift).astype(BF)

    def whole_block(value):
        low, high = by_core(core, value, swap_cores(value))
        return jnp.concatenate([low, high])

    mixed = whole_block(my_mixed)

    grad_shrink = dot(activated, all_cotangent, ((0,), (0,)))
    grad_expand = dot(normed_feed, grad_expanded, ((0,), (0,)))
    grad_shrink = grad_shrink[:units] + swap_cores(grad_shrink[units:].astype(BF)).astype(F32)
    grad_expand = grad_expand[:, :units] + swap_cores(grad_expand[:, units:].astype(BF)).astype(F32)
    shrink_deal = grad_shrink.astype(BF).reshape(units, blocks, depth).transpose(1, 0, 2)
    expand_deal = grad_expand.astype(BF).reshape(blocks, depth, units)
    shrink_grad = lax.all_to_all(shrink_deal, "blk", 0, 0, tiled=True)
    shrink_grad = shrink_grad.reshape(-1, depth).astype(F32)
    expand_grad = lax.all_to_all(expand_deal, "blk", 0, 0, tiled=True)
    expand_grad = expand_grad.transpose(1, 0, 2).reshape(depth, -1).astype(F32)

    def by_pieces(value):
        return value.reshape(share, group, columns).transpose(1, 0, 2)

    own_cosine, own_sine = cosine[:share], -sine[:share]
    back = [
        turn_pieces(by_pieces(grad_queries), own_cosine, own_sine),
        turn_pieces(by_pieces(grad_keys), own_cosine, own_sine),
        by_pieces(grad_values),
    ]
    back = jnp.concatenate(back, axis=2).astype(BF)
    back = jnp.concatenate([back, by_pieces(attended)], axis=2)
    back = jnp.stack([back[0]] + [from_peer(back[r], r) for r in masks_x])
    back = gathered_order(back)
    grad_linear, attended_near = back[:, : 3 * columns], back[:, 3 * columns :]
    grad_triple = dot(normed_attend, grad_linear, ((0,), (0,)))
    grad_out = dot(attended_near, all_cotangent, ((0,), (0,)))
    grad_triple = grad_triple.reshape(blocks, cores, cut, 3, columns).transpose(1, 0, 3, 2, 4)
    grad_triple = grad_triple.reshape(cores, blocks, 3 * cut, columns)
    grad_out = grad_out.reshape(cores, near, blocks, depth).transpose(0, 2, 1, 3)
    grad_out = grad_out.reshape(cores, blocks, near * depth // columns, columns)
    dealt = jnp.concatenate([grad_triple, grad_out], axis=2)
    keep = lax.dynamic_index_in_dim(dealt, core, 0, keepdims=False)
    give = lax.dynamic_index_in_dim(dealt, 1 - core, 0, keepdims=False)
    dealt = (keep + swap_cores(give.astype(BF)).astype(F32)).astype(BF)
    dealt = lax.all_to_all(dealt, "blk", 0, 0, tiled=True)
    dealt = dealt.reshape((cores, own_heads) + dealt.shape[1:])
    keep = lax.dynamic_index_in_dim(dealt, core, 0, keepdims=False)
    give = lax.dynamic_index_in_dim(dealt, 1 - core, 0, keepdims=False)
    dealt = jnp.stack(by_core(core, keep, swap_cores(give)))
    triple_grad = dealt[:, :, :at].reshape(cores, own_heads, 3, cut, columns)
    triple_grad = triple_grad.transpose(2, 0, 3, 1, 4).reshape(3, depth, -1).astype(F32)
    output_grad = dealt[:, :, at:].reshape(cores, own_heads, near, depth)
    output_grad = output_grad.transpose(1, 0, 2, 3).reshape(-1, depth).astype(F32)

    grad_attend_norm = dot(grad_linear, w_triple, ((1,), (1,)))
    grad_feed_norm = dot(grad_expanded, w_expand, ((1,), (1,)))
    combined = (gains[0] * grad_attend_norm + gains[1] * grad_feed_norm).astype(BF)
    combined = scatter(combined[: count // 2], combined[count // 2 :]).reshape(part, width)
    my_center = my_inputs - jnp.mean(my_inputs, axis=-1, keepdims=True)
    my_inverse = lax.rsqrt(jnp.mean(my_center * my_center, axis=-1, keepdims=True) + EPSILON)
    my_normal = my_center * my_inverse
    my_grad = my_inverse * (
        combined
        - jnp.mean(combined, axis=-1, keepdims=True)
        - my_normal * jnp.mean(combined * my_normal, axis=-1, keepdims=True)
    )
    tokens_grad = whole_block((my_cotangent.astype(F32) + my_grad).astype(BF))

    sums = [
        jnp.sum(normal * grad_attend_norm, axis=0),
        jnp.sum(normal * grad_feed_norm, axis=0),
        jnp.sum(grad_attend_norm, axis=0),
        jnp.sum(grad_feed_norm, axis=0),
        jnp.sum(all_cotangent.astype(F32), axis=0),
        jnp.sum(grad_expanded.astype(F32), axis=0),
        jnp.sum(grad_linear.astype(F32), axis=0),
    ]
    sums = jnp.concatenate(sums)
    other = swap_cores(sums)
    added = sums + other
    norm_sums = added[: 4 * width].reshape(4, width // 128, blocks, -1).transpose(2, 0, 1, 3)
    residual_sum = added[4 * width : 5 * width].reshape(width // 128, 128)
    lanes = 128 // blocks
    residual_grad = lax.dynamic_slice_in_dim(residual_sum, me * lanes, lanes, 1)
    unit_sum = sums[5 * width : 5 * width + units] + other[5 * width + units : 5 * width + 2 * units]
    unit_sums = lax.dynamic_update_slice_in_dim(
        jnp.zeros((w_in.shape[1],), F32), unit_sum, me * units, 0
    )
    unit_sums = unit_sums.reshape(-1, blocks, lanes).transpose(1, 0, 2)
    line_sum = added[5 * width + 2 * units :].reshape(3, columns)
    line_sums = lax.dynamic_update_slice_in_dim(
        jnp.zeros((3, width), F32), line_sum, me * columns, 1
    )
    line_sums = lax.dynamic_slice_in_dim(line_sums, core * (width // cores), width // cores, 1)
    line_sums = line_sums.reshape(3, -1, blocks, lanes).transpose(2, 0, 1, 3)
    tiny = jnp.concatenate(
        [norm_sums.reshape(blocks, -1), unit_sums.reshape(blocks, -1), line_sums.reshape(blocks, -1)],
        axis=1,
    )
    tiny = jnp.sum(lax.all_to_all(tiny, "blk", 0, 0, tiled=True), axis=0)
    first = norm_gain.size
    gain_grad = tiny[:first].reshape(norm_gain.shape)
    shift_grad = tiny[first : 2 * first].reshape(norm_shift.shape)
    expand_bias_grad = tiny[2 * first : 2 * first + b_in.size].reshape(b_in.shape)
    triple_bias_grad = tiny[2 * first + b_in.size :].reshape(b_qkv.shape)
    return (
        mixed,
        tokens_grad,
        triple_grad,
        triple_bias_grad,
        output_grad,
        residual_grad,
        expand_grad,
        expand_bias_grad,
        shrink_grad,
        residual_grad,
        gain_grad,
        shift_grad,
    )


VMEM = pl.BlockSpec(memory_space=pltpu.VMEM)
SMEM = pl.BlockSpec(memory_space=pltpu.SMEM)
GRANT = 50 * 1024 * 1024
MARK_COS, MARK_SIN = 32, 64


def run_kernel(kernel, outs, grid=None, ins=None, out_specs=None, scratch=(), flops=0, moved=0):
    outs = [jax.ShapeDtypeStruct(shape, kind) for shape, kind in outs]
    single = len(outs) == 1
    out_specs = out_specs or [VMEM] * len(outs)
    extra = {} if grid is None else {"grid": grid}
    return pl.pallas_call(
        kernel,
        out_shape=outs[0] if single else outs,
        in_specs=ins,
        out_specs=out_specs[0] if single else out_specs,
        scratch_shapes=list(scratch),
        compiler_params=pltpu.CompilerParams(vmem_limit_bytes=GRANT),
        cost_estimate=pl.CostEstimate(flops=int(flops), bytes_accessed=int(moved), transcendentals=0),
        **extra,
    )


def chunk_bits(half, at, lanes):
    z = at % lanes
    low, high = (at // lanes) % 2, at // (2 * lanes)
    x, y = (high, low) if half == 0 else (low, high)
    return x + 2 * y + 4 * z


class Rows:
    def __init__(self, blocks, cores, rows):
        self.blocks, self.rows = blocks, rows
        self.part = rows // cores
        self.chunk = self.part // 2
        self.half = blocks * self.chunk
        self.count = 2 * self.half
        self.share = self.half
        self.sizes_z = blocks // 4

    def natural(self, me, core, half, at):
        block = me ^ chunk_bits(half, at, self.sizes_z)
        return block * self.rows + core * self.part + half * self.chunk

    def x_rows(self, x):
        h, q = self.half // 2, self.half // 4
        return [
            (x * h, 0, h),
            (self.half + x * q, h, q),
            (self.half + 2 * q + x * q, h + q, q),
        ]

    def pairs(self):
        mine, peer = self.x_rows(0), self.x_rows(1)
        both = [(a[0], b[0], a[2]) for a, b in zip(mine, peer)]
        return both + [(b, a, n) for a, b, n in both]


def nn(left, right):
    return lax.dot_general(left, right, (((1,), (0,)), ((), ())), preferred_element_type=F32)


def nt(left, right):
    return lax.dot_general(left, right, (((1,), (1,)), ((), ())), preferred_element_type=F32)


def lane_of(shape):
    return lax.broadcasted_iota(jnp.int32, shape, len(shape) - 1)


def turn_lanes(values, table, active, sign):
    lane = lane_of(values.shape)
    first, second = lane < ROT // 2, lane < ROT
    to_first = 128 - MARK_COS
    cosine = jnp.where(first, pltpu.roll(table, to_first, 1), table)
    sine_first = pltpu.roll(table, 128 - MARK_SIN, 1)
    sine_second = pltpu.roll(table, 128 - MARK_SIN + ROT // 2, 1)
    sine = jnp.where(first, -sine_first, sine_second) * sign
    cosine = jnp.where(second & active, cosine, 1.0)
    sine = jnp.where(second & active, sine, 0.0)
    partner = jnp.where(first, pltpu.roll(values, 128 - ROT // 2, 1), pltpu.roll(values, ROT // 2, 1))
    return values * cosine + partner * sine


def deal_kernel(cut, blocks, ids, here, there, triple, near):
    core = ids[1]
    for source in range(blocks):
        for who, ref in ((core, here), (1 - core, there)):
            at = pl.multiple_of(source * 2 * cut + who * cut, cut)
            for s in range(3):
                triple[pl.ds(at, cut), s * 128 : (s + 1) * 128] = ref[source, s * cut : (s + 1) * cut, :]
            at = pl.multiple_of(who * cut, cut)
            near[pl.ds(at, cut), source * 128 : (source + 1) * 128] = ref[source, 3 * cut : 4 * cut, :]


def shrink_kernel(blocks, units, mine, other, out):
    for source in range(blocks):
        out[:units, source * 128 : (source + 1) * 128] = mine[source]
        out[units:, source * 128 : (source + 1) * 128] = other[source]


def norm_kernel(r, ids, t0, t1, t2, t3, norms, weight, bias, marks, attend, feed, normal, mine, tile, table):
    i = pl.program_id(0)
    me, core = ids[0], ids[1]
    for k, ref in enumerate((t0, t1, t2, t3)):

        @pl.when(i == k)
        def _(ref=ref):
            tile[...] = ref[...]

    for half in (0, 1):

        @pl.when(i // 2 == half)
        def _(half=half):
            for q in range(8):
                at = r.natural(me, core, half, (i % 2) * 8 + q)
                table[q * r.chunk : (q + 1) * r.chunk, :] = marks[pl.ds(pl.multiple_of(at, r.chunk), r.chunk), :]

    step = 16

    @pl.loop(0, tile.shape[0] // step)
    def _(j):
        rows = pl.ds(pl.multiple_of(j * step, step), step)
        values = tile[rows, :].astype(F32)
        center = values - jnp.mean(values, axis=-1, keepdims=True)
        spread = jnp.mean(center * center, axis=-1, keepdims=True)
        value = center * lax.rsqrt(spread + EPSILON)
        normal[rows, :] = value.astype(BF)
        attend[rows, :] = (value * norms[0:1, :] + norms[2:3, :]).astype(BF)
        feed[rows, :] = (value * norms[1:2, :] + norms[3:4, :]).astype(BF)

    linear = nn(attend[...], weight[...]) + bias[...]
    active = me % 2 == 0
    for s in (0, 1):
        cols = slice(s * 128, (s + 1) * 128)
        mine[:, cols] = turn_lanes(linear[:, cols], table[...], active, 1.0).astype(BF)
    mine[:, 256:] = linear[:, 256:].astype(BF)


def cotangent_kernel(t0, t1, t2, t3, near, peer, whole, grads, sums):
    i = pl.program_id(0)
    for k, ref in enumerate((t0, t1, t2, t3)):

        @pl.when(i == k)
        def _(ref=ref):
            whole[...] = ref[...]

    grads[:, :128] = nt(whole[...], near[...]).astype(BF)
    grads[:, 128:] = nt(whole[...], peer[...]).astype(BF)

    @pl.when(i == 0)
    def _():
        sums[...] = jnp.zeros_like(sums)

    sums[0:1, :] += jnp.sum(whole[...].astype(F32), axis=0, keepdims=True)


def gather_columns(r, out, low, high, column):
    cols = slice(column * 128, (column + 1) * 128)
    out[:, :128] = low[:, cols]
    for here, there, size in r.pairs():
        out[here : here + size, 128:] = high[there : there + size, cols]


def gather_marks(r, ids, marks, table, line):
    me, core = ids[0], ids[1]
    for w in (0, 1):
        who = core if w == 0 else 1 - core
        for half in (0, 1):
            for q in range(16):
                at = r.natural(me, who, half, q)
                to = w * r.count + half * r.half + q * r.chunk
                table[to : to + r.chunk, :] = marks[pl.ds(pl.multiple_of(at, r.chunk), r.chunk), :]
    for b in range(2 * r.count // 128):
        line[:, b * 128 : (b + 1) * 128] = table[b * 128 : (b + 1) * 128, :].T[:8, :]


def own_rows(r, out, ref, columns=slice(None)):
    for row, place, size in r.x_rows(0):
        out[place : place + size, :] = ref[row : row + size, columns]


def query_kernel(r, scale, ids, a00, a01, a10, a11, grads, marks, attended, keep, send, lines,
                 keys, values, queries, pushes, table, line, mine):
    i = pl.program_id(0)
    me = ids[0]
    count, tile = r.count, r.share // 2

    @pl.when(i == 0)
    def _():
        gather_columns(r, keys.at[:count], a00, a01, 1)
        gather_columns(r, keys.at[count:], a10, a11, 1)
        gather_columns(r, values.at[:count], a00, a01, 2)
        gather_columns(r, values.at[count:], a10, a11, 2)
        for row, place, size in r.x_rows(0):
            queries[place : place + size, :128] = a00[row : row + size, :128]
        for (row, place, size), (there, _, _) in zip(r.x_rows(0), r.x_rows(1)):
            queries[place : place + size, 128:] = a01[there : there + size, :128]
        own_rows(r, pushes, grads)
        gather_marks(r, ids, marks, table, line)
        own_rows(r, mine, table.at[:count])

    rows = pl.ds(pl.multiple_of(i * tile, tile), tile)
    mark = mine[rows, :]
    q_at, q_start = mark[:, 0:1], mark[:, 2:3]
    k_at, k_live = line[0:1, :], line[1:2, :]
    mask = ((k_live >= q_start) & (k_at <= q_at)) | (k_at == q_at)
    scores = jnp.where(mask, nt(queries[rows, :], keys[...]) * scale, NEGATIVE)
    top = jnp.max(scores, axis=-1, keepdims=True)
    weight = jnp.where(mask, jnp.exp(scores - top), 0.0)
    total = jnp.sum(weight, axis=-1, keepdims=True)
    prob = weight * (1.0 / total)
    result = nn(prob.astype(BF), values[...])
    grad = pushes[rows, :]
    delta = jnp.sum(grad.astype(F32) * result, axis=-1, keepdims=True)
    slope = (prob * (nt(grad, values[...]) - delta)).astype(BF)
    back = nn(slope, keys[...]) * scale
    result = result.astype(BF)
    attended[...] = result
    for k, ref in enumerate((keep, send)):
        cols = slice(k * 128, (k + 1) * 128)
        ref[:, :128] = turn_lanes(back[:, cols], mark, me % 2 == k, -1.0).astype(BF)
        ref[:, 128:] = result[:, cols]
    lane = lane_of((tile, 128))
    both = jnp.where(lane == 0, top + jnp.log(total), jnp.where(lane == 1, delta, 0.0))
    for b in range(tile // 128):
        lines[:, b * 128 : (b + 1) * 128] = both[b * 128 : (b + 1) * 128, :].T[:8, :]


def key_kernel(r, scale, ids, a00, a01, a10, a11, grads, other_grads, l00, l01, l10, l11, marks, keep, send,
               queries, pushes, keys, values, table, line, mine, tops):
    i = pl.program_id(0)
    me = ids[0]
    count, tile = r.count, r.share // 2

    @pl.when(i == 0)
    def _():
        gather_columns(r, queries.at[:count], a00, a01, 0)
        gather_columns(r, queries.at[count:], a10, a11, 0)
        pushes[:count, :] = grads[...]
        pushes[count:, :] = other_grads[...]
        for k, out in ((1, keys), (2, values)):
            cols = slice(k * 128, (k + 1) * 128)
            for row, place, size in r.x_rows(0):
                out[place : place + size, :128] = a00[row : row + size, cols]
            for (row, place, size), (there, _, _) in zip(r.x_rows(0), r.x_rows(1)):
                out[place : place + size, 128:] = a01[there : there + size, cols]
        gather_marks(r, ids, marks, table, line)
        own_rows(r, mine, table.at[:count])
        for base, low, high in ((0, l00, l01), (count, l10, l11)):
            for x, ref in ((0, low), (1, high)):
                for row, place, size in r.x_rows(x):
                    tops[:, base + row : base + row + size] = ref[:, place : place + size]

    rows = pl.ds(pl.multiple_of(i * tile, tile), tile)
    mark = mine[rows, :]
    k_at, k_live = mark[:, 0:1], mark[:, 1:2]
    q_at, q_start = line[0:1, :], line[2:3, :]
    mask = ((k_live >= q_start) & (k_at <= q_at)) | (k_at == q_at)
    scores = nt(keys[rows, :], queries[...]) * scale
    prob = jnp.where(mask, jnp.exp(scores - tops[0:1, :]), 0.0)
    grad_values = nn(prob.astype(BF), pushes[...])
    slope = (prob * (nt(values[rows, :], pushes[...]) - tops[1:2, :])).astype(BF)
    back = nn(slope, queries[...]) * scale
    for k, ref in enumerate((keep, send)):
        cols = slice(k * 128, (k + 1) * 128)
        ref[:, :128] = turn_lanes(back[:, cols], mark, me % 2 == k, -1.0).astype(BF)
        ref[:, 128:] = grad_values[:, cols].astype(BF)


def feed_kernel(units, normed, cotangent, expand, shrink, bias, act0, act1, grad0, grad1, sums):
    i = pl.program_id(0)
    expanded = nn(normed[...], expand[...]) + bias[...]
    activated, bend = gelu_and_slope(expanded)
    activated = activated.astype(BF)
    act0[...] = activated[:, :units]
    act1[...] = activated[:, units:]
    grad = (bend * nt(cotangent[...], shrink[...])).astype(BF)
    grad0[...] = grad[:, :units]
    grad1[...] = grad[:, units:]

    @pl.when(i == 0)
    def _():
        sums[...] = jnp.zeros_like(sums)

    sums[0:1, :] += jnp.sum(grad.astype(F32), axis=0, keepdims=True)


def branch_kernel(r, act0, act1, attended, shrink, near, peer, o0, o1, o2, o3, rows):
    i = pl.program_id(0)
    units = act0.shape[1]

    @pl.when(i == 0)
    def _():
        rows[...] = jnp.zeros_like(rows)
        for row, place, size in r.x_rows(0):
            rows[row : row + size, :] = attended[place : place + size, :]

    tile = act0.shape[0]
    here = pl.ds(pl.multiple_of(i * tile, tile), tile)
    result = nn(act0[...], shrink[:units, :]) + nn(act1[...], shrink[units:, :])
    result = result + nn(rows[here, :128], near[...]) + nn(rows[here, 128:], peer[...])
    result = result.astype(BF)
    for k, ref in enumerate((o0, o1, o2, o3)):

        @pl.when(i == k)
        def _(ref=ref):
            ref[...] = result


def inputs_kernel(r, keep1, keep2, got1, got2, grad0, grad1, normal, triple, expand, gains,
                  o0, o1, o2, o3, linear, near, sums, line_sums, rows):
    i = pl.program_id(0)
    units = grad0.shape[1]
    tile = grad0.shape[0]

    @pl.when(i == 0)
    def _():
        sums[...] = jnp.zeros_like(sums)
        line_sums[...] = jnp.zeros_like(line_sums)
        for x, one, two in ((0, keep1, keep2), (1, got1, got2)):
            for row, place, size in r.x_rows(x):
                rows[row : row + size, :128] = one[place : place + size, :128]
                rows[row : row + size, 128:384] = two[place : place + size, :]
                near[row : row + size, :] = one[place : place + size, 128:]

    here = pl.ds(pl.multiple_of(i * tile, tile), tile)
    line = rows[here, :]
    linear[...] = line
    line_sums[0:1, :] += jnp.sum(line.astype(F32), axis=0, keepdims=True)
    wide = 256
    for j in range(normal.shape[1] // wide):
        cols = slice(j * wide, (j + 1) * wide)
        attend = nt(line, triple[cols, :])
        feed = nt(grad0[...], expand[cols, :units]) + nt(grad1[...], expand[cols, units:])
        value = normal[:, cols].astype(F32)
        sums[0:1, cols] += jnp.sum(value * attend, axis=0, keepdims=True)
        sums[1:2, cols] += jnp.sum(value * feed, axis=0, keepdims=True)
        sums[2:3, cols] += jnp.sum(attend, axis=0, keepdims=True)
        sums[3:4, cols] += jnp.sum(feed, axis=0, keepdims=True)
        both = (gains[0:1, cols] * attend + gains[1:2, cols] * feed).astype(BF)
        for k, ref in enumerate((o0, o1, o2, o3)):

            @pl.when(i == k)
            def _(ref=ref, cols=cols, both=both):
                ref[:, cols] = both


def pack_kernel(cut, blocks, ids, triple, outward, keep, give):
    core = ids[1]
    for b in range(blocks):
        for who, out in ((core, keep), (1 - core, give)):
            at = pl.multiple_of(b * 2 * cut + who * cut, cut)
            for s in range(3):
                out[b, s * cut : (s + 1) * cut, :] = triple[pl.ds(at, cut), s * 128 : (s + 1) * 128].astype(out.dtype)
            at = pl.multiple_of(who * cut, cut)
            out[b, 3 * cut :, :] = outward[pl.ds(at, cut), b * 128 : (b + 1) * 128].astype(out.dtype)


def unpack_kernel(cut, heads, ids, mine, other, triple, outward):
    core = ids[1]
    for who, ref in ((core, mine), (1 - core, other)):
        at = pl.multiple_of(who * cut, cut)
        for k in range(heads):
            for s in range(3):
                triple[s, pl.ds(at, cut), k * 128 : (k + 1) * 128] = ref[k, s * cut : (s + 1) * cut, :].astype(F32)
            to = pl.multiple_of(k * 2 * cut + who * cut, cut)
            outward[pl.ds(to, cut), :] = ref[k, 3 * cut :, :].astype(F32)


def body(
    tokens,
    w_qkv,
    b_qkv,
    w_out,
    b_out,
    w_in,
    b_in,
    w_out2,
    b_out2,
    norm_gain,
    norm_shift,
    doc_start,
    live,
    cotangent,
):
    blocks = lax.axis_size("blk")
    cores = lax.axis_size("tp")
    me, core = lax.axis_index("blk"), lax.axis_index("tp")
    ids = jnp.stack([me, core]).astype(jnp.int32)
    rows, width = tokens.shape
    depth = w_in.shape[0]
    r = Rows(blocks, cores, rows)
    part, count, share = r.part, r.count, r.share
    quarter = count // 4
    units = w_in.shape[1] // blocks
    cut = depth // cores
    scale = 1.0 / math.sqrt(HEAD)
    masks_z = [4 * i for i in range(1, blocks // 4)]

    def gather(value):
        over_z = spread(value, masks_z)
        one, two = over_z[:, : r.chunk], over_z[:, r.chunk :]
        one, two = spread(one, [2]), spread(two, [1])
        return [
            piece.reshape(quarter, width)
            for piece in (one, from_peer(one, 1), two, from_peer(two, 2))
        ]

    def scatter(quarters):
        def fold(keep, send, mask):
            got = from_peer(send, mask).astype(F32)
            half = keep.shape[0] // 2
            keep = keep.astype(F32)
            return (keep[:half] + got[:half]).astype(BF), (keep[half:] + got[half:]).astype(BF)

        one = fold(quarters[0], quarters[1], 1)
        two = fold(quarters[2], quarters[3], 2)
        one = one[0].astype(F32) + from_peer(one[1], 2).astype(F32)
        two = two[0].astype(F32) + from_peer(two[1], 1).astype(F32)
        one = one.reshape(-1, r.chunk, width)
        two = two.reshape(-1, r.chunk, width)
        return collect([jnp.concatenate([a, b]).astype(BF) for a, b in zip(one, two)], masks_z)

    my_tokens = lax.dynamic_slice_in_dim(tokens, core * part, part, 0)
    my_cotangent = lax.dynamic_slice_in_dim(cotangent, core * part, part, 0)
    all_tokens = gather(my_tokens)
    all_cotangent = gather(my_cotangent)

    lanes = norm_gain.shape[-1]
    small = [norm_gain, norm_shift, b_out, b_out2, b_qkv, b_in]
    sizes = [value.size // lanes for value in small]
    small = jnp.concatenate([value.reshape(-1) for value in small])
    start_high, start_low = doc_start // 256, doc_start % 256
    places = jnp.stack([start_high, start_low, live]).astype(BF)
    small = jnp.pad(small, (0, -small.size % 128)).reshape(-1, 128)
    small_lines = small.shape[0]
    small = jnp.concatenate([small, places])
    small = jnp.pad(small, ((0, -small.shape[0] % 16), (0, 0)))

    own_heads = HEADS // cores * 2
    triple = w_qkv.reshape(3, cores, cut, own_heads, 128).transpose(1, 3, 0, 2, 4)
    triple = triple.reshape(cores, own_heads, 3 * cut, 128)
    outward = w_out.reshape(own_heads, cores, cut, 128).transpose(1, 0, 2, 3)
    dealt = jnp.concatenate([triple, outward], axis=2)
    keep = lax.dynamic_index_in_dim(dealt, core, 0, keepdims=False)
    give = lax.dynamic_index_in_dim(dealt, 1 - core, 0, keepdims=False)
    heads_low, heads_high = by_core(core, keep, swap_cores(give))
    deal = jnp.concatenate(
        [
            jnp.concatenate([heads_low, heads_high]),
            jnp.broadcast_to(small, (blocks,) + small.shape),
        ],
        axis=1,
    )
    here = lax.all_to_all(deal, "blk", 0, 0, tiled=True)
    there = swap_cores(here)
    w_triple, w_near = run_kernel(
        lambda *refs: deal_kernel(cut, blocks, *refs),
        [((width, 384), BF), ((128, width), BF)],
        ins=[SMEM, VMEM, VMEM],
        moved=5e6,
    )(ids, here, there)
    w_peer = from_peer(w_near, 1)

    expand_deal = w_in.reshape(depth, blocks, units).transpose(1, 0, 2)
    expand_mine = lax.all_to_all(expand_deal, "blk", 0, 0, tiled=True).reshape(width, units)
    w_expand = jnp.concatenate([expand_mine, swap_cores(expand_mine)], axis=1)
    shrink_mine = lax.all_to_all(w_out2.reshape(blocks, units, depth), "blk", 0, 0, tiled=True)
    w_shrink = run_kernel(
        lambda *refs: shrink_kernel(blocks, units, *refs),
        [((2 * units, width), BF)],
        ins=[VMEM, VMEM],
        moved=4e6,
    )(shrink_mine, swap_cores(shrink_mine))

    tail = jnp.stack([here[:, 4 * cut :], there[:, 4 * cut :]])
    places = tail[0, :, small_lines : small_lines + 3].astype(F32)
    lines = sum(sizes)
    tail = tail[:, :, :small_lines].reshape(2, blocks, -1)[:, :, : lines * lanes]
    tail = tail.reshape(2, blocks, lines, lanes).transpose(0, 2, 1, 3).reshape(2, lines, 128).astype(F32)
    ends = [sum(sizes[: k + 1]) for k in range(len(sizes))]
    norms = tail[0, : ends[1]].reshape(4, width)
    residual_shift = (tail[0, ends[1] : ends[2]] + tail[0, ends[2] : ends[3]]).reshape(1, width)
    triple_lines = tail[:, ends[3] : ends[4]].reshape(2, 3, own_heads, 128)
    triple_lines = jnp.where(me // own_heads == core, triple_lines[0], triple_lines[1])
    triple_shift = lax.dynamic_index_in_dim(triple_lines, me % own_heads, 1, keepdims=False).reshape(1, 384)
    expand_lines = lax.dynamic_slice_in_dim(tail[:, ends[4] :], me * (units // 128), units // 128, 1)
    expand_shift = expand_lines.reshape(1, 2 * units)

    start = (places[:, 0] * 256.0 + places[:, 1]).reshape(-1, 1)
    is_live = places[:, 2].reshape(-1, 1)
    index = lax.broadcasted_iota(F32, start.shape, 0)
    steps = jnp.arange(ROT // 2, dtype=F32)
    angle = (index - start) * (10000.0 ** (-2.0 * steps / ROT))[None, :]
    marks = jnp.concatenate(
        [
            index,
            jnp.where(is_live == 1.0, index, -1.0),
            start,
            jnp.zeros((start.shape[0], MARK_COS - 3), F32),
            jnp.cos(angle),
            jnp.sin(angle),
            jnp.zeros((start.shape[0], 128 - MARK_SIN - ROT // 2), F32),
        ],
        axis=1,
    )

    def tiled(columns):
        return pl.BlockSpec((quarter, columns), lambda i: (i, 0))

    def fixed(value):
        return pl.BlockSpec(value.shape, lambda i: (0,) * value.ndim)

    def fixed_shape(*shape):
        return pl.BlockSpec(shape, lambda i: (0,) * len(shape))

    normed_attend, normed_feed, normal, mine = run_kernel(
        lambda *refs: norm_kernel(r, *refs),
        [((count, width), BF)] * 3 + [((count, 384), BF)],
        grid=(4,),
        ins=[SMEM] + [fixed(t) for t in all_tokens] + [fixed(norms), fixed(w_triple), fixed(triple_shift), fixed(marks)],
        out_specs=[tiled(width)] * 3 + [tiled(384)],
        scratch=[pltpu.VMEM((quarter, width), BF), pltpu.VMEM((quarter, 128), F32)],
        flops=2 * count * width * 384,
        moved=22e6,
    )(ids, *all_tokens, norms, w_triple, triple_shift, marks)
    peer = from_peer(mine, 1)
    mine_there = swap_cores(mine)
    peer_there = swap_cores(peer)

    whole_cotangent, grads, cotangent_sums = run_kernel(
        cotangent_kernel,
        [((count, width), BF), ((count, 256), BF), ((8, width), F32)],
        grid=(4,),
        ins=[fixed(t) for t in all_cotangent] + [fixed(w_near), fixed(w_peer)],
        out_specs=[tiled(width), tiled(256), fixed_shape(8, width)],
        flops=2 * count * width * 256,
        moved=11e6,
    )(*all_cotangent, w_near, w_peer)
    grads_there = swap_cores(grads)

    act0, act1, grad0, grad1, unit_sums = run_kernel(
        lambda *refs: feed_kernel(units, *refs),
        [((count, units), BF)] * 4 + [((8, 2 * units), F32)],
        grid=(4,),
        ins=[tiled(width), tiled(width), fixed(w_expand), fixed(w_shrink), fixed(expand_shift)],
        out_specs=[tiled(units)] * 4 + [fixed_shape(8, 2 * units)],
        flops=8 * count * width * units,
        moved=14e6,
    )(normed_feed, whole_cotangent, w_expand, w_shrink, expand_shift)

    tokens_first = ((0,), (0,))
    shrink_there = swap_cores(dot(act1, whole_cotangent, tokens_first).astype(BF))
    expand_there = swap_cores(dot(normed_feed, grad1, tokens_first).astype(BF))
    grad_shrink = (dot(act0, whole_cotangent, tokens_first) + shrink_there.astype(F32)).astype(BF)
    grad_expand = (dot(normed_feed, grad0, tokens_first) + expand_there.astype(F32)).astype(BF)
    shrink_deal = grad_shrink.reshape(units, blocks, depth).transpose(1, 0, 2)
    expand_deal = grad_expand.reshape(blocks, depth, units)
    shrink_grad = lax.all_to_all(shrink_deal, "blk", 0, 0, tiled=True)
    shrink_grad = shrink_grad.reshape(-1, depth).astype(F32)
    expand_grad = lax.all_to_all(expand_deal, "blk", 0, 0, tiled=True)
    expand_grad = expand_grad.transpose(1, 0, 2).reshape(depth, -1).astype(F32)

    tile = share // 2
    half_tile = lambda columns: pl.BlockSpec((tile, columns), lambda i: (i, 0))
    line_tile = pl.BlockSpec((8, tile), lambda i: (0, i))
    four = [mine, peer, mine_there, peer_there]
    attended, keep1, send1, lines = run_kernel(
        lambda *refs: query_kernel(r, scale, *refs),
        [((share, 256), BF)] * 3 + [((8, share), F32)],
        grid=(2,),
        ins=[SMEM] + [fixed(mine)] * 4 + [fixed(grads), fixed(marks)],
        out_specs=[half_tile(256)] * 3 + [line_tile],
        scratch=[
            pltpu.VMEM((2 * count, 256), BF),
            pltpu.VMEM((2 * count, 256), BF),
            pltpu.VMEM((share, 256), BF),
            pltpu.VMEM((share, 256), BF),
            pltpu.VMEM((2 * count, 128), F32),
            pltpu.VMEM((8, 2 * count), F32),
            pltpu.VMEM((share, 128), F32),
        ],
        flops=8 * share * 2 * count * 256,
        moved=6e6,
    )(ids, *four, grads, marks)
    got1 = from_peer(send1, 1)
    lines_peer = from_peer(lines, 1)
    lines_there, lines_peer_there = swap_cores(lines), swap_cores(lines_peer)
    keep2, send2 = run_kernel(
        lambda *refs: key_kernel(r, scale, *refs),
        [((share, 256), BF)] * 2,
        grid=(2,),
        ins=[SMEM] + [fixed(mine)] * 4 + [fixed(grads)] * 2 + [fixed(lines)] * 4 + [fixed(marks)],
        out_specs=[half_tile(256)] * 2,
        scratch=[
            pltpu.VMEM((2 * count, 256), BF),
            pltpu.VMEM((2 * count, 256), BF),
            pltpu.VMEM((share, 256), BF),
            pltpu.VMEM((share, 256), BF),
            pltpu.VMEM((2 * count, 128), F32),
            pltpu.VMEM((8, 2 * count), F32),
            pltpu.VMEM((share, 128), F32),
            pltpu.VMEM((8, 2 * count), F32),
        ],
        flops=8 * share * 2 * count * 256,
        moved=6e6,
    )(ids, *four, grads, grads_there, lines, lines_peer, lines_there, lines_peer_there, marks)
    got2 = from_peer(send2, 1)

    branches = run_kernel(
        lambda *refs: branch_kernel(r, *refs),
        [((quarter, width), BF)] * 4,
        grid=(4,),
        ins=[tiled(units)] * 2 + [fixed(attended), fixed(w_shrink), fixed(w_near), fixed(w_peer)],
        out_specs=[fixed_shape(quarter, width)] * 4,
        scratch=[pltpu.VMEM((count, 256), BF)],
        flops=2 * count * width * (2 * units + 256),
        moved=9e6,
    )(act0, act1, attended, w_shrink, w_near, w_peer)
    my_inputs = my_tokens.astype(F32)
    my_mixed = (my_inputs + scatter(branches) + residual_shift).astype(BF)

    def whole_block(value):
        return jnp.concatenate(by_core(core, value, swap_cores(value)))

    mixed = whole_block(my_mixed)

    *combined, grad_linear, attended_near, sums, line_sums = run_kernel(
        lambda *refs: inputs_kernel(r, *refs),
        [((quarter, width), BF)] * 4 + [((count, 384), BF), ((count, 128), BF), ((8, width), F32), ((8, 384), F32)],
        grid=(4,),
        ins=[fixed(keep1)] * 4 + [tiled(units)] * 2 + [tiled(width), fixed(w_triple), fixed(w_expand), fixed(norms)],
        out_specs=[fixed_shape(quarter, width)] * 4
        + [tiled(384), fixed_shape(count, 128), fixed_shape(8, width), fixed_shape(8, 384)],
        scratch=[pltpu.VMEM((count, 384), BF)],
        flops=2 * count * width * (384 + 2 * units),
        moved=16e6,
    )(keep1, keep2, got1, got2, grad0, grad1, normal, w_triple, w_expand, norms)
    combined = scatter(combined)
    my_center = my_inputs - jnp.mean(my_inputs, axis=-1, keepdims=True)
    my_inverse = lax.rsqrt(jnp.mean(my_center * my_center, axis=-1, keepdims=True) + EPSILON)
    my_normal = my_center * my_inverse
    my_grad = my_inverse * (
        combined
        - jnp.mean(combined, axis=-1, keepdims=True)
        - my_normal * jnp.mean(combined * my_normal, axis=-1, keepdims=True)
    )
    tokens_grad = whole_block((my_cotangent.astype(F32) + my_grad).astype(BF))

    grad_triple = dot(normed_attend, grad_linear, tokens_first)
    grad_out = dot(attended_near, whole_cotangent, tokens_first)
    keep, give = run_kernel(
        lambda *refs: pack_kernel(cut, blocks, *refs),
        [((blocks, 4 * cut, 128), F32), ((blocks, 4 * cut, 128), BF)],
        ins=[SMEM, VMEM, VMEM],
        moved=7e6,
    )(ids, grad_triple, grad_out)
    dealt = (keep + swap_cores(give).astype(F32)).astype(BF)
    dealt = lax.all_to_all(dealt, "blk", 0, 0, tiled=True)
    keep = lax.dynamic_slice_in_dim(dealt, core * own_heads, own_heads, 0)
    give = lax.dynamic_slice_in_dim(dealt, (1 - core) * own_heads, own_heads, 0)
    triple_grad, output_grad = run_kernel(
        lambda *refs: unpack_kernel(cut, own_heads, *refs),
        [((3, depth, own_heads * 128), F32), ((own_heads * 128, depth), F32)],
        ins=[SMEM, VMEM, VMEM],
        moved=4e6,
    )(ids, keep, swap_cores(give))

    packed = jnp.concatenate(
        [sums[:4].reshape(-1), cotangent_sums[0], line_sums[0], unit_sums[0]]
    )
    other = swap_cores(packed)
    added = packed + other
    first, second = 4 * width, 5 * width
    norm_sums = added[:first].reshape(4, width // 128, blocks, lanes).transpose(2, 0, 1, 3)
    residual_sum = added[first:second].reshape(width // 128, 128)
    residual_grad = lax.dynamic_slice_in_dim(residual_sum, me * lanes, lanes, 1)
    line_sum = added[second : second + 384].reshape(3, 1, 128)
    third = second + 384
    unit_sum = (packed[third : third + units] + other[third + units :]).reshape(-1, 128)
    unit_sum = lax.dynamic_update_slice_in_dim(
        jnp.zeros((w_in.shape[1] // 128, 128), F32), unit_sum, me * (units // 128), 0
    )
    unit_sum = unit_sum.reshape(-1, blocks, lanes).transpose(1, 0, 2)
    ours = (me // own_heads == core).astype(F32)
    line_sum = lax.dynamic_update_slice_in_dim(
        jnp.zeros((3, own_heads, 128), F32), line_sum * ours, me % own_heads, 1
    )
    line_sum = line_sum.reshape(3, own_heads, blocks, lanes).transpose(2, 0, 1, 3)
    tiny = jnp.concatenate([value.reshape(blocks, -1) for value in (norm_sums, unit_sum, line_sum)], axis=1)
    tiny = jnp.sum(lax.all_to_all(tiny, "blk", 0, 0, tiled=True), axis=0)
    first = norm_gain.size
    gain_grad = tiny[:first].reshape(norm_gain.shape)
    shift_grad = tiny[first : 2 * first].reshape(norm_shift.shape)
    expand_bias_grad = tiny[2 * first : 2 * first + b_in.size].reshape(b_in.shape)
    triple_bias_grad = tiny[2 * first + b_in.size :].reshape(b_qkv.shape)
    return (
        mixed,
        tokens_grad,
        triple_grad,
        triple_bias_grad,
        output_grad,
        residual_grad,
        expand_grad,
        expand_bias_grad,
        shrink_grad,
        residual_grad,
        gain_grad,
        shift_grad,
    )


def solution(mesh):
    placed = (
        P("blk", None),
        P(None, "blk", "tp"),
        P(None, "tp", "blk"),
        P("tp", "blk"),
        P(None, "blk"),
        P("blk", "tp"),
        P("tp", "blk"),
        P("tp", "blk"),
        P(None, "blk"),
        P(None, None, "blk"),
        P(None, None, "blk"),
        P("blk"),
        P("blk"),
        P("blk", None),
    )
    two_to_a_head = mesh.shape["blk"] == 2 * HEADS
    return jax.shard_map(
        body if two_to_a_head else general_body,
        mesh=mesh,
        in_specs=placed,
        out_specs=(
            P("blk", None),
            P("blk", None),
            P(None, "blk", "tp"),
            P(None, "tp", "blk"),
            P("tp", "blk"),
            P(None, "blk"),
            P("blk", "tp"),
            P("tp", "blk"),
            P("tp", "blk"),
            P(None, "blk"),
            P(None, None, "blk"),
            P(None, None, "blk"),
        ),
        check_vma=False,
    )
```

```python
import math

import jax
import jax.numpy as jnp
from jax import lax
from jax.experimental import pallas as pl
from jax.experimental.pallas import tpu as pltpu
from jax.sharding import PartitionSpec as P

HEADS = 8
HEAD = 256
ROT = 64

EPSILON = 1e-05
NEGATIVE = -1e30
BF = jnp.bfloat16
F32 = jnp.float32


def dot(left, right, dims):
    return lax.dot_general(left, right, (dims, ((), ())), preferred_element_type=F32)


def swap_cores(value):
    return lax.ppermute(value, "tp", [(0, 1), (1, 0)])


def from_peer(value, mask):
    count = lax.axis_size("blk")
    return lax.ppermute(value, "blk", [(i, i ^ mask) for i in range(count)])


def spread(value, masks):
    return jnp.stack([value] + [from_peer(value, mask) for mask in masks])


def collect(parts, masks):
    total = parts[0].astype(F32)
    for at, mask in enumerate(masks):
        total = total + from_peer(parts[at + 1], mask).astype(F32)
    return total


def by_core(core, mine, other):
    first = core == 0
    return jnp.where(first, mine, other), jnp.where(first, other, mine)


def gelu_and_slope(values):
    cumulative = 0.5 * (1.0 + lax.erf(values * (1.0 / math.sqrt(2.0))))
    density = jnp.exp(-0.5 * values * values) * (1.0 / math.sqrt(2.0 * math.pi))
    return values * cumulative, cumulative + values * density


def turn(values, cosine, sine):
    half = ROT // 2
    first, second = values[:, :half], values[:, half:ROT]
    return jnp.concatenate(
        [first * cosine - second * sine, second * cosine + first * sine, values[:, ROT:]],
        axis=1,
    )


def general_body(
    tokens,
    w_qkv,
    b_qkv,
    w_out,
    b_out,
    w_in,
    b_in,
    w_out2,
    b_out2,
    norm_gain,
    norm_shift,
    doc_start,
    live,
    cotangent,
):
    blocks = lax.axis_size("blk")
    cores = lax.axis_size("tp")
    me, core = lax.axis_index("blk"), lax.axis_index("tp")
    rows, width = tokens.shape
    depth = w_in.shape[0]
    part = rows // cores
    quarter = part // 2
    group = blocks // HEADS
    columns = HEAD // group
    units = w_in.shape[1] // blocks
    cut = depth // cores
    near = columns // cores
    scale = 1.0 / math.sqrt(HEAD)

    masks_x = list(range(1, group))
    masks_y = [group]
    masks_z = [2 * group * i for i in range(1, blocks // (2 * group))]
    size_x, size_y, size_z = group, 2, len(masks_z) + 1

    def gather(value):
        over_z = spread(value, masks_z)
        one = spread(spread(over_z[:, :quarter], masks_y), masks_x)
        two = spread(spread(over_z[:, quarter:], masks_x), masks_y)
        return one.reshape(-1, value.shape[-1]), two.reshape(-1, value.shape[-1])

    def scatter(one, two):
        one = one.reshape(size_x, size_y, size_z, quarter, width)
        two = two.reshape(size_y, size_x, size_z, quarter, width)
        one = collect(collect(one, masks_x).astype(BF), masks_y)
        two = collect(collect(two, masks_y).astype(BF), masks_x)
        return collect(jnp.concatenate([one, two], axis=1).astype(BF), masks_z)

    small = jnp.concatenate(
        [
            norm_gain.reshape(-1),
            norm_shift.reshape(-1),
            b_out.reshape(-1),
            b_out2.reshape(-1),
            b_qkv.reshape(-1),
            b_in.reshape(-1),
            (doc_start // 256).astype(BF),
            (doc_start % 256).astype(BF),
            live.astype(BF),
        ]
    )
    small_rows = -(-small.size // 2048) * 16
    small = jnp.pad(small, (0, small_rows * 128 - small.size)).reshape(small_rows * 128 // columns, columns)
    lines = small.shape[0]

    own_heads = HEADS // cores * group
    triple = w_qkv.reshape(3, cores, cut, own_heads, columns).transpose(1, 3, 0, 2, 4)
    triple = triple.reshape(cores, own_heads, 3 * cut, columns)
    outward = w_out.reshape(own_heads, cores, near, depth).transpose(1, 0, 2, 3)
    outward = outward.reshape(cores, own_heads, near * depth // columns, columns)
    dealt = jnp.concatenate([triple, outward], axis=2)
    keep = lax.dynamic_index_in_dim(dealt, core, 0, keepdims=False)
    give = lax.dynamic_index_in_dim(dealt, 1 - core, 0, keepdims=False)
    got = swap_cores(give)
    heads_low, heads_high = by_core(core, keep, got)
    deal = jnp.concatenate(
        [
            jnp.concatenate([heads_low, heads_high]),
            jnp.broadcast_to(small, (blocks,) + small.shape),
        ],
        axis=1,
    )
    here = lax.all_to_all(deal, "blk", 0, 0, tiled=True)
    there = swap_cores(here)
    both = jnp.stack(by_core(core, here, there))

    expand_deal = w_in.reshape(depth, blocks, units).transpose(1, 0, 2)
    expand_mine = lax.all_to_all(expand_deal, "blk", 0, 0, tiled=True).reshape(width, units)
    expand_other = swap_cores(expand_mine)
    shrink_mine = lax.all_to_all(
        w_out2.reshape(blocks, units, depth), "blk", 0, 0, tiled=True
    )
    shrink_other = swap_cores(shrink_mine)
    w_expand = jnp.concatenate([expand_mine, expand_other], axis=1)
    w_shrink = jnp.concatenate([shrink_mine, shrink_other], axis=1)
    w_shrink = w_shrink.transpose(1, 0, 2).reshape(2 * units, width)

    my_tokens = lax.dynamic_slice_in_dim(tokens, core * part, part, 0)
    my_cotangent = lax.dynamic_slice_in_dim(cotangent, core * part, part, 0)
    all_tokens = jnp.concatenate(gather(my_tokens))
    all_cotangent = jnp.concatenate(gather(my_cotangent))
    count = all_tokens.shape[0]

    at = 3 * cut
    mid = at + near * depth // columns
    w_triple = both[:, :, :at].reshape(cores, blocks, 3, cut, columns)
    w_triple = w_triple.transpose(1, 0, 3, 2, 4).reshape(width, 3 * columns)
    w_near = both[:, :, at:mid].reshape(cores, blocks, near, depth)
    w_near = w_near.transpose(0, 2, 1, 3).reshape(columns, width)
    w_head = spread(w_near, masks_x).reshape(HEAD, width)
    flat = both[:, :, mid:].reshape(cores, blocks, -1)

    def take(offset, like):
        return flat[:, :, offset : offset + like.size].reshape((cores, blocks) + like.shape), offset + like.size

    offset = 0
    gain_all, offset = take(offset, norm_gain)
    shift_all, offset = take(offset, norm_shift)
    out_all, offset = take(offset, b_out)
    out2_all, offset = take(offset, b_out2)
    triple_all, offset = take(offset, b_qkv)
    expand_all, offset = take(offset, b_in)
    start_high, offset = take(offset, doc_start)
    start_low, offset = take(offset, doc_start)
    live_all, offset = take(offset, live)
    gains = gain_all[0].transpose(1, 2, 0, 3).reshape(2, width).astype(F32)
    shifts = shift_all[0].transpose(1, 2, 0, 3).reshape(2, width).astype(F32)
    residual_shift = (out_all[0].astype(F32) + out2_all[0].astype(F32)).transpose(1, 0, 2).reshape(width)
    triple_shift = triple_all.astype(F32).transpose(2, 0, 3, 1, 4).reshape(3, width)
    triple_shift = lax.dynamic_slice_in_dim(triple_shift, me * columns, columns, 1).reshape(-1)
    expand_shift = expand_all.astype(F32).transpose(0, 2, 1, 3).reshape(cores, -1)
    expand_shift = lax.dynamic_slice_in_dim(expand_shift, me * units, units, 1)
    expand_shift = jnp.concatenate(by_core(core, expand_shift[0], expand_shift[1]))
    starts = (start_high[0].astype(F32) * 256.0 + start_low[0].astype(F32)).astype(jnp.int32)
    lives = live_all[0].astype(jnp.int32)

    x_at = jnp.arange(size_x)[:, None, None]
    y_at = group * jnp.arange(size_y)[None, :, None]
    z_at = 2 * group * jnp.arange(size_z)[None, None, :]
    order = (x_at + y_at + z_at) ^ me
    inside = jnp.arange(quarter, dtype=jnp.int32)

    def index_of(which):
        base = order[..., None] * rows + which * part + inside
        one, two = base, base + quarter
        return jnp.concatenate(
            [one.reshape(size_x, -1), two.reshape(size_x, -1)], axis=1
        )

    def heads_order(value):
        tail = value.shape[1:]
        one = value[: count // 2].reshape((size_x, -1) + tail)
        two = value[count // 2 :].reshape((size_y, size_x, -1) + tail)
        two = jnp.swapaxes(two, 0, 1).reshape((size_x, -1) + tail)
        return jnp.concatenate([one, two], axis=1)

    def gathered_order(value):
        tail = value.shape[2:]
        middle = value.shape[1] // 2
        one = value[:, :middle].reshape((count // 2,) + tail)
        two = value[:, middle:].reshape((size_x, size_y, -1) + tail)
        two = jnp.swapaxes(two, 0, 1).reshape((count // 2,) + tail)
        return jnp.concatenate([one, two])

    index_mine, index_other = index_of(core), index_of(1 - core)
    index = jnp.concatenate([index_mine.reshape(-1), index_other.reshape(-1)])
    token_start = starts.reshape(-1)[index]
    token_live = lives.reshape(-1)[index]

    inputs = all_tokens.astype(F32)
    center = inputs - jnp.mean(inputs, axis=-1, keepdims=True)
    inverse = lax.rsqrt(jnp.mean(center * center, axis=-1, keepdims=True) + EPSILON)
    normal = center * inverse
    normed_attend = (normal * gains[0] + shifts[0]).astype(BF)
    normed_feed = (normal * gains[1] + shifts[1]).astype(BF)

    linear = dot(normed_attend, w_triple, ((1,), (0,))) + triple_shift
    linear = heads_order(linear).reshape(count, 3, columns)
    steps = jnp.arange(ROT // 2, dtype=F32)
    speed = 10000.0 ** (-2.0 * steps / ROT)
    place = (index - token_start).astype(F32)
    angle = place[:count, None] * speed[None, :]
    cosine, sine = jnp.cos(angle), jnp.sin(angle)
    slot = me % group

    def turn_pieces(pieces, cosine, sine):
        if columns >= ROT:
            return jnp.stack(
                [
                    turn(
                        pieces[r],
                        jnp.where(slot == r, cosine, 1.0),
                        jnp.where(slot == r, sine, 0.0),
                    )
                    for r in range(group)
                ]
            )
        place_of = jnp.arange(group) ^ slot
        whole = jnp.swapaxes(pieces[place_of], 0, 1).reshape(pieces.shape[1], HEAD)
        whole = turn(whole, cosine, sine).reshape(-1, group, columns)
        return jnp.swapaxes(whole, 0, 1)[place_of]

    if columns >= ROT:
        own_cosine = jnp.where(slot == 0, cosine, 1.0)
        own_sine = jnp.where(slot == 0, sine, 0.0)
        queries = turn(linear[:, 0], own_cosine, own_sine)
        keys = turn(linear[:, 1], own_cosine, own_sine)
    else:
        queries, keys = linear[:, 0], linear[:, 1]
    mine = jnp.concatenate([queries, keys, linear[:, 2]], axis=1).astype(BF)

    def align(value, r):
        slabs = value.reshape((size_x, -1) + value.shape[1:])
        return jnp.stack([slabs[x ^ r] for x in range(size_x)]).reshape(value.shape)

    pieces = [mine] + [align(from_peer(mine, r), r) for r in masks_x]
    pieces = jnp.stack(pieces).reshape(group, count, 3, columns)
    if columns < ROT:
        turned = [turn_pieces(pieces[:, :, s].astype(F32), cosine, sine).astype(BF) for s in (0, 1)]
        pieces = jnp.stack(turned + [pieces[:, :, 2]], axis=2)
    own_triple = pieces.transpose(2, 1, 0, 3).reshape(3, count, HEAD)
    other_triple = swap_cores(own_triple)
    queries, keys, values = jnp.concatenate([own_triple, other_triple], axis=1)

    cotangent_x = heads_order(all_cotangent)
    grad_attended = dot(all_cotangent, w_head, ((1,), (1,))).astype(BF)
    grad_attended = heads_order(grad_attended).reshape(count, HEAD)
    grad_attended = jnp.concatenate([grad_attended, swap_cores(grad_attended)])

    share = count // size_x
    mine_index, mine_start, mine_live = index[:share], token_start[:share], token_live[:share]

    def allowed(query_index, query_start, key_index, key_start, key_live):
        same = query_start == key_start
        causal = key_index <= query_index
        usable = (key_live == 1) | (key_index == query_index)
        return same & causal & usable

    mask = allowed(mine_index[:, None], mine_start[:, None], index[None], token_start[None], token_live[None])
    scores = dot(queries[:share], keys, ((1,), (1,))) * scale
    masked = jnp.where(mask, scores, NEGATIVE)
    top = jnp.max(masked, axis=-1, keepdims=True)
    weight = jnp.where(mask, jnp.exp(masked - top), 0.0)
    total = jnp.sum(weight, axis=-1, keepdims=True)
    prob = weight / total
    attended = dot(prob.astype(BF), values, ((1,), (0,)))
    log_total = top + jnp.log(total)
    delta = jnp.sum(grad_attended[:share].astype(F32) * attended, axis=-1, keepdims=True)
    push = dot(grad_attended[:share], values, ((1,), (1,)))
    slope = (prob * (push - delta)).astype(BF)
    grad_queries = dot(slope, keys, ((1,), (0,))) * scale
    attended = attended.astype(BF)

    marks = jnp.concatenate([log_total, delta], axis=1).T
    marks = spread(marks, masks_x).transpose(1, 0, 2).reshape(2, count)
    marks = jnp.concatenate([marks, swap_cores(marks)], axis=1)
    mask = allowed(index[None], token_start[None], mine_index[:, None], mine_start[:, None], mine_live[:, None])
    scores = dot(keys[:share], queries, ((1,), (1,))) * scale
    prob = jnp.where(mask, jnp.exp(jnp.where(mask, scores, NEGATIVE) - marks[0][None]), 0.0)
    grad_values = dot(prob.astype(BF), grad_attended, ((1,), (0,)))
    push = dot(values[:share], grad_attended, ((1,), (1,)))
    slope = (prob * (push - marks[1][None])).astype(BF)
    grad_keys = dot(slope, queries, ((1,), (0,))) * scale

    expanded = dot(normed_feed, w_expand, ((1,), (0,))) + expand_shift
    activated, bend = gelu_and_slope(expanded)
    activated = activated.astype(BF)
    grad_activated = dot(all_cotangent, w_shrink, ((1,), (1,)))
    grad_expanded = (bend * grad_activated).astype(BF)

    branch = dot(activated, w_shrink, ((1,), (0,)))
    attend_part = dot(attended, w_head, ((1,), (0,)))
    rest = jnp.zeros((size_x - 1,) + attend_part.shape, F32)
    attend_part = gathered_order(jnp.concatenate([attend_part[None], rest]))
    branch = (branch + attend_part).astype(BF)
    branch = scatter(branch[: count // 2], branch[count // 2 :])
    my_inputs = my_tokens.astype(F32)
    my_mixed = (my_inputs + branch.reshape(part, width) + residual_shift).astype(BF)

    def whole_block(value):
        low, high = by_core(core, value, swap_cores(value))
        return jnp.concatenate([low, high])

    mixed = whole_block(my_mixed)

    grad_shrink = dot(activated, all_cotangent, ((0,), (0,)))
    grad_expand = dot(normed_feed, grad_expanded, ((0,), (0,)))
    grad_shrink = grad_shrink[:units] + swap_cores(grad_shrink[units:].astype(BF)).astype(F32)
    grad_expand = grad_expand[:, :units] + swap_cores(grad_expand[:, units:].astype(BF)).astype(F32)
    shrink_deal = grad_shrink.astype(BF).reshape(units, blocks, depth).transpose(1, 0, 2)
    expand_deal = grad_expand.astype(BF).reshape(blocks, depth, units)
    shrink_grad = lax.all_to_all(shrink_deal, "blk", 0, 0, tiled=True)
    shrink_grad = shrink_grad.reshape(-1, depth).astype(F32)
    expand_grad = lax.all_to_all(expand_deal, "blk", 0, 0, tiled=True)
    expand_grad = expand_grad.transpose(1, 0, 2).reshape(depth, -1).astype(F32)

    def by_pieces(value):
        return value.reshape(share, group, columns).transpose(1, 0, 2)

    own_cosine, own_sine = cosine[:share], -sine[:share]
    back = [
        turn_pieces(by_pieces(grad_queries), own_cosine, own_sine),
        turn_pieces(by_pieces(grad_keys), own_cosine, own_sine),
        by_pieces(grad_values),
    ]
    back = jnp.concatenate(back, axis=2).astype(BF)
    back = jnp.concatenate([back, by_pieces(attended)], axis=2)
    back = jnp.stack([back[0]] + [from_peer(back[r], r) for r in masks_x])
    back = gathered_order(back)
    grad_linear, attended_near = back[:, : 3 * columns], back[:, 3 * columns :]
    grad_triple = dot(normed_attend, grad_linear, ((0,), (0,)))
    grad_out = dot(attended_near, all_cotangent, ((0,), (0,)))
    grad_triple = grad_triple.reshape(blocks, cores, cut, 3, columns).transpose(1, 0, 3, 2, 4)
    grad_triple = grad_triple.reshape(cores, blocks, 3 * cut, columns)
    grad_out = grad_out.reshape(cores, near, blocks, depth).transpose(0, 2, 1, 3)
    grad_out = grad_out.reshape(cores, blocks, near * depth // columns, columns)
    dealt = jnp.concatenate([grad_triple, grad_out], axis=2)
    keep = lax.dynamic_index_in_dim(dealt, core, 0, keepdims=False)
    give = lax.dynamic_index_in_dim(dealt, 1 - core, 0, keepdims=False)
    dealt = (keep + swap_cores(give.astype(BF)).astype(F32)).astype(BF)
    dealt = lax.all_to_all(dealt, "blk", 0, 0, tiled=True)
    dealt = dealt.reshape((cores, own_heads) + dealt.shape[1:])
    keep = lax.dynamic_index_in_dim(dealt, core, 0, keepdims=False)
    give = lax.dynamic_index_in_dim(dealt, 1 - core, 0, keepdims=False)
    dealt = jnp.stack(by_core(core, keep, swap_cores(give)))
    triple_grad = dealt[:, :, :at].reshape(cores, own_heads, 3, cut, columns)
    triple_grad = triple_grad.transpose(2, 0, 3, 1, 4).reshape(3, depth, -1).astype(F32)
    output_grad = dealt[:, :, at:].reshape(cores, own_heads, near, depth)
    output_grad = output_grad.transpose(1, 0, 2, 3).reshape(-1, depth).astype(F32)

    grad_attend_norm = dot(grad_linear, w_triple, ((1,), (1,)))
    grad_feed_norm = dot(grad_expanded, w_expand, ((1,), (1,)))
    combined = (gains[0] * grad_attend_norm + gains[1] * grad_feed_norm).astype(BF)
    combined = scatter(combined[: count // 2], combined[count // 2 :]).reshape(part, width)
    my_center = my_inputs - jnp.mean(my_inputs, axis=-1, keepdims=True)
    my_inverse = lax.rsqrt(jnp.mean(my_center * my_center, axis=-1, keepdims=True) + EPSILON)
    my_normal = my_center * my_inverse
    my_grad = my_inverse * (
        combined
        - jnp.mean(combined, axis=-1, keepdims=True)
        - my_normal * jnp.mean(combined * my_normal, axis=-1, keepdims=True)
    )
    tokens_grad = whole_block((my_cotangent.astype(F32) + my_grad).astype(BF))

    sums = [
        jnp.sum(normal * grad_attend_norm, axis=0),
        jnp.sum(normal * grad_feed_norm, axis=0),
        jnp.sum(grad_attend_norm, axis=0),
        jnp.sum(grad_feed_norm, axis=0),
        jnp.sum(all_cotangent.astype(F32), axis=0),
        jnp.sum(grad_expanded.astype(F32), axis=0),
        jnp.sum(grad_linear.astype(F32), axis=0),
    ]
    sums = jnp.concatenate(sums)
    other = swap_cores(sums)
    added = sums + other
    norm_sums = added[: 4 * width].reshape(4, width // 128, blocks, -1).transpose(2, 0, 1, 3)
    residual_sum = added[4 * width : 5 * width].reshape(width // 128, 128)
    lanes = 128 // blocks
    residual_grad = lax.dynamic_slice_in_dim(residual_sum, me * lanes, lanes, 1)
    unit_sum = sums[5 * width : 5 * width + units] + other[5 * width + units : 5 * width + 2 * units]
    unit_sums = lax.dynamic_update_slice_in_dim(
        jnp.zeros((w_in.shape[1],), F32), unit_sum, me * units, 0
    )
    unit_sums = unit_sums.reshape(-1, blocks, lanes).transpose(1, 0, 2)
    line_sum = added[5 * width + 2 * units :].reshape(3, columns)
    line_sums = lax.dynamic_update_slice_in_dim(
        jnp.zeros((3, width), F32), line_sum, me * columns, 1
    )
    line_sums = lax.dynamic_slice_in_dim(line_sums, core * (width // cores), width // cores, 1)
    line_sums = line_sums.reshape(3, -1, blocks, lanes).transpose(2, 0, 1, 3)
    tiny = jnp.concatenate(
        [norm_sums.reshape(blocks, -1), unit_sums.reshape(blocks, -1), line_sums.reshape(blocks, -1)],
        axis=1,
    )
    tiny = jnp.sum(lax.all_to_all(tiny, "blk", 0, 0, tiled=True), axis=0)
    first = norm_gain.size
    gain_grad = tiny[:first].reshape(norm_gain.shape)
    shift_grad = tiny[first : 2 * first].reshape(norm_shift.shape)
    expand_bias_grad = tiny[2 * first : 2 * first + b_in.size].reshape(b_in.shape)
    triple_bias_grad = tiny[2 * first + b_in.size :].reshape(b_qkv.shape)
    return (
        mixed,
        tokens_grad,
        triple_grad,
        triple_bias_grad,
        output_grad,
        residual_grad,
        expand_grad,
        expand_bias_grad,
        shrink_grad,
        residual_grad,
        gain_grad,
        shift_grad,
    )


VMEM = pl.BlockSpec(memory_space=pltpu.VMEM)
SMEM = pl.BlockSpec(memory_space=pltpu.SMEM)
GRANT = 28 * 1024 * 1024
MARK_COS, MARK_SIN = 32, 64
COST = 1.0
WIDE = 256


def run_kernel(kernel, outs, grid=None, ins=None, out_specs=None, scratch=(), flops=0, moved=0, name=None):
    outs = [jax.ShapeDtypeStruct(shape, kind) for shape, kind in outs]
    single = len(outs) == 1
    out_specs = out_specs or [VMEM] * len(outs)
    extra = {} if grid is None else {"grid": grid}
    return pl.pallas_call(
        kernel,
        out_shape=outs[0] if single else outs,
        in_specs=ins,
        out_specs=out_specs[0] if single else out_specs,
        scratch_shapes=list(scratch),
        compiler_params=pltpu.CompilerParams(vmem_limit_bytes=GRANT),
        cost_estimate=pl.CostEstimate(flops=int(flops * COST), bytes_accessed=int(moved * COST), transcendentals=0),
        name=name,
        **extra,
    )


def chunk_bits(half, at, lanes):
    z = at % lanes
    low, high = (at // lanes) % 2, at // (2 * lanes)
    x, y = (high, low) if half == 0 else (low, high)
    return x + 2 * y + 4 * z


class Rows:
    def __init__(self, blocks, cores, rows):
        self.blocks, self.rows = blocks, rows
        self.part = rows // cores
        self.chunk = self.part // 2
        self.half = blocks * self.chunk
        self.count = 2 * self.half
        self.share = self.half
        self.sizes_z = blocks // 4

    def natural(self, me, core, half, at):
        block = me ^ chunk_bits(half, at, self.sizes_z)
        return block * self.rows + core * self.part + half * self.chunk

    def x_rows(self, x):
        h, q = self.half // 2, self.half // 4
        return [
            (x * h, 0, h),
            (self.half + x * q, h, q),
            (self.half + 2 * q + x * q, h + q, q),
        ]

    def pairs(self):
        mine, peer = self.x_rows(0), self.x_rows(1)
        both = [(a[0], b[0], a[2]) for a, b in zip(mine, peer)]
        return both + [(b, a, n) for a, b, n in both]


def nn(left, right):
    return lax.dot_general(left, right, (((1,), (0,)), ((), ())), preferred_element_type=F32)


def nt(left, right):
    return lax.dot_general(left, right, (((1,), (1,)), ((), ())), preferred_element_type=F32)


def lane_of(shape):
    return lax.broadcasted_iota(jnp.int32, shape, len(shape) - 1)


def turn_lanes(values, table, active, sign):
    lane = lane_of(values.shape)
    first, second = lane < ROT // 2, lane < ROT
    cosine = jnp.where(first, pltpu.roll(table, 128 - MARK_COS, 1), table)
    sine_first = pltpu.roll(table, 128 - MARK_SIN, 1)
    sine_second = pltpu.roll(table, 128 - MARK_SIN + ROT // 2, 1)
    sine = jnp.where(first, -sine_first, sine_second) * sign
    cosine = jnp.where(second & active, cosine, 1.0)
    sine = jnp.where(second & active, sine, 0.0)
    partner = jnp.where(first, pltpu.roll(values, 128 - ROT // 2, 1), pltpu.roll(values, ROT // 2, 1))
    return values * cosine + partner * sine


def deal_kernel(cut, blocks, ids, speed, here, there, triple, near, marks, norms, shifts, lines, flip):
    me, core = ids[0], ids[1]
    width = lines.shape[2]
    for source in range(blocks):
        for who, ref in ((core, here), (1 - core, there)):
            at = pl.multiple_of(source * 2 * cut + who * cut, cut)
            for s in range(3):
                triple[pl.ds(at, cut), s * 128 : (s + 1) * 128] = ref[source, s * cut : (s + 1) * cut, :]
            at = pl.multiple_of(who * cut, cut)
            near[pl.ds(at, cut), source * 128 : (source + 1) * 128] = ref[source, 3 * cut : 4 * cut, :]

    lanes = 128 // blocks
    row = lax.broadcasted_iota(jnp.int32, (128, width), 0)
    lane = lane_of((128, width))
    deal = ((row // lanes == lane // 128) & (row % lanes == lane % lanes)).astype(BF)
    lane = lane_of((16, width)) % 128 // lanes
    flip[...] = jnp.zeros_like(flip)
    for which, ref in enumerate((here, there)):
        total = jnp.zeros((16, width), F32)
        for source in range(blocks):
            small = ref[source, 4 * cut : 4 * cut + 16, :]
            total = total + jnp.where(lane == source, nn(small, deal), 0.0)
            if which == 0:
                small = small.astype(F32)
                flip[source : source + 1, :] = small[10:11] * 256.0 + small[11:12]
                flip[blocks + source : blocks + source + 1, :] = small[12:13]
        lines[which] = total
    norms[:4, :] = lines[0, :4, :]
    norms[4:5, :] = lines[0, 4:5, :] + lines[0, 5:6, :]
    norms[5:, :] = jnp.zeros((3, width), F32)
    shifts[...] = jnp.zeros_like(shifts)
    heads = blocks // 2
    ours = me // heads == core
    for s in range(3):
        at = pl.multiple_of((me % heads + s % 2 * heads) * 128, 128)
        both = [lines[k, 6 + s // 2 : 7 + s // 2, pl.ds(at, 128)] for k in (0, 1)]
        shifts[0:1, s * 128 : (s + 1) * 128] = jnp.where(ours, both[0], both[1])
    units = 2 * width // blocks
    at = pl.multiple_of(me % heads * units, units)
    for k in (0, 1):
        shifts[1:2, k * units : (k + 1) * units] = lines[k, pl.ds(8 + me // heads, 1), pl.ds(at, units)]

    turned = flip[...].T
    lane = lane_of((128, 128))
    row = lax.broadcasted_iota(jnp.int32, (128, 128), 0).astype(F32)
    for q in range(blocks // 4):
        place = jnp.zeros((128, 128), F32)
        for g in range(4):
            b = 4 * q + g
            place = jnp.where(lane // 32 == g, row + b * 128.0 - turned[:, b : b + 1], place)
        angle = place * speed[0:1, :]
        cosine, sine = jnp.cos(angle), jnp.sin(angle)
        for g in range(4):
            b = 4 * q + g
            index = row + b * 128.0
            table = jnp.where(lane == 0, index, 0.0)
            table = jnp.where(lane == 1, jnp.where(turned[:, blocks + b : blocks + b + 1] == 1.0, index, -1.0), table)
            table = jnp.where(lane == 2, turned[:, b : b + 1], table)
            table = jnp.where(lane // 32 == 1, pltpu.roll(cosine, (MARK_COS - g * 32) % 128, 1), table)
            table = jnp.where(lane // 32 == 2, pltpu.roll(sine, (MARK_SIN - g * 32) % 128, 1), table)
            marks[b * 128 : (b + 1) * 128, :] = table


def feed_deal_kernel(blocks, units, expand, shrink, out):
    for k in range(blocks):
        out[k, :units, :] = expand[:, k * units : (k + 1) * units].T
        out[k, units:, :] = shrink[k * units : (k + 1) * units, :]


def pick(i, refs, tile):
    for k, ref in enumerate(refs):

        @pl.when(i == k)
        def _(ref=ref):
            tile[...] = ref[...]


def norm_kernel(r, ids, t0, t1, t2, t3, norms, weight, shifts, marks, feed, stats, mine, tile, table, attend):
    i = pl.program_id(0)
    me, core = ids[0], ids[1]
    pick(i, (t0, t1, t2, t3), tile)
    for half in (0, 1):

        @pl.when(i // 2 == half)
        def _(half=half):
            for q in range(8):
                at = r.natural(me, core, half, (i % 2) * 8 + q)
                table[q * r.chunk : (q + 1) * r.chunk, :] = marks[pl.ds(pl.multiple_of(at, r.chunk), r.chunk), :]

    step = 16
    lane = lane_of((step, 128))

    @pl.loop(0, tile.shape[0] // step, unroll=4)
    def _(j):
        rows = pl.ds(pl.multiple_of(j * step, step), step)
        values = tile[rows, :].astype(F32)
        mean = jnp.mean(values, axis=-1, keepdims=True)
        center = values - mean
        inverse = lax.rsqrt(jnp.mean(center * center, axis=-1, keepdims=True) + EPSILON)
        value = center * inverse
        attend[rows, :] = (value * norms[0:1, :] + norms[2:3, :]).astype(BF)
        feed[rows, :] = (value * norms[1:2, :] + norms[3:4, :]).astype(BF)
        stats[rows, :] = jnp.where(lane == 0, mean, inverse)

    linear = nn(attend[...], weight[...]) + shifts[0:1, :384]
    active = me % 2 == 0
    for s in (0, 1):
        cols = slice(s * 128, (s + 1) * 128)
        mine[:, cols] = turn_lanes(linear[:, cols], table[...], active, 1.0).astype(BF)
    mine[:, 256:] = linear[:, 256:].astype(BF)


def normal_of(tile, stats):
    return (tile.astype(F32) - stats[:, 0:1]) * stats[:, 1:2]


def gather_columns(r, out, low, high, column):
    cols = slice(column * 128, (column + 1) * 128)
    out[:, :128] = low[:, cols]
    for here, there, size in r.pairs():
        out[here : here + size, 128:] = high[there : there + size, cols]


def gather_marks(r, ids, marks, table, line):
    me, core = ids[0], ids[1]
    for w in (0, 1):
        who = core if w == 0 else 1 - core
        for half in (0, 1):
            for q in range(16):
                at = r.natural(me, who, half, q)
                to = w * r.count + half * r.half + q * r.chunk
                table[to : to + r.chunk, :] = marks[pl.ds(pl.multiple_of(at, r.chunk), r.chunk), :]
    for b in range(2 * r.count // 128):
        line[:, b * 128 : (b + 1) * 128] = table[b * 128 : (b + 1) * 128, :].T[:8, :]


def own_rows(r, out, ref, columns=slice(None)):
    for row, place, size in r.x_rows(0):
        out[place : place + size, :] = ref[row : row + size, columns]


def query_kernel(r, scale, ids, a00, a01, a10, a11, grads, marks, attended, keep, send, lines,
                 keys, values, queries, pushes, table, line, mine):
    i = pl.program_id(0)
    me = ids[0]
    count, tile = r.count, r.share // 2

    @pl.when(i == 0)
    def _():
        gather_columns(r, keys.at[:count], a00, a01, 1)
        gather_columns(r, keys.at[count:], a10, a11, 1)
        gather_columns(r, values.at[:count], a00, a01, 2)
        gather_columns(r, values.at[count:], a10, a11, 2)
        for row, place, size in r.x_rows(0):
            queries[place : place + size, :128] = a00[row : row + size, :128]
        for (row, place, size), (there, _, _) in zip(r.x_rows(0), r.x_rows(1)):
            queries[place : place + size, 128:] = a01[there : there + size, :128]
        own_rows(r, pushes, grads)
        gather_marks(r, ids, marks, table, line)
        own_rows(r, mine, table.at[:count])

    rows = pl.ds(pl.multiple_of(i * tile, tile), tile)
    mark = mine[rows, :]
    q_at, q_start = mark[:, 0:1], mark[:, 2:3]
    k_at, k_live = line[0:1, :], line[1:2, :]
    mask = ((k_live >= q_start) & (k_at <= q_at)) | (k_at == q_at)
    scores = jnp.where(mask, nt(queries[rows, :], keys[...]) * scale, NEGATIVE)
    top = jnp.max(scores, axis=-1, keepdims=True)
    weight = jnp.where(mask, jnp.exp(scores - top), 0.0)
    total = jnp.sum(weight, axis=-1, keepdims=True)
    prob = weight * (1.0 / total)
    result = nn(prob.astype(BF), values[...])
    grad = pushes[rows, :]
    delta = jnp.sum(grad.astype(F32) * result, axis=-1, keepdims=True)
    slope = (prob * (nt(grad, values[...]) - delta)).astype(BF)
    back = nn(slope, keys[...]) * scale
    result = result.astype(BF)
    attended[...] = result
    for k, ref in enumerate((keep, send)):
        cols = slice(k * 128, (k + 1) * 128)
        ref[:, :128] = turn_lanes(back[:, cols], mark, me % 2 == k, -1.0).astype(BF)
        ref[:, 128:] = result[:, cols]
    lane = lane_of((tile, 128))
    both = jnp.where(lane == 0, top + jnp.log(total), jnp.where(lane == 1, delta, 0.0))
    for b in range(tile // 128):
        lines[:, b * 128 : (b + 1) * 128] = both[b * 128 : (b + 1) * 128, :].T[:8, :]


def key_kernel(r, scale, ids, a00, a01, a10, a11, grads, other_grads, l00, l01, l10, l11, marks, keep, send,
               queries, pushes, keys, values, table, line, mine, tops):
    i = pl.program_id(0)
    me = ids[0]
    count, tile = r.count, r.share // 2

    @pl.when(i == 0)
    def _():
        gather_columns(r, queries.at[:count], a00, a01, 0)
        gather_columns(r, queries.at[count:], a10, a11, 0)
        pushes[:count, :] = grads[...]
        pushes[count:, :] = other_grads[...]
        for k, out in ((1, keys), (2, values)):
            cols = slice(k * 128, (k + 1) * 128)
            for row, place, size in r.x_rows(0):
                out[place : place + size, :128] = a00[row : row + size, cols]
            for (row, place, size), (there, _, _) in zip(r.x_rows(0), r.x_rows(1)):
                out[place : place + size, 128:] = a01[there : there + size, cols]
        gather_marks(r, ids, marks, table, line)
        own_rows(r, mine, table.at[:count])
        for base, low, high in ((0, l00, l01), (count, l10, l11)):
            for x, ref in ((0, low), (1, high)):
                for row, place, size in r.x_rows(x):
                    tops[:, base + row : base + row + size] = ref[:, place : place + size]

    rows = pl.ds(pl.multiple_of(i * tile, tile), tile)
    mark = mine[rows, :]
    k_at, k_live = mark[:, 0:1], mark[:, 1:2]
    q_at, q_start = line[0:1, :], line[2:3, :]
    mask = ((k_live >= q_start) & (k_at <= q_at)) | (k_at == q_at)
    scores = nt(keys[rows, :], queries[...]) * scale
    prob = jnp.where(mask, jnp.exp(scores - tops[0:1, :]), 0.0)
    grad_values = nn(prob.astype(BF), pushes[...])
    slope = (prob * (nt(values[rows, :], pushes[...]) - tops[1:2, :])).astype(BF)
    back = nn(slope, queries[...]) * scale
    for k, ref in enumerate((keep, send)):
        cols = slice(k * 128, (k + 1) * 128)
        ref[:, :128] = turn_lanes(back[:, cols], mark, me % 2 == k, -1.0).astype(BF)
        ref[:, 128:] = grad_values[:, cols].astype(BF)


def feed_kernel(units, blocks, normed, c0, c1, c2, c3, mine, other, shifts, near, peer,
                act, grad, act_turned, grad_turned, expand, shrink, sums, pushes, push_sums, tile, turned):
    i = pl.program_id(0)

    @pl.when(i == 0)
    def _():
        sums[...] = jnp.zeros_like(sums)
        push_sums[...] = jnp.zeros_like(push_sums)
        turned[:, :128] = near[...].T
        turned[:, 128:] = peer[...].T
        for source in range(blocks):
            cols = slice(source * 128, (source + 1) * 128)
            for at, ref in ((0, mine), (units, other)):
                expand[at : at + units, cols] = ref[source, :units, :]
                shrink[at : at + units, cols] = ref[source, units:, :]

    pick(i, (c0, c1, c2, c3), tile)
    pushes[...] = nn(tile[...], turned[...]).astype(BF)
    expanded = nt(normed[...], expand[...]) + shifts[1:2, : 2 * units]
    activated, bend = gelu_and_slope(expanded)
    activated = activated.astype(BF)
    act[...] = activated
    act_turned[...] = activated.T
    slope = (bend * nt(tile[...], shrink[...])).astype(BF)
    grad[...] = slope
    grad_turned[...] = slope.T
    sums[0:1, :] += jnp.sum(slope.astype(F32), axis=0, keepdims=True)
    push_sums[0:1, :] += jnp.sum(tile[...].astype(F32), axis=0, keepdims=True)


def by_quarter(left, quarters):
    size = quarters[0].shape[0]
    total = nn(left[:, :size], quarters[0][...])
    for k in range(1, len(quarters)):
        total = total + nn(left[:, k * size : (k + 1) * size], quarters[k][...])
    return total


def outer_kernel(units, grad_turned, act_turned, normed, c0, c1, c2, c3, *rest):
    out = rest[-1]
    for k in (0, 1):
        result = by_quarter(act_turned, (c0, c1, c2, c3)) if k else nn(grad_turned[...], normed[...])
        for b in range(WIDE // 128):
            lanes = slice(b * 128, (b + 1) * 128)
            rows = slice(k * units, (k + 1) * units)
            part = result[:, lanes]
            if len(rest) > 1:
                part = part + rest[0][b, rows, :].astype(F32)
            out[b, rows, :] = part.astype(BF)


def branch_kernel(r, act, attended, shrink, near, peer, o0, o1, o2, o3):
    outs = (o0, o1, o2, o3)
    size = r.count // 4
    extra = nn(attended[:, :128], near[...]) + nn(attended[:, 128:], peer[...])
    for k in range(4):
        result = nn(act[k * size : (k + 1) * size, :], shrink[...])
        covered = False
        for row, place, length in r.x_rows(0):
            if row == k * size:
                outs[k][:length, :] = (result[:length] + extra[place : place + length]).astype(BF)
                if length < size:
                    outs[k][length:, :] = result[length:].astype(BF)
                covered = True
        if not covered:
            outs[k][...] = result.astype(BF)


def inputs_kernel(r, keep1, keep2, got1, got2, grad, t0, t1, t2, t3, stats, triple, expand, gains, cotangent_sums, unit_sums,
                  o0, o1, o2, o3, linear, near, sums, line_sums):
    j = pl.program_id(0)
    size = r.count // 4

    @pl.when(j == 0)
    def _():
        for x, one, two in ((0, keep1, keep2), (1, got1, got2)):
            for row, place, length in r.x_rows(x):
                linear[row : row + length, :128] = one[place : place + length, :128]
                linear[row : row + length, 128:] = two[place : place + length, :]
                near[row : row + length, :] = one[place : place + length, 128:]
        line_sums[...] = jnp.zeros_like(line_sums)
        line_sums[0:1, :384] = jnp.sum(linear[...].astype(F32), axis=0, keepdims=True)

    sums[...] = jnp.zeros_like(sums)
    for k, (ref, tokens) in enumerate(((o0, t0), (o1, t1), (o2, t2), (o3, t3))):
        rows = slice(k * size, (k + 1) * size)
        attend = nt(linear[rows, :], triple[...])
        feed = nn(grad[rows, :], expand[...])
        value = normal_of(tokens[...], stats[rows, :])
        sums[0:1, :] += jnp.sum(value * attend, axis=0, keepdims=True)
        sums[1:2, :] += jnp.sum(value * feed, axis=0, keepdims=True)
        sums[2:3, :] += jnp.sum(attend, axis=0, keepdims=True)
        sums[3:4, :] += jnp.sum(feed, axis=0, keepdims=True)
        ref[...] = (gains[0:1, :] * attend + gains[1:2, :] * feed).astype(BF)
    sums[4:5, :] = cotangent_sums[0:1, :]
    for k in (0, 1):

        @pl.when(j == k)
        def _(k=k):
            sums[5:6, :] = line_sums[0:1, k * WIDE : (k + 1) * WIDE]
            sums[6:7, :] = unit_sums[0:1, k * WIDE : (k + 1) * WIDE]


def small_kernel(blocks, units, ids, mine, other, out, lines):
    me, core = ids[0], ids[1]
    width = lines.shape[1]
    heads, lanes = blocks // 2, 128 // blocks
    lines[...] = jnp.zeros_like(lines)
    lines[0:5, :] = mine[0:5, :] + other[0:5, :]
    ours = jnp.where(me // heads == core, 1.0, 0.0)
    for s in range(3):
        at = pl.multiple_of((me % heads + s % 2 * heads) * 128, 128)
        cols = slice(s * 128, (s + 1) * 128)
        lines[6 + s // 2 : 7 + s // 2, pl.ds(at, 128)] = (mine[5:6, cols] + other[5:6, cols]) * ours
    at = pl.multiple_of(me % heads * units, units)
    total = mine[6:7, :units] + other[6:7, units : 2 * units]
    for k in (0, 1):

        @pl.when(me // heads == k)
        def _(k=k):
            lines[8 + k : 9 + k, pl.ds(at, units)] = total

    row = lax.broadcasted_iota(jnp.int32, (width, 128), 0)
    lane = lane_of((width, 128))
    deal = ((lane // lanes == row // 128) & (lane % lanes == row % lanes)).astype(BF)
    value = lines[...]
    high = value.astype(BF)
    low = (value - high.astype(F32)).astype(BF)
    lane = lane_of((16, width)) % 128 // lanes
    line = lax.broadcasted_iota(jnp.int32, (16, width), 0)
    for b in range(blocks):
        sent = (lane == b) & ((line != 4) | (me == b))
        for k, part in enumerate((high, low)):
            part = jnp.where(sent, part.astype(F32), 0.0).astype(BF)
            out[b, k * 16 : (k + 1) * 16, :] = nn(part, deal).astype(BF)


def fold_kernel(keep1, got1, keep2, got2, one, one_send, two, two_send):
    for keep, got, outs in ((keep1, got1, (one, one_send)), (keep2, got2, (two, two_send))):
        half = outs[0].shape[0]
        for k, out in enumerate(outs):
            rows = slice(k * half, (k + 1) * half)
            out[...] = (keep[rows, :].astype(F32) + got[rows, :].astype(F32)).astype(BF)


def by_z_kernel(chunk, one, one_got, two, two_got, *outs):
    for half, (mine, got) in enumerate(((one, one_got), (two, two_got))):
        for z, out in enumerate(outs):
            rows = slice(z * chunk, (z + 1) * chunk)
            value = mine[rows, :].astype(F32) + got[rows, :].astype(F32)
            out[half * chunk : (half + 1) * chunk, :] = value.astype(BF)


def line_outer_kernel(cut, ids, linear, near, t0, t1, t2, t3, stats, norms, c0, c1, c2, c3,
                      keep, give, turned, near_turned, normed, result):
    core = ids[1]

    @pl.when(pl.program_id(0) == 0)
    def _():
        turned[...] = linear[...].T
        near_turned[...] = near[...].T

    size = t0.shape[0]
    for k, tokens in enumerate((t0, t1, t2, t3)):
        rows = slice(k * size, (k + 1) * size)
        value = normal_of(tokens[...], stats[rows, :])
        normed[rows, :] = (value * norms[0:1, :] + norms[2:3, :]).astype(BF)
    result[:384, :] = nn(turned[...], normed[...])
    result[384:, :] = by_quarter(near_turned, (c0, c1, c2, c3))
    for who, out in ((core, keep), (1 - core, give)):
        for s in range(4):
            at = pl.multiple_of(s * 2 * cut + who * cut, cut)
            for b in range(WIDE // 128):
                part = result[pl.ds(at, cut), b * 128 : (b + 1) * 128]
                out[b, s * cut : (s + 1) * cut, :] = part.astype(out.dtype)


def unpack_kernel(cut, heads, ids, mine, other, whole, triple, outward, small, pair):
    core = ids[1]
    for k in range(heads):
        for s in range(4):
            for who, ref in ((core, mine), (1 - core, other)):
                pair[pl.ds(pl.multiple_of(who * cut, cut), cut), :] = ref[k, s * cut : (s + 1) * cut, :].astype(F32)
            if s < 3:
                triple[s, :, k * 128 : (k + 1) * 128] = pair[...].T
            else:
                outward[k * 128 : (k + 1) * 128, :] = pair[...]
    total = jnp.zeros(small.shape, F32)
    for b in range(2 * heads):
        for k in (0, 1):
            at = 4 * cut + 16 * k
            total = total + whole[b, at : at + 16, :].astype(F32)
    small[...] = total


def feed_unpack_kernel(units, got, expand, shrink):
    k = pl.program_id(0)
    expand[...] = got[0, :units, :].astype(F32).T
    shrink[...] = got[0, units:, :].astype(F32)


def join(*values):
    return lax.optimization_barrier(values)


def body(
    tokens,
    w_qkv,
    b_qkv,
    w_out,
    b_out,
    w_in,
    b_in,
    w_out2,
    b_out2,
    norm_gain,
    norm_shift,
    doc_start,
    live,
    cotangent,
):
    blocks = lax.axis_size("blk")
    cores = lax.axis_size("tp")
    me, core = lax.axis_index("blk"), lax.axis_index("tp")
    ids = jnp.stack([me, core]).astype(jnp.int32)
    rows, width = tokens.shape
    depth = w_in.shape[0]
    r = Rows(blocks, cores, rows)
    part, count, share = r.part, r.count, r.share
    quarter = count // 4
    units = w_in.shape[1] // blocks
    cut = depth // cores
    own_heads = HEADS // cores * 2
    scale = 1.0 / math.sqrt(HEAD)
    masks_z = [4 * i for i in range(1, blocks // 4)]
    grid = (width // WIDE,)

    once = pl.Buffered(1)

    def tiled(columns):
        return pl.BlockSpec((quarter, columns), lambda i: (i, 0))

    def across(lines):
        return pl.BlockSpec((lines, WIDE), lambda j: (0, j))

    def fixed(value):
        return pl.BlockSpec(value.shape, lambda i: (0,) * value.ndim, pipeline_mode=once)

    def fixed_shape(*shape):
        return pl.BlockSpec(shape, lambda i: (0,) * len(shape))

    def packed_rows(value, lines):
        flat = value.reshape(-1)
        return jnp.pad(flat, (0, lines * 128 - flat.size)).reshape(lines, 128)

    small = jnp.concatenate(
        [
            packed_rows(norm_gain, 2),
            packed_rows(norm_shift, 2),
            packed_rows(b_out, 1),
            packed_rows(b_out2, 1),
            packed_rows(b_qkv, 2),
            packed_rows(b_in, 2),
            jnp.stack([doc_start // 256, doc_start % 256, live]).astype(BF),
            jnp.zeros((3, 128), BF),
        ]
    )

    def over_z(value):
        return [from_peer(value, mask) for mask in masks_z]

    def halves(pieces):
        one = jnp.concatenate([value[: r.chunk] for value in pieces])
        two = jnp.concatenate([value[r.chunk :] for value in pieces])
        return one, two

    my_tokens = lax.dynamic_slice_in_dim(tokens, core * part, part, 0)
    my_cotangent = lax.dynamic_slice_in_dim(cotangent, core * part, part, 0)
    triple = w_qkv.reshape(3, cores, cut, own_heads, 128).transpose(1, 3, 0, 2, 4)
    triple = triple.reshape(cores, own_heads, 3 * cut, 128)
    outward = w_out.reshape(own_heads, cores, cut, 128).transpose(1, 0, 2, 3)
    dealt = jnp.concatenate([triple, outward], axis=2)
    keep = lax.dynamic_index_in_dim(dealt, core, 0, keepdims=False)
    give = lax.dynamic_index_in_dim(dealt, 1 - core, 0, keepdims=False)
    feed_deal = run_kernel(
        lambda *refs: feed_deal_kernel(blocks, units, *refs),
        [((blocks, 2 * units, depth), BF)],
        ins=[VMEM, VMEM],
        name="feed_deal",
        moved=4e6,
    )(w_in, w_out2)
    tokens_z = join(my_tokens, *over_z(my_tokens))
    keep, got, feed_deal, my_cotangent, *tokens_z = join(keep, swap_cores(give), feed_deal, my_cotangent, *tokens_z)

    heads_low, heads_high = by_core(core, keep, got)
    deal = jnp.concatenate(
        [
            jnp.concatenate([heads_low, heads_high]),
            jnp.broadcast_to(small, (blocks,) + small.shape),
        ],
        axis=1,
    )
    here = lax.all_to_all(deal, "blk", 0, 0, tiled=True)
    one, two = halves(tokens_z)
    cotangent_z = over_z(my_cotangent)
    one, one_y, two, two_x = join(one, from_peer(one, 2), two, from_peer(two, 1))

    one, two = jnp.concatenate([one, one_y]), jnp.concatenate([two, two_x])
    mine_one, mine_two = halves(join(my_cotangent, *cotangent_z))
    here, feed_deal, one, one_x, two, two_y, mine_one, mine_y, mine_two, mine_x = join(
        here,
        feed_deal,
        one,
        from_peer(one, 1),
        two,
        from_peer(two, 2),
        mine_one,
        from_peer(mine_one, 2),
        mine_two,
        from_peer(mine_two, 1),
    )
    all_tokens = [one, one_x, two, two_y]

    one, two = jnp.concatenate([mine_one, mine_y]), jnp.concatenate([mine_two, mine_x])
    here, there = join(here, swap_cores(here))
    steps = jnp.arange(ROT // 2, dtype=F32)
    speed = jnp.tile(10000.0 ** (-2.0 * steps / ROT), 4).reshape(1, 128)
    w_triple, w_near, marks, norms, shifts = run_kernel(
        lambda *refs: deal_kernel(cut, blocks, *refs),
        [
            ((width, 384), BF),
            ((128, width), BF),
            ((blocks * rows, 128), F32),
            ((8, width), F32),
            ((8, 512), F32),
        ],
        ins=[SMEM, VMEM, VMEM, VMEM],
        scratch=[pltpu.VMEM((2, 16, width), F32), pltpu.VMEM((128, 128), F32)],
        name="deal",
        moved=8e6,
    )(ids, speed, here, there)
    norms, feed_deal = join(norms, feed_deal)
    feed_mine = lax.all_to_all(feed_deal, "blk", 0, 0, tiled=True)
    normed_feed, stats, mine = run_kernel(
        lambda *refs: norm_kernel(r, *refs),
        [((count, width), BF), ((count, 128), F32), ((count, 384), BF)],
        grid=(4,),
        ins=[SMEM] + [fixed(t) for t in all_tokens] + [fixed(norms), fixed(w_triple), fixed(shifts), fixed(marks)],
        out_specs=[tiled(width), tiled(128), tiled(384)],
        scratch=[pltpu.VMEM((quarter, width), BF), pltpu.VMEM((quarter, 128), F32), pltpu.VMEM((quarter, width), BF)],
        flops=2 * count * width * 384,
        name="norm",
        moved=22e6,
    )(ids, *all_tokens, norms, w_triple, shifts, marks)
    w_peer = from_peer(w_near, 1)
    mine, one, one_x, two, two_y = join(mine, one, from_peer(one, 1), two, from_peer(two, 2))

    peer, mine_there = from_peer(mine, 1), swap_cores(mine)
    all_cotangent = [one, one_x, two, two_y]
    feed_mine, w_peer, *all_cotangent = join(feed_mine, w_peer, *all_cotangent)

    feed_mine, feed_other = join(feed_mine, swap_cores(feed_mine))

    turned = pl.BlockSpec((2 * units, quarter), lambda i: (0, i))
    act, grad, act_turned, grad_turned, w_expand, w_shrink, unit_sums, grads, cotangent_sums = run_kernel(
        lambda *refs: feed_kernel(units, blocks, *refs),
        [((count, 2 * units), BF)] * 2
        + [((2 * units, count), BF)] * 2
        + [((2 * units, width), BF)] * 2
        + [((8, 2 * units), F32), ((count, 256), BF), ((8, width), F32)],
        grid=(4,),
        ins=[tiled(width)]
        + [fixed(t) for t in all_cotangent]
        + [fixed(feed_mine), fixed(feed_mine), fixed(shifts), fixed(w_near), fixed(w_peer)],
        out_specs=[tiled(2 * units)] * 2
        + [turned] * 2
        + [fixed_shape(2 * units, width)] * 2
        + [fixed_shape(8, 2 * units), tiled(256), fixed_shape(8, width)],
        scratch=[pltpu.VMEM((quarter, width), BF), pltpu.VMEM((width, 256), BF)],
        flops=8 * count * width * units,
        name="feed",
        moved=20e6,
    )(normed_feed, *all_cotangent, feed_mine, feed_other, shifts, w_near, w_peer)
    mine, peer, mine_there, act_turned, grad_turned = join(mine, peer, mine_there, act_turned, grad_turned)

    dealt_spec = pl.BlockSpec((WIDE // 128, 2 * units, 128), lambda j: (j, 0, 0))

    def outer(half, *extra):
        some = pl.BlockSpec((units, count), lambda j: (half, 0))
        return run_kernel(
            lambda *refs: outer_kernel(units, *refs),
            [((blocks, 2 * units, 128), BF)],
            grid=grid,
            ins=[some, some, across(count)] + [across(quarter)] * 4 + [dealt_spec] * len(extra),
            out_specs=[dealt_spec],
            flops=4 * count * width * units,
            name="outer",
            moved=12e6,
        )(grad_turned, act_turned, normed_feed, *all_cotangent, *extra)

    peer_there, feed_sent, grads = join(swap_cores(peer), outer(1), grads)

    tile = share // 2
    half_tile = lambda columns: pl.BlockSpec((tile, columns), lambda i: (i, 0))
    line_tile = pl.BlockSpec((8, tile), lambda i: (0, i))
    four = [mine, peer, mine_there, peer_there]
    common = [
        pltpu.VMEM((2 * count, 256), BF),
        pltpu.VMEM((2 * count, 256), BF),
        pltpu.VMEM((share, 256), BF),
        pltpu.VMEM((share, 256), BF),
        pltpu.VMEM((2 * count, 128), F32),
        pltpu.VMEM((8, 2 * count), F32),
        pltpu.VMEM((share, 128), F32),
    ]
    attended, keep1, send1, lines = run_kernel(
        lambda *refs: query_kernel(r, scale, *refs),
        [((share, 256), BF)] * 3 + [((8, share), F32)],
        grid=(2,),
        ins=[SMEM] + [fixed(mine)] * 4 + [fixed(grads), fixed(marks)],
        out_specs=[half_tile(256)] * 3 + [line_tile],
        scratch=common,
        flops=8 * share * 2 * count * 256,
        name="query",
        moved=6e6,
    )(ids, *four, grads, marks)
    feed_got, grads_there, attended, send1, lines = join(
        swap_cores(feed_sent), swap_cores(grads), attended, send1, lines
    )

    diagonal = [(2 * b + c, 2 * (b ^ 1) + 1 - c) for b in range(blocks) for c in (0, 1)]
    lines_peer, lines_there = from_peer(lines, 1), swap_cores(lines)
    lines_far = lax.ppermute(lines, ("blk", "tp"), diagonal)
    feed_grads = outer(0, feed_got)
    feed_grads, lines, lines_peer, lines_there, lines_far = join(feed_grads, lines, lines_peer, lines_there, lines_far)

    keep2, send2 = run_kernel(
        lambda *refs: key_kernel(r, scale, *refs),
        [((share, 256), BF)] * 2,
        grid=(2,),
        ins=[SMEM] + [fixed(mine)] * 4 + [fixed(grads)] * 2 + [fixed(lines)] * 4 + [fixed(marks)],
        out_specs=[half_tile(256)] * 2,
        scratch=common + [pltpu.VMEM((8, 2 * count), F32)],
        flops=8 * share * 2 * count * 256,
        name="key",
        moved=6e6,
    )(ids, *four, grads, grads_there, lines, lines_peer, lines_there, lines_far, marks)
    send2, feed_grads, attended = join(send2, feed_grads, attended)
    feed_dealt = lax.all_to_all(feed_grads, "blk", 0, 0, tiled=True)
    branches = run_kernel(
        lambda *refs: branch_kernel(r, *refs),
        [((quarter, width), BF)] * 4,
        grid=grid,
        ins=[fixed(act), fixed(attended), across(2 * units), across(128), across(128)],
        out_specs=[across(quarter)] * 4,
        flops=2 * count * width * (2 * units + 128),
        name="branch",
        moved=9e6,
    )(act, attended, w_shrink, w_near, w_peer)
    got1, got2, *branches = join(from_peer(send1, 1), from_peer(send2, 1), *branches)
    mixed_one, mixed_two = from_peer(branches[1], 1), from_peer(branches[3], 2)

    def fold(*refs):
        return run_kernel(
            fold_kernel,
            [((quarter // 2, width), BF)] * 4,
            grid=grid,
            ins=[across(quarter)] * 4,
            out_specs=[across(quarter // 2)] * 4,
            name="fold",
            moved=6e6,
        )(*refs)

    def by_z(*refs):
        return run_kernel(
            lambda *refs: by_z_kernel(r.chunk, *refs),
            [((part, width), BF)] * (1 + len(masks_z)),
            grid=grid,
            ins=[across(quarter // 2)] * 4,
            out_specs=[across(part)] * (1 + len(masks_z)),
            name="by_z",
            moved=3e6,
        )(*refs)

    def total(pieces, got):
        value = pieces[0].astype(F32)
        for piece in got:
            value = value + piece.astype(F32)
        return value

    def pieces_over_z(pieces):
        return [from_peer(piece, mask) for piece, mask in zip(pieces[1:], masks_z)]

    *combined, grad_linear, attended_near, sums, _ = run_kernel(
        lambda *refs: inputs_kernel(r, *refs),
        [((quarter, width), BF)] * 4 + [((count, 384), BF), ((count, 128), BF), ((8, width), F32), ((8, 512), F32)],
        grid=grid,
        ins=[fixed(keep1)] * 4
        + [fixed(grad)]
        + [across(quarter)] * 4
        + [fixed(stats), pl.BlockSpec((WIDE, 384), lambda j: (j, 0)), across(2 * units)]
        + [across(8), across(8), fixed(unit_sums)],
        out_specs=[across(quarter)] * 4
        + [fixed_shape(count, 384), fixed_shape(count, 128), across(8), fixed_shape(8, 512)],
        flops=2 * count * width * (384 + 2 * units),
        name="inputs",
        moved=16e6,
    )(keep1, keep2, got1, got2, grad, *all_tokens, stats, w_triple, w_expand, norms, cotangent_sums, unit_sums)
    grad_linear, sums, *combined = join(grad_linear, sums, *combined)

    got_one, got_two = from_peer(combined[1], 1), from_peer(combined[3], 2)
    line_spec = pl.BlockSpec((WIDE // 128, 4 * cut, 128), lambda j: (j, 0, 0))
    keep, give = run_kernel(
        lambda *refs: line_outer_kernel(cut, *refs),
        [((blocks, 4 * cut, 128), F32), ((blocks, 4 * cut, 128), BF)],
        grid=grid,
        ins=[SMEM, fixed(grad_linear), fixed(attended_near)]
        + [across(quarter)] * 4
        + [fixed(stats), across(8)]
        + [across(quarter)] * 4,
        out_specs=[line_spec] * 2,
        scratch=[
            pltpu.VMEM((384, count), BF),
            pltpu.VMEM((128, count), BF),
            pltpu.VMEM((count, WIDE), BF),
            pltpu.VMEM((512, WIDE), F32),
        ],
        flops=2 * count * width * 512,
        name="line_outer",
        moved=12e6,
    )(ids, grad_linear, attended_near, *all_tokens, stats, norms, *all_cotangent)
    mixed_one, mixed_two, keep, give, sums, sums_other = join(
        mixed_one, mixed_two, keep, give, sums, swap_cores(sums)
    )

    one, one_send, two, two_send = fold(branches[0], mixed_one, branches[2], mixed_two)
    small = run_kernel(
        lambda *refs: small_kernel(blocks, units, *refs),
        [((blocks, 32, 128), BF)],
        ins=[SMEM, VMEM, VMEM],
        scratch=[pltpu.VMEM((16, width), F32)],
        name="small",
        moved=1e6,
    )(ids, sums, sums_other)
    got, small, one, one_send, two, two_send = join(swap_cores(give), small, one, one_send, two, two_send)
    mixed_one, mixed_two = from_peer(one_send, 2), from_peer(two_send, 1)
    dealt = jnp.concatenate([(keep + got.astype(F32)).astype(BF), small], axis=1)
    dealt, feed_dealt = join(dealt, feed_dealt)
    dealt = lax.all_to_all(dealt, "blk", 0, 0, tiled=True)
    expand_grad, shrink_grad = run_kernel(
        lambda *refs: feed_unpack_kernel(units, *refs),
        [(w_in.shape, F32), (w_out2.shape, F32)],
        grid=(blocks,),
        ins=[pl.BlockSpec((1, 2 * units, 128), lambda k: (k, 0, 0))],
        out_specs=[pl.BlockSpec((depth, units), lambda k: (0, k)), pl.BlockSpec((units, depth), lambda k: (k, 0))],
        name="feed_unpack",
        moved=6e6,
    )(feed_dealt)
    got_one, got_two, mixed_one, mixed_two, expand_grad, shrink_grad = join(
        got_one, got_two, mixed_one, mixed_two, expand_grad, shrink_grad
    )
    mixed_pieces = by_z(one, mixed_one, two, mixed_two)
    one, one_send, two, two_send, *mixed_pieces = join(
        *fold(combined[0], got_one, combined[2], got_two), *mixed_pieces
    )
    got_one, got_two, *mixed_got = join(
        from_peer(one_send, 2), from_peer(two_send, 1), *pieces_over_z(mixed_pieces)
    )

    joined = join(*by_z(one, got_one, two, got_two), *mixed_got)
    pieces, mixed_got = joined[: 1 + len(masks_z)], joined[1 + len(masks_z) :]
    combined_got = pieces_over_z(pieces)

    def whole_block(value):
        return jnp.concatenate(by_core(core, value, swap_cores(value)))

    my_inputs = my_tokens.astype(F32)
    mixed = whole_block((my_inputs + total(mixed_pieces, mixed_got) + norms[4:5, :]).astype(BF))
    dealt, mixed = join(dealt, mixed)
    keep = lax.dynamic_slice_in_dim(dealt, core * own_heads, own_heads, 0)
    give = lax.dynamic_slice_in_dim(dealt, (1 - core) * own_heads, own_heads, 0)
    triple_grad, output_grad, small = run_kernel(
        lambda *refs: unpack_kernel(cut, own_heads, *refs),
        [((3, depth, own_heads * 128), F32), ((own_heads * 128, depth), F32), ((16, 128), F32)],
        ins=[SMEM, VMEM, VMEM, VMEM],
        scratch=[pltpu.VMEM((128, 128), F32)],
        name="unpack",
        moved=4e6,
    )(ids, keep, swap_cores(give), dealt)
    small = small.reshape(16, 16, -1)
    residual_grad = small[4]
    small, triple_grad, output_grad, *combined_got = join(small, triple_grad, output_grad, *combined_got)

    combined_sum = total(pieces, combined_got)
    my_center = my_inputs - jnp.mean(my_inputs, axis=-1, keepdims=True)
    my_inverse = lax.rsqrt(jnp.mean(my_center * my_center, axis=-1, keepdims=True) + EPSILON)
    my_normal = my_center * my_inverse
    my_grad = my_inverse * (
        combined_sum
        - jnp.mean(combined_sum, axis=-1, keepdims=True)
        - my_normal * jnp.mean(combined_sum * my_normal, axis=-1, keepdims=True)
    )
    tokens_grad = whole_block((my_cotangent.astype(F32) + my_grad).astype(BF))
    return (
        mixed,
        tokens_grad,
        triple_grad,
        small[6:8].reshape(32, -1)[:24].reshape(b_qkv.shape),
        output_grad,
        residual_grad,
        expand_grad,
        small[8:10].reshape(b_in.shape),
        shrink_grad,
        residual_grad,
        small[0:2],
        small[2:4],
    )


def solution(mesh):
    placed = (
        P("blk", None),
        P(None, "blk", "tp"),
        P(None, "tp", "blk"),
        P("tp", "blk"),
        P(None, "blk"),
        P("blk", "tp"),
        P("tp", "blk"),
        P("tp", "blk"),
        P(None, "blk"),
        P(None, None, "blk"),
        P(None, None, "blk"),
        P("blk"),
        P("blk"),
        P("blk", None),
    )
    two_to_a_head = mesh.shape["blk"] == 2 * HEADS
    return jax.shard_map(
        body if two_to_a_head else general_body,
        mesh=mesh,
        in_specs=placed,
        out_specs=(
            P("blk", None),
            P("blk", None),
            P(None, "blk", "tp"),
            P(None, "tp", "blk"),
            P("tp", "blk"),
            P(None, "blk"),
            P("blk", "tp"),
            P("tp", "blk"),
            P("tp", "blk"),
            P(None, "blk"),
            P(None, None, "blk"),
            P(None, None, "blk"),
        ),
        check_vma=False,
    )
```

```python
import math

import jax
import jax.numpy as jnp
from jax import lax
from jax.experimental import pallas as pl
from jax.experimental.pallas import tpu as pltpu
from jax.sharding import PartitionSpec as P

HEADS = 8
HEAD = 256
ROT = 64

EPSILON = 1e-05
NEGATIVE = -1e30
BF = jnp.bfloat16
F32 = jnp.float32


def dot(left, right, dims):
    return lax.dot_general(left, right, (dims, ((), ())), preferred_element_type=F32)


def swap_cores(value):
    return lax.ppermute(value, "tp", [(0, 1), (1, 0)])


def from_peer(value, mask):
    count = lax.axis_size("blk")
    return lax.ppermute(value, "blk", [(i, i ^ mask) for i in range(count)])


def spread(value, masks):
    return jnp.stack([value] + [from_peer(value, mask) for mask in masks])


def collect(parts, masks):
    total = parts[0].astype(F32)
    for at, mask in enumerate(masks):
        total = total + from_peer(parts[at + 1], mask).astype(F32)
    return total


def by_core(core, mine, other):
    first = core == 0
    return jnp.where(first, mine, other), jnp.where(first, other, mine)


def gelu_and_slope(values):
    cumulative = 0.5 * (1.0 + lax.erf(values * (1.0 / math.sqrt(2.0))))
    density = jnp.exp(-0.5 * values * values) * (1.0 / math.sqrt(2.0 * math.pi))
    return values * cumulative, cumulative + values * density


def turn(values, cosine, sine):
    half = ROT // 2
    first, second = values[:, :half], values[:, half:ROT]
    return jnp.concatenate(
        [first * cosine - second * sine, second * cosine + first * sine, values[:, ROT:]],
        axis=1,
    )


def general_body(
    tokens,
    w_qkv,
    b_qkv,
    w_out,
    b_out,
    w_in,
    b_in,
    w_out2,
    b_out2,
    norm_gain,
    norm_shift,
    doc_start,
    live,
    cotangent,
):
    blocks = lax.axis_size("blk")
    cores = lax.axis_size("tp")
    me, core = lax.axis_index("blk"), lax.axis_index("tp")
    rows, width = tokens.shape
    depth = w_in.shape[0]
    part = rows // cores
    quarter = part // 2
    group = blocks // HEADS
    columns = HEAD // group
    units = w_in.shape[1] // blocks
    cut = depth // cores
    near = columns // cores
    scale = 1.0 / math.sqrt(HEAD)

    masks_x = list(range(1, group))
    masks_y = [group]
    masks_z = [2 * group * i for i in range(1, blocks // (2 * group))]
    size_x, size_y, size_z = group, 2, len(masks_z) + 1

    def gather(value):
        over_z = spread(value, masks_z)
        one = spread(spread(over_z[:, :quarter], masks_y), masks_x)
        two = spread(spread(over_z[:, quarter:], masks_x), masks_y)
        return one.reshape(-1, value.shape[-1]), two.reshape(-1, value.shape[-1])

    def scatter(one, two):
        one = one.reshape(size_x, size_y, size_z, quarter, width)
        two = two.reshape(size_y, size_x, size_z, quarter, width)
        one = collect(collect(one, masks_x).astype(BF), masks_y)
        two = collect(collect(two, masks_y).astype(BF), masks_x)
        return collect(jnp.concatenate([one, two], axis=1).astype(BF), masks_z)

    small = jnp.concatenate(
        [
            norm_gain.reshape(-1),
            norm_shift.reshape(-1),
            b_out.reshape(-1),
            b_out2.reshape(-1),
            b_qkv.reshape(-1),
            b_in.reshape(-1),
            (doc_start // 256).astype(BF),
            (doc_start % 256).astype(BF),
            live.astype(BF),
        ]
    )
    small_rows = -(-small.size // 2048) * 16
    small = jnp.pad(small, (0, small_rows * 128 - small.size)).reshape(small_rows * 128 // columns, columns)
    lines = small.shape[0]

    own_heads = HEADS // cores * group
    triple = w_qkv.reshape(3, cores, cut, own_heads, columns).transpose(1, 3, 0, 2, 4)
    triple = triple.reshape(cores, own_heads, 3 * cut, columns)
    outward = w_out.reshape(own_heads, cores, near, depth).transpose(1, 0, 2, 3)
    outward = outward.reshape(cores, own_heads, near * depth // columns, columns)
    dealt = jnp.concatenate([triple, outward], axis=2)
    keep = lax.dynamic_index_in_dim(dealt, core, 0, keepdims=False)
    give = lax.dynamic_index_in_dim(dealt, 1 - core, 0, keepdims=False)
    got = swap_cores(give)
    heads_low, heads_high = by_core(core, keep, got)
    deal = jnp.concatenate(
        [
            jnp.concatenate([heads_low, heads_high]),
            jnp.broadcast_to(small, (blocks,) + small.shape),
        ],
        axis=1,
    )
    here = lax.all_to_all(deal, "blk", 0, 0, tiled=True)
    there = swap_cores(here)
    both = jnp.stack(by_core(core, here, there))

    expand_deal = w_in.reshape(depth, blocks, units).transpose(1, 0, 2)
    expand_mine = lax.all_to_all(expand_deal, "blk", 0, 0, tiled=True).reshape(width, units)
    expand_other = swap_cores(expand_mine)
    shrink_mine = lax.all_to_all(
        w_out2.reshape(blocks, units, depth), "blk", 0, 0, tiled=True
    )
    shrink_other = swap_cores(shrink_mine)
    w_expand = jnp.concatenate([expand_mine, expand_other], axis=1)
    w_shrink = jnp.concatenate([shrink_mine, shrink_other], axis=1)
    w_shrink = w_shrink.transpose(1, 0, 2).reshape(2 * units, width)

    my_tokens = lax.dynamic_slice_in_dim(tokens, core * part, part, 0)
    my_cotangent = lax.dynamic_slice_in_dim(cotangent, core * part, part, 0)
    all_tokens = jnp.concatenate(gather(my_tokens))
    all_cotangent = jnp.concatenate(gather(my_cotangent))
    count = all_tokens.shape[0]

    at = 3 * cut
    mid = at + near * depth // columns
    w_triple = both[:, :, :at].reshape(cores, blocks, 3, cut, columns)
    w_triple = w_triple.transpose(1, 0, 3, 2, 4).reshape(width, 3 * columns)
    w_near = both[:, :, at:mid].reshape(cores, blocks, near, depth)
    w_near = w_near.transpose(0, 2, 1, 3).reshape(columns, width)
    w_head = spread(w_near, masks_x).reshape(HEAD, width)
    flat = both[:, :, mid:].reshape(cores, blocks, -1)

    def take(offset, like):
        return flat[:, :, offset : offset + like.size].reshape((cores, blocks) + like.shape), offset + like.size

    offset = 0
    gain_all, offset = take(offset, norm_gain)
    shift_all, offset = take(offset, norm_shift)
    out_all, offset = take(offset, b_out)
    out2_all, offset = take(offset, b_out2)
    triple_all, offset = take(offset, b_qkv)
    expand_all, offset = take(offset, b_in)
    start_high, offset = take(offset, doc_start)
    start_low, offset = take(offset, doc_start)
    live_all, offset = take(offset, live)
    gains = gain_all[0].transpose(1, 2, 0, 3).reshape(2, width).astype(F32)
    shifts = shift_all[0].transpose(1, 2, 0, 3).reshape(2, width).astype(F32)
    residual_shift = (out_all[0].astype(F32) + out2_all[0].astype(F32)).transpose(1, 0, 2).reshape(width)
    triple_shift = triple_all.astype(F32).transpose(2, 0, 3, 1, 4).reshape(3, width)
    triple_shift = lax.dynamic_slice_in_dim(triple_shift, me * columns, columns, 1).reshape(-1)
    expand_shift = expand_all.astype(F32).transpose(0, 2, 1, 3).reshape(cores, -1)
    expand_shift = lax.dynamic_slice_in_dim(expand_shift, me * units, units, 1)
    expand_shift = jnp.concatenate(by_core(core, expand_shift[0], expand_shift[1]))
    starts = (start_high[0].astype(F32) * 256.0 + start_low[0].astype(F32)).astype(jnp.int32)
    lives = live_all[0].astype(jnp.int32)

    x_at = jnp.arange(size_x)[:, None, None]
    y_at = group * jnp.arange(size_y)[None, :, None]
    z_at = 2 * group * jnp.arange(size_z)[None, None, :]
    order = (x_at + y_at + z_at) ^ me
    inside = jnp.arange(quarter, dtype=jnp.int32)

    def index_of(which):
        base = order[..., None] * rows + which * part + inside
        one, two = base, base + quarter
        return jnp.concatenate(
            [one.reshape(size_x, -1), two.reshape(size_x, -1)], axis=1
        )

    def heads_order(value):
        tail = value.shape[1:]
        one = value[: count // 2].reshape((size_x, -1) + tail)
        two = value[count // 2 :].reshape((size_y, size_x, -1) + tail)
        two = jnp.swapaxes(two, 0, 1).reshape((size_x, -1) + tail)
        return jnp.concatenate([one, two], axis=1)

    def gathered_order(value):
        tail = value.shape[2:]
        middle = value.shape[1] // 2
        one = value[:, :middle].reshape((count // 2,) + tail)
        two = value[:, middle:].reshape((size_x, size_y, -1) + tail)
        two = jnp.swapaxes(two, 0, 1).reshape((count // 2,) + tail)
        return jnp.concatenate([one, two])

    index_mine, index_other = index_of(core), index_of(1 - core)
    index = jnp.concatenate([index_mine.reshape(-1), index_other.reshape(-1)])
    token_start = starts.reshape(-1)[index]
    token_live = lives.reshape(-1)[index]

    inputs = all_tokens.astype(F32)
    center = inputs - jnp.mean(inputs, axis=-1, keepdims=True)
    inverse = lax.rsqrt(jnp.mean(center * center, axis=-1, keepdims=True) + EPSILON)
    normal = center * inverse
    normed_attend = (normal * gains[0] + shifts[0]).astype(BF)
    normed_feed = (normal * gains[1] + shifts[1]).astype(BF)

    linear = dot(normed_attend, w_triple, ((1,), (0,))) + triple_shift
    linear = heads_order(linear).reshape(count, 3, columns)
    steps = jnp.arange(ROT // 2, dtype=F32)
    speed = 10000.0 ** (-2.0 * steps / ROT)
    place = (index - token_start).astype(F32)
    angle = place[:count, None] * speed[None, :]
    cosine, sine = jnp.cos(angle), jnp.sin(angle)
    slot = me % group

    def turn_pieces(pieces, cosine, sine):
        if columns >= ROT:
            return jnp.stack(
                [
                    turn(
                        pieces[r],
                        jnp.where(slot == r, cosine, 1.0),
                        jnp.where(slot == r, sine, 0.0),
                    )
                    for r in range(group)
                ]
            )
        place_of = jnp.arange(group) ^ slot
        whole = jnp.swapaxes(pieces[place_of], 0, 1).reshape(pieces.shape[1], HEAD)
        whole = turn(whole, cosine, sine).reshape(-1, group, columns)
        return jnp.swapaxes(whole, 0, 1)[place_of]

    if columns >= ROT:
        own_cosine = jnp.where(slot == 0, cosine, 1.0)
        own_sine = jnp.where(slot == 0, sine, 0.0)
        queries = turn(linear[:, 0], own_cosine, own_sine)
        keys = turn(linear[:, 1], own_cosine, own_sine)
    else:
        queries, keys = linear[:, 0], linear[:, 1]
    mine = jnp.concatenate([queries, keys, linear[:, 2]], axis=1).astype(BF)

    def align(value, r):
        slabs = value.reshape((size_x, -1) + value.shape[1:])
        return jnp.stack([slabs[x ^ r] for x in range(size_x)]).reshape(value.shape)

    pieces = [mine] + [align(from_peer(mine, r), r) for r in masks_x]
    pieces = jnp.stack(pieces).reshape(group, count, 3, columns)
    if columns < ROT:
        turned = [turn_pieces(pieces[:, :, s].astype(F32), cosine, sine).astype(BF) for s in (0, 1)]
        pieces = jnp.stack(turned + [pieces[:, :, 2]], axis=2)
    own_triple = pieces.transpose(2, 1, 0, 3).reshape(3, count, HEAD)
    other_triple = swap_cores(own_triple)
    queries, keys, values = jnp.concatenate([own_triple, other_triple], axis=1)

    cotangent_x = heads_order(all_cotangent)
    grad_attended = dot(all_cotangent, w_head, ((1,), (1,))).astype(BF)
    grad_attended = heads_order(grad_attended).reshape(count, HEAD)
    grad_attended = jnp.concatenate([grad_attended, swap_cores(grad_attended)])

    share = count // size_x
    mine_index, mine_start, mine_live = index[:share], token_start[:share], token_live[:share]

    def allowed(query_index, query_start, key_index, key_start, key_live):
        same = query_start == key_start
        causal = key_index <= query_index
        usable = (key_live == 1) | (key_index == query_index)
        return same & causal & usable

    mask = allowed(mine_index[:, None], mine_start[:, None], index[None], token_start[None], token_live[None])
    scores = dot(queries[:share], keys, ((1,), (1,))) * scale
    masked = jnp.where(mask, scores, NEGATIVE)
    top = jnp.max(masked, axis=-1, keepdims=True)
    weight = jnp.where(mask, jnp.exp(masked - top), 0.0)
    total = jnp.sum(weight, axis=-1, keepdims=True)
    prob = weight / total
    attended = dot(prob.astype(BF), values, ((1,), (0,)))
    log_total = top + jnp.log(total)
    delta = jnp.sum(grad_attended[:share].astype(F32) * attended, axis=-1, keepdims=True)
    push = dot(grad_attended[:share], values, ((1,), (1,)))
    slope = (prob * (push - delta)).astype(BF)
    grad_queries = dot(slope, keys, ((1,), (0,))) * scale
    attended = attended.astype(BF)

    marks = jnp.concatenate([log_total, delta], axis=1).T
    marks = spread(marks, masks_x).transpose(1, 0, 2).reshape(2, count)
    marks = jnp.concatenate([marks, swap_cores(marks)], axis=1)
    mask = allowed(index[None], token_start[None], mine_index[:, None], mine_start[:, None], mine_live[:, None])
    scores = dot(keys[:share], queries, ((1,), (1,))) * scale
    prob = jnp.where(mask, jnp.exp(jnp.where(mask, scores, NEGATIVE) - marks[0][None]), 0.0)
    grad_values = dot(prob.astype(BF), grad_attended, ((1,), (0,)))
    push = dot(values[:share], grad_attended, ((1,), (1,)))
    slope = (prob * (push - marks[1][None])).astype(BF)
    grad_keys = dot(slope, queries, ((1,), (0,))) * scale

    expanded = dot(normed_feed, w_expand, ((1,), (0,))) + expand_shift
    activated, bend = gelu_and_slope(expanded)
    activated = activated.astype(BF)
    grad_activated = dot(all_cotangent, w_shrink, ((1,), (1,)))
    grad_expanded = (bend * grad_activated).astype(BF)

    branch = dot(activated, w_shrink, ((1,), (0,)))
    attend_part = dot(attended, w_head, ((1,), (0,)))
    rest = jnp.zeros((size_x - 1,) + attend_part.shape, F32)
    attend_part = gathered_order(jnp.concatenate([attend_part[None], rest]))
    branch = (branch + attend_part).astype(BF)
    branch = scatter(branch[: count // 2], branch[count // 2 :])
    my_inputs = my_tokens.astype(F32)
    my_mixed = (my_inputs + branch.reshape(part, width) + residual_shift).astype(BF)

    def whole_block(value):
        low, high = by_core(core, value, swap_cores(value))
        return jnp.concatenate([low, high])

    mixed = whole_block(my_mixed)

    grad_shrink = dot(activated, all_cotangent, ((0,), (0,)))
    grad_expand = dot(normed_feed, grad_expanded, ((0,), (0,)))
    grad_shrink = grad_shrink[:units] + swap_cores(grad_shrink[units:].astype(BF)).astype(F32)
    grad_expand = grad_expand[:, :units] + swap_cores(grad_expand[:, units:].astype(BF)).astype(F32)
    shrink_deal = grad_shrink.astype(BF).reshape(units, blocks, depth).transpose(1, 0, 2)
    expand_deal = grad_expand.astype(BF).reshape(blocks, depth, units)
    shrink_grad = lax.all_to_all(shrink_deal, "blk", 0, 0, tiled=True)
    shrink_grad = shrink_grad.reshape(-1, depth).astype(F32)
    expand_grad = lax.all_to_all(expand_deal, "blk", 0, 0, tiled=True)
    expand_grad = expand_grad.transpose(1, 0, 2).reshape(depth, -1).astype(F32)

    def by_pieces(value):
        return value.reshape(share, group, columns).transpose(1, 0, 2)

    own_cosine, own_sine = cosine[:share], -sine[:share]
    back = [
        turn_pieces(by_pieces(grad_queries), own_cosine, own_sine),
        turn_pieces(by_pieces(grad_keys), own_cosine, own_sine),
        by_pieces(grad_values),
    ]
    back = jnp.concatenate(back, axis=2).astype(BF)
    back = jnp.concatenate([back, by_pieces(attended)], axis=2)
    back = jnp.stack([back[0]] + [from_peer(back[r], r) for r in masks_x])
    back = gathered_order(back)
    grad_linear, attended_near = back[:, : 3 * columns], back[:, 3 * columns :]
    grad_triple = dot(normed_attend, grad_linear, ((0,), (0,)))
    grad_out = dot(attended_near, all_cotangent, ((0,), (0,)))
    grad_triple = grad_triple.reshape(blocks, cores, cut, 3, columns).transpose(1, 0, 3, 2, 4)
    grad_triple = grad_triple.reshape(cores, blocks, 3 * cut, columns)
    grad_out = grad_out.reshape(cores, near, blocks, depth).transpose(0, 2, 1, 3)
    grad_out = grad_out.reshape(cores, blocks, near * depth // columns, columns)
    dealt = jnp.concatenate([grad_triple, grad_out], axis=2)
    keep = lax.dynamic_index_in_dim(dealt, core, 0, keepdims=False)
    give = lax.dynamic_index_in_dim(dealt, 1 - core, 0, keepdims=False)
    dealt = (keep + swap_cores(give.astype(BF)).astype(F32)).astype(BF)
    dealt = lax.all_to_all(dealt, "blk", 0, 0, tiled=True)
    dealt = dealt.reshape((cores, own_heads) + dealt.shape[1:])
    keep = lax.dynamic_index_in_dim(dealt, core, 0, keepdims=False)
    give = lax.dynamic_index_in_dim(dealt, 1 - core, 0, keepdims=False)
    dealt = jnp.stack(by_core(core, keep, swap_cores(give)))
    triple_grad = dealt[:, :, :at].reshape(cores, own_heads, 3, cut, columns)
    triple_grad = triple_grad.transpose(2, 0, 3, 1, 4).reshape(3, depth, -1).astype(F32)
    output_grad = dealt[:, :, at:].reshape(cores, own_heads, near, depth)
    output_grad = output_grad.transpose(1, 0, 2, 3).reshape(-1, depth).astype(F32)

    grad_attend_norm = dot(grad_linear, w_triple, ((1,), (1,)))
    grad_feed_norm = dot(grad_expanded, w_expand, ((1,), (1,)))
    combined = (gains[0] * grad_attend_norm + gains[1] * grad_feed_norm).astype(BF)
    combined = scatter(combined[: count // 2], combined[count // 2 :]).reshape(part, width)
    my_center = my_inputs - jnp.mean(my_inputs, axis=-1, keepdims=True)
    my_inverse = lax.rsqrt(jnp.mean(my_center * my_center, axis=-1, keepdims=True) + EPSILON)
    my_normal = my_center * my_inverse
    my_grad = my_inverse * (
        combined
        - jnp.mean(combined, axis=-1, keepdims=True)
        - my_normal * jnp.mean(combined * my_normal, axis=-1, keepdims=True)
    )
    tokens_grad = whole_block((my_cotangent.astype(F32) + my_grad).astype(BF))

    sums = [
        jnp.sum(normal * grad_attend_norm, axis=0),
        jnp.sum(normal * grad_feed_norm, axis=0),
        jnp.sum(grad_attend_norm, axis=0),
        jnp.sum(grad_feed_norm, axis=0),
        jnp.sum(all_cotangent.astype(F32), axis=0),
        jnp.sum(grad_expanded.astype(F32), axis=0),
        jnp.sum(grad_linear.astype(F32), axis=0),
    ]
    sums = jnp.concatenate(sums)
    other = swap_cores(sums)
    added = sums + other
    norm_sums = added[: 4 * width].reshape(4, width // 128, blocks, -1).transpose(2, 0, 1, 3)
    residual_sum = added[4 * width : 5 * width].reshape(width // 128, 128)
    lanes = 128 // blocks
    residual_grad = lax.dynamic_slice_in_dim(residual_sum, me * lanes, lanes, 1)
    unit_sum = sums[5 * width : 5 * width + units] + other[5 * width + units : 5 * width + 2 * units]
    unit_sums = lax.dynamic_update_slice_in_dim(
        jnp.zeros((w_in.shape[1],), F32), unit_sum, me * units, 0
    )
    unit_sums = unit_sums.reshape(-1, blocks, lanes).transpose(1, 0, 2)
    line_sum = added[5 * width + 2 * units :].reshape(3, columns)
    line_sums = lax.dynamic_update_slice_in_dim(
        jnp.zeros((3, width), F32), line_sum, me * columns, 1
    )
    line_sums = lax.dynamic_slice_in_dim(line_sums, core * (width // cores), width // cores, 1)
    line_sums = line_sums.reshape(3, -1, blocks, lanes).transpose(2, 0, 1, 3)
    tiny = jnp.concatenate(
        [norm_sums.reshape(blocks, -1), unit_sums.reshape(blocks, -1), line_sums.reshape(blocks, -1)],
        axis=1,
    )
    tiny = jnp.sum(lax.all_to_all(tiny, "blk", 0, 0, tiled=True), axis=0)
    first = norm_gain.size
    gain_grad = tiny[:first].reshape(norm_gain.shape)
    shift_grad = tiny[first : 2 * first].reshape(norm_shift.shape)
    expand_bias_grad = tiny[2 * first : 2 * first + b_in.size].reshape(b_in.shape)
    triple_bias_grad = tiny[2 * first + b_in.size :].reshape(b_qkv.shape)
    return (
        mixed,
        tokens_grad,
        triple_grad,
        triple_bias_grad,
        output_grad,
        residual_grad,
        expand_grad,
        expand_bias_grad,
        shrink_grad,
        residual_grad,
        gain_grad,
        shift_grad,
    )


VMEM = pl.BlockSpec(memory_space=pltpu.VMEM)
SMEM = pl.BlockSpec(memory_space=pltpu.SMEM)
GRANT = 28 * 1024 * 1024
MARK_COS, MARK_SIN = 32, 64
COST = 1.0
WIDE = 256


def run_kernel(kernel, outs, grid=None, ins=None, out_specs=None, scratch=(), flops=0, moved=0, name=None):
    outs = [jax.ShapeDtypeStruct(shape, kind) for shape, kind in outs]
    single = len(outs) == 1
    out_specs = out_specs or [VMEM] * len(outs)
    extra = {} if grid is None else {"grid": grid}
    return pl.pallas_call(
        kernel,
        out_shape=outs[0] if single else outs,
        in_specs=ins,
        out_specs=out_specs[0] if single else out_specs,
        scratch_shapes=list(scratch),
        compiler_params=pltpu.CompilerParams(vmem_limit_bytes=GRANT),
        cost_estimate=pl.CostEstimate(flops=int(flops * COST), bytes_accessed=int(moved * COST), transcendentals=0),
        name=name,
        **extra,
    )


def chunk_bits(half, at, lanes):
    z = at % lanes
    low, high = (at // lanes) % 2, at // (2 * lanes)
    x, y = (high, low) if half == 0 else (low, high)
    return x + 2 * y + 4 * z


class Rows:
    def __init__(self, blocks, cores, rows):
        self.blocks, self.rows = blocks, rows
        self.part = rows // cores
        self.chunk = self.part // 2
        self.half = blocks * self.chunk
        self.count = 2 * self.half
        self.share = self.half
        self.sizes_z = blocks // 4

    def natural(self, me, core, half, at):
        block = me ^ chunk_bits(half, at, self.sizes_z)
        return block * self.rows + core * self.part + half * self.chunk

    def x_rows(self, x):
        h, q = self.half // 2, self.half // 4
        return [
            (x * h, 0, h),
            (self.half + x * q, h, q),
            (self.half + 2 * q + x * q, h + q, q),
        ]

    def pairs(self):
        mine, peer = self.x_rows(0), self.x_rows(1)
        both = [(a[0], b[0], a[2]) for a, b in zip(mine, peer)]
        return both + [(b, a, n) for a, b, n in both]


def nn(left, right):
    return lax.dot_general(left, right, (((1,), (0,)), ((), ())), preferred_element_type=F32)


def nt(left, right):
    return lax.dot_general(left, right, (((1,), (1,)), ((), ())), preferred_element_type=F32)


def lane_of(shape):
    return lax.broadcasted_iota(jnp.int32, shape, len(shape) - 1)


def turn_lanes(values, table, active, sign):
    lane = lane_of(values.shape)
    first, second = lane < ROT // 2, lane < ROT
    cosine = jnp.where(first, pltpu.roll(table, 128 - MARK_COS, 1), table)
    sine_first = pltpu.roll(table, 128 - MARK_SIN, 1)
    sine_second = pltpu.roll(table, 128 - MARK_SIN + ROT // 2, 1)
    sine = jnp.where(first, -sine_first, sine_second) * sign
    cosine = jnp.where(second & active, cosine, 1.0)
    sine = jnp.where(second & active, sine, 0.0)
    partner = jnp.where(first, pltpu.roll(values, 128 - ROT // 2, 1), pltpu.roll(values, ROT // 2, 1))
    return values * cosine + partner * sine


def deal_kernel(cut, blocks, ids, speed, here, there, triple, near, marks, norms, shifts, lines, flip):
    me, core = ids[0], ids[1]
    width = lines.shape[2]
    for source in range(blocks):
        for who, ref in ((core, here), (1 - core, there)):
            at = pl.multiple_of(source * 2 * cut + who * cut, cut)
            for s in range(3):
                triple[pl.ds(at, cut), s * 128 : (s + 1) * 128] = ref[source, s * cut : (s + 1) * cut, :]
            at = pl.multiple_of(who * cut, cut)
            near[pl.ds(at, cut), source * 128 : (source + 1) * 128] = ref[source, 3 * cut : 4 * cut, :]

    lanes = 128 // blocks
    row = lax.broadcasted_iota(jnp.int32, (128, width), 0)
    lane = lane_of((128, width))
    deal = ((row // lanes == lane // 128) & (row % lanes == lane % lanes)).astype(BF)
    lane = lane_of((16, width)) % 128 // lanes
    flip[...] = jnp.zeros_like(flip)
    for which, ref in enumerate((here, there)):
        total = jnp.zeros((16, width), F32)
        for source in range(blocks):
            small = ref[source, 4 * cut : 4 * cut + 16, :]
            total = total + jnp.where(lane == source, nn(small, deal), 0.0)
            if which == 0:
                small = small.astype(F32)
                flip[source : source + 1, :] = small[10:11] * 256.0 + small[11:12]
                flip[blocks + source : blocks + source + 1, :] = small[12:13]
        lines[which] = total
    norms[:4, :] = lines[0, :4, :]
    norms[4:5, :] = lines[0, 4:5, :] + lines[0, 5:6, :]
    norms[5:, :] = jnp.zeros((3, width), F32)
    shifts[...] = jnp.zeros_like(shifts)
    heads = blocks // 2
    ours = me // heads == core
    for s in range(3):
        at = pl.multiple_of((me % heads + s % 2 * heads) * 128, 128)
        both = [lines[k, 6 + s // 2 : 7 + s // 2, pl.ds(at, 128)] for k in (0, 1)]
        shifts[0:1, s * 128 : (s + 1) * 128] = jnp.where(ours, both[0], both[1])
    units = 2 * width // blocks
    at = pl.multiple_of(me % heads * units, units)
    for k in (0, 1):
        shifts[1:2, k * units : (k + 1) * units] = lines[k, pl.ds(8 + me // heads, 1), pl.ds(at, units)]

    turned = flip[...].T
    lane = lane_of((128, 128))
    row = lax.broadcasted_iota(jnp.int32, (128, 128), 0).astype(F32)
    for q in range(blocks // 4):
        place = jnp.zeros((128, 128), F32)
        for g in range(4):
            b = 4 * q + g
            place = jnp.where(lane // 32 == g, row + b * 128.0 - turned[:, b : b + 1], place)
        angle = place * speed[0:1, :]
        cosine, sine = jnp.cos(angle), jnp.sin(angle)
        for g in range(4):
            b = 4 * q + g
            index = row + b * 128.0
            table = jnp.where(lane == 0, index, 0.0)
            table = jnp.where(lane == 1, jnp.where(turned[:, blocks + b : blocks + b + 1] == 1.0, index, -1.0), table)
            table = jnp.where(lane == 2, turned[:, b : b + 1], table)
            table = jnp.where(lane // 32 == 1, pltpu.roll(cosine, (MARK_COS - g * 32) % 128, 1), table)
            table = jnp.where(lane // 32 == 2, pltpu.roll(sine, (MARK_SIN - g * 32) % 128, 1), table)
            marks[b * 128 : (b + 1) * 128, :] = table


def feed_deal_kernel(blocks, units, expand, shrink, out):
    for k in range(blocks):
        out[k, :units, :] = expand[:, k * units : (k + 1) * units].T
        out[k, units:, :] = shrink[k * units : (k + 1) * units, :]


def pick(i, refs, tile):
    for k, ref in enumerate(refs):

        @pl.when(i == k)
        def _(ref=ref):
            tile[...] = ref[...]


def norm_kernel(r, ids, t0, t1, t2, t3, norms, weight, shifts, marks, feed, stats, mine, tile, table, attend):
    i = pl.program_id(0)
    me, core = ids[0], ids[1]
    pick(i, (t0, t1, t2, t3), tile)
    for half in (0, 1):

        @pl.when(i // 2 == half)
        def _(half=half):
            for q in range(8):
                at = r.natural(me, core, half, (i % 2) * 8 + q)
                table[q * r.chunk : (q + 1) * r.chunk, :] = marks[pl.ds(pl.multiple_of(at, r.chunk), r.chunk), :]

    step = 16
    lane = lane_of((step, 128))

    @pl.loop(0, tile.shape[0] // step, unroll=4)
    def _(j):
        rows = pl.ds(pl.multiple_of(j * step, step), step)
        values = tile[rows, :].astype(F32)
        mean = jnp.mean(values, axis=-1, keepdims=True)
        center = values - mean
        inverse = lax.rsqrt(jnp.mean(center * center, axis=-1, keepdims=True) + EPSILON)
        value = center * inverse
        attend[rows, :] = (value * norms[0:1, :] + norms[2:3, :]).astype(BF)
        feed[rows, :] = (value * norms[1:2, :] + norms[3:4, :]).astype(BF)
        stats[rows, :] = jnp.where(lane == 0, mean, inverse)

    linear = nn(attend[...], weight[...]) + shifts[0:1, :384]
    active = me % 2 == 0
    for s in (0, 1):
        cols = slice(s * 128, (s + 1) * 128)
        mine[:, cols] = turn_lanes(linear[:, cols], table[...], active, 1.0).astype(BF)
    mine[:, 256:] = linear[:, 256:].astype(BF)


def normal_of(tile, stats):
    return (tile.astype(F32) - stats[:, 0:1]) * stats[:, 1:2]


def gather_columns(r, out, low, high, column):
    cols = slice(column * 128, (column + 1) * 128)
    out[:, :128] = low[:, cols]
    for here, there, size in r.pairs():
        out[here : here + size, 128:] = high[there : there + size, cols]


def gather_marks(r, ids, marks, table, line):
    me, core = ids[0], ids[1]
    for w in (0, 1):
        who = core if w == 0 else 1 - core
        for half in (0, 1):
            for q in range(16):
                at = r.natural(me, who, half, q)
                to = w * r.count + half * r.half + q * r.chunk
                table[to : to + r.chunk, :] = marks[pl.ds(pl.multiple_of(at, r.chunk), r.chunk), :]
    for b in range(2 * r.count // 128):
        line[:, b * 128 : (b + 1) * 128] = table[b * 128 : (b + 1) * 128, :].T[:8, :]


def own_rows(r, out, ref, columns=slice(None)):
    for row, place, size in r.x_rows(0):
        out[place : place + size, :] = ref[row : row + size, columns]


def query_kernel(r, scale, ids, a00, a01, a10, a11, grads, marks, attended, keep, send, lines,
                 keys, values, queries, pushes, table, line, mine):
    i = pl.program_id(0)
    me = ids[0]
    count, tile = r.count, r.share // 2

    @pl.when(i == 0)
    def _():
        gather_columns(r, keys.at[:count], a00, a01, 1)
        gather_columns(r, keys.at[count:], a10, a11, 1)
        gather_columns(r, values.at[:count], a00, a01, 2)
        gather_columns(r, values.at[count:], a10, a11, 2)
        for row, place, size in r.x_rows(0):
            queries[place : place + size, :128] = a00[row : row + size, :128]
        for (row, place, size), (there, _, _) in zip(r.x_rows(0), r.x_rows(1)):
            queries[place : place + size, 128:] = a01[there : there + size, :128]
        own_rows(r, pushes, grads)
        gather_marks(r, ids, marks, table, line)
        own_rows(r, mine, table.at[:count])

    rows = pl.ds(pl.multiple_of(i * tile, tile), tile)
    mark = mine[rows, :]
    q_at, q_start = mark[:, 0:1], mark[:, 2:3]
    k_at, k_live = line[0:1, :], line[1:2, :]
    mask = ((k_live >= q_start) & (k_at <= q_at)) | (k_at == q_at)
    scores = jnp.where(mask, nt(queries[rows, :], keys[...]) * scale, NEGATIVE)
    top = jnp.max(scores, axis=-1, keepdims=True)
    weight = jnp.where(mask, jnp.exp(scores - top), 0.0)
    total = jnp.sum(weight, axis=-1, keepdims=True)
    prob = weight * (1.0 / total)
    result = nn(prob.astype(BF), values[...])
    grad = pushes[rows, :]
    delta = jnp.sum(grad.astype(F32) * result, axis=-1, keepdims=True)
    slope = (prob * (nt(grad, values[...]) - delta)).astype(BF)
    back = nn(slope, keys[...]) * scale
    result = result.astype(BF)
    attended[...] = result
    for k, ref in enumerate((keep, send)):
        cols = slice(k * 128, (k + 1) * 128)
        ref[:, :128] = turn_lanes(back[:, cols], mark, me % 2 == k, -1.0).astype(BF)
        ref[:, 128:] = result[:, cols]
    lane = lane_of((tile, 128))
    both = jnp.where(lane == 0, top + jnp.log(total), jnp.where(lane == 1, delta, 0.0))
    for b in range(tile // 128):
        lines[:, b * 128 : (b + 1) * 128] = both[b * 128 : (b + 1) * 128, :].T[:8, :]


def key_kernel(r, scale, ids, a00, a01, a10, a11, grads, other_grads, l00, l01, l10, l11, marks, keep, send,
               queries, pushes, keys, values, table, line, mine, tops):
    i = pl.program_id(0)
    me = ids[0]
    count, tile = r.count, r.share // 2

    @pl.when(i == 0)
    def _():
        gather_columns(r, queries.at[:count], a00, a01, 0)
        gather_columns(r, queries.at[count:], a10, a11, 0)
        pushes[:count, :] = grads[...]
        pushes[count:, :] = other_grads[...]
        for k, out in ((1, keys), (2, values)):
            cols = slice(k * 128, (k + 1) * 128)
            for row, place, size in r.x_rows(0):
                out[place : place + size, :128] = a00[row : row + size, cols]
            for (row, place, size), (there, _, _) in zip(r.x_rows(0), r.x_rows(1)):
                out[place : place + size, 128:] = a01[there : there + size, cols]
        gather_marks(r, ids, marks, table, line)
        own_rows(r, mine, table.at[:count])
        for base, low, high in ((0, l00, l01), (count, l10, l11)):
            for x, ref in ((0, low), (1, high)):
                for row, place, size in r.x_rows(x):
                    tops[:, base + row : base + row + size] = ref[:, place : place + size]

    rows = pl.ds(pl.multiple_of(i * tile, tile), tile)
    mark = mine[rows, :]
    k_at, k_live = mark[:, 0:1], mark[:, 1:2]
    q_at, q_start = line[0:1, :], line[2:3, :]
    mask = ((k_live >= q_start) & (k_at <= q_at)) | (k_at == q_at)
    scores = nt(keys[rows, :], queries[...]) * scale
    prob = jnp.where(mask, jnp.exp(scores - tops[0:1, :]), 0.0)
    grad_values = nn(prob.astype(BF), pushes[...])
    slope = (prob * (nt(values[rows, :], pushes[...]) - tops[1:2, :])).astype(BF)
    back = nn(slope, queries[...]) * scale
    for k, ref in enumerate((keep, send)):
        cols = slice(k * 128, (k + 1) * 128)
        ref[:, :128] = turn_lanes(back[:, cols], mark, me % 2 == k, -1.0).astype(BF)
        ref[:, 128:] = grad_values[:, cols].astype(BF)


def feed_kernel(units, blocks, normed, c0, c1, c2, c3, mine, other, shifts, near, peer,
                act, grad, act_turned, grad_turned, expand, shrink, sums, pushes, push_sums, tile, turned):
    i = pl.program_id(0)

    @pl.when(i == 0)
    def _():
        sums[...] = jnp.zeros_like(sums)
        push_sums[...] = jnp.zeros_like(push_sums)
        turned[:, :128] = near[...].T
        turned[:, 128:] = peer[...].T
        for source in range(blocks):
            cols = slice(source * 128, (source + 1) * 128)
            for at, ref in ((0, mine), (units, other)):
                expand[at : at + units, cols] = ref[source, :units, :]
                shrink[at : at + units, cols] = ref[source, units:, :]

    pick(i, (c0, c1, c2, c3), tile)
    pushes[...] = nn(tile[...], turned[...]).astype(BF)
    expanded = nt(normed[...], expand[...]) + shifts[1:2, : 2 * units]
    activated, bend = gelu_and_slope(expanded)
    activated = activated.astype(BF)
    act[...] = activated
    act_turned[...] = activated.T
    slope = (bend * nt(tile[...], shrink[...])).astype(BF)
    grad[...] = slope
    grad_turned[...] = slope.T
    sums[0:1, :] += jnp.sum(slope.astype(F32), axis=0, keepdims=True)
    push_sums[0:1, :] += jnp.sum(tile[...].astype(F32), axis=0, keepdims=True)


def by_quarter(left, quarters):
    size = quarters[0].shape[0]
    total = nn(left[:, :size], quarters[0][...])
    for k in range(1, len(quarters)):
        total = total + nn(left[:, k * size : (k + 1) * size], quarters[k][...])
    return total


def outer_kernel(units, grad_turned, act_turned, normed, c0, c1, c2, c3, *rest):
    out = rest[-1]
    for k in (0, 1):
        result = by_quarter(act_turned, (c0, c1, c2, c3)) if k else nn(grad_turned[...], normed[...])
        for b in range(WIDE // 128):
            lanes = slice(b * 128, (b + 1) * 128)
            rows = slice(k * units, (k + 1) * units)
            part = result[:, lanes]
            if len(rest) > 1:
                part = part + rest[0][b, rows, :].astype(F32)
            out[b, rows, :] = part.astype(BF)


def branch_kernel(r, act, attended, shrink, near, peer, o0, o1, o2, o3):
    outs = (o0, o1, o2, o3)
    size = r.count // 4
    extra = nn(attended[:, :128], near[...]) + nn(attended[:, 128:], peer[...])
    for k in range(4):
        result = nn(act[k * size : (k + 1) * size, :], shrink[...])
        covered = False
        for row, place, length in r.x_rows(0):
            if row == k * size:
                outs[k][:length, :] = (result[:length] + extra[place : place + length]).astype(BF)
                if length < size:
                    outs[k][length:, :] = result[length:].astype(BF)
                covered = True
        if not covered:
            outs[k][...] = result.astype(BF)


def inputs_kernel(r, keep1, keep2, got1, got2, grad, t0, t1, t2, t3, stats, triple, expand, gains, cotangent_sums, unit_sums,
                  o0, o1, o2, o3, linear, near, sums, line_sums):
    j = pl.program_id(0)
    size = r.count // 4

    @pl.when(j == 0)
    def _():
        for x, one, two in ((0, keep1, keep2), (1, got1, got2)):
            for row, place, length in r.x_rows(x):
                linear[row : row + length, :128] = one[place : place + length, :128]
                linear[row : row + length, 128:] = two[place : place + length, :]
                near[row : row + length, :] = one[place : place + length, 128:]
        line_sums[...] = jnp.zeros_like(line_sums)
        line_sums[0:1, :384] = jnp.sum(linear[...].astype(F32), axis=0, keepdims=True)

    sums[...] = jnp.zeros_like(sums)
    for k, (ref, tokens) in enumerate(((o0, t0), (o1, t1), (o2, t2), (o3, t3))):
        rows = slice(k * size, (k + 1) * size)
        attend = nt(linear[rows, :], triple[...])
        feed = nn(grad[rows, :], expand[...])
        value = normal_of(tokens[...], stats[rows, :])
        sums[0:1, :] += jnp.sum(value * attend, axis=0, keepdims=True)
        sums[1:2, :] += jnp.sum(value * feed, axis=0, keepdims=True)
        sums[2:3, :] += jnp.sum(attend, axis=0, keepdims=True)
        sums[3:4, :] += jnp.sum(feed, axis=0, keepdims=True)
        ref[...] = (gains[0:1, :] * attend + gains[1:2, :] * feed).astype(BF)
    sums[4:5, :] = cotangent_sums[0:1, :]
    for k in (0, 1):

        @pl.when(j == k)
        def _(k=k):
            sums[5:6, :] = line_sums[0:1, k * WIDE : (k + 1) * WIDE]
            sums[6:7, :] = unit_sums[0:1, k * WIDE : (k + 1) * WIDE]


def small_kernel(blocks, units, ids, mine, other, out, lines):
    me, core = ids[0], ids[1]
    width = lines.shape[1]
    heads, lanes = blocks // 2, 128 // blocks
    lines[...] = jnp.zeros_like(lines)
    lines[0:5, :] = mine[0:5, :] + other[0:5, :]
    ours = jnp.where(me // heads == core, 1.0, 0.0)
    for s in range(3):
        at = pl.multiple_of((me % heads + s % 2 * heads) * 128, 128)
        cols = slice(s * 128, (s + 1) * 128)
        lines[6 + s // 2 : 7 + s // 2, pl.ds(at, 128)] = (mine[5:6, cols] + other[5:6, cols]) * ours
    at = pl.multiple_of(me % heads * units, units)
    total = mine[6:7, :units] + other[6:7, units : 2 * units]
    for k in (0, 1):

        @pl.when(me // heads == k)
        def _(k=k):
            lines[8 + k : 9 + k, pl.ds(at, units)] = total

    row = lax.broadcasted_iota(jnp.int32, (width, 128), 0)
    lane = lane_of((width, 128))
    deal = ((lane // lanes == row // 128) & (lane % lanes == row % lanes)).astype(BF)
    value = lines[...]
    high = value.astype(BF)
    low = (value - high.astype(F32)).astype(BF)
    lane = lane_of((16, width)) % 128 // lanes
    line = lax.broadcasted_iota(jnp.int32, (16, width), 0)
    for b in range(blocks):
        sent = (lane == b) & ((line != 4) | (me == b))
        for k, part in enumerate((high, low)):
            part = jnp.where(sent, part.astype(F32), 0.0).astype(BF)
            out[b, k * 16 : (k + 1) * 16, :] = nn(part, deal).astype(BF)


def fold_kernel(keep1, got1, keep2, got2, one, one_send, two, two_send):
    for keep, got, outs in ((keep1, got1, (one, one_send)), (keep2, got2, (two, two_send))):
        half = outs[0].shape[0]
        for k, out in enumerate(outs):
            rows = slice(k * half, (k + 1) * half)
            out[...] = (keep[rows, :].astype(F32) + got[rows, :].astype(F32)).astype(BF)


def by_z_kernel(chunk, one, one_got, two, two_got, *outs):
    for half, (mine, got) in enumerate(((one, one_got), (two, two_got))):
        for z, out in enumerate(outs):
            rows = slice(z * chunk, (z + 1) * chunk)
            value = mine[rows, :].astype(F32) + got[rows, :].astype(F32)
            out[half * chunk : (half + 1) * chunk, :] = value.astype(BF)


def line_outer_kernel(cut, ids, linear, near, t0, t1, t2, t3, stats, norms, c0, c1, c2, c3,
                      keep, give, turned, near_turned, normed, result):
    core = ids[1]

    @pl.when(pl.program_id(0) == 0)
    def _():
        turned[...] = linear[...].T
        near_turned[...] = near[...].T

    size = t0.shape[0]
    for k, tokens in enumerate((t0, t1, t2, t3)):
        rows = slice(k * size, (k + 1) * size)
        value = normal_of(tokens[...], stats[rows, :])
        normed[rows, :] = (value * norms[0:1, :] + norms[2:3, :]).astype(BF)
    result[:384, :] = nn(turned[...], normed[...])
    result[384:, :] = by_quarter(near_turned, (c0, c1, c2, c3))
    for who, out in ((core, keep), (1 - core, give)):
        for s in range(4):
            at = pl.multiple_of(s * 2 * cut + who * cut, cut)
            for b in range(WIDE // 128):
                part = result[pl.ds(at, cut), b * 128 : (b + 1) * 128]
                out[b, s * cut : (s + 1) * cut, :] = part.astype(out.dtype)


def unpack_kernel(cut, heads, ids, mine, other, whole, triple, outward, small, pair):
    core = ids[1]
    for k in range(heads):
        for s in range(4):
            for who, ref in ((core, mine), (1 - core, other)):
                pair[pl.ds(pl.multiple_of(who * cut, cut), cut), :] = ref[k, s * cut : (s + 1) * cut, :].astype(F32)
            if s < 3:
                triple[s, :, k * 128 : (k + 1) * 128] = pair[...].T
            else:
                outward[k * 128 : (k + 1) * 128, :] = pair[...]
    total = jnp.zeros(small.shape, F32)
    for b in range(2 * heads):
        for k in (0, 1):
            at = 4 * cut + 16 * k
            total = total + whole[b, at : at + 16, :].astype(F32)
    small[...] = total


def feed_unpack_kernel(units, got, expand, shrink):
    k = pl.program_id(0)
    expand[...] = got[0, :units, :].astype(F32).T
    shrink[...] = got[0, units:, :].astype(F32)


def join(*values):
    return lax.optimization_barrier(values)


def body(
    tokens,
    w_qkv,
    b_qkv,
    w_out,
    b_out,
    w_in,
    b_in,
    w_out2,
    b_out2,
    norm_gain,
    norm_shift,
    doc_start,
    live,
    cotangent,
):
    blocks = lax.axis_size("blk")
    cores = lax.axis_size("tp")
    me, core = lax.axis_index("blk"), lax.axis_index("tp")
    ids = jnp.stack([me, core]).astype(jnp.int32)
    rows, width = tokens.shape
    depth = w_in.shape[0]
    r = Rows(blocks, cores, rows)
    part, count, share = r.part, r.count, r.share
    quarter = count // 4
    units = w_in.shape[1] // blocks
    cut = depth // cores
    own_heads = HEADS // cores * 2
    scale = 1.0 / math.sqrt(HEAD)
    masks_z = [4 * i for i in range(1, blocks // 4)]
    grid = (width // WIDE,)

    once = pl.Buffered(1)

    def tiled(columns):
        return pl.BlockSpec((quarter, columns), lambda i: (i, 0))

    def across(lines):
        return pl.BlockSpec((lines, WIDE), lambda j: (0, j))

    def fixed(value):
        return pl.BlockSpec(value.shape, lambda i: (0,) * value.ndim, pipeline_mode=once)

    def fixed_shape(*shape):
        return pl.BlockSpec(shape, lambda i: (0,) * len(shape))

    def packed_rows(value, lines):
        flat = value.reshape(-1)
        return jnp.pad(flat, (0, lines * 128 - flat.size)).reshape(lines, 128)

    small = jnp.concatenate(
        [
            packed_rows(norm_gain, 2),
            packed_rows(norm_shift, 2),
            packed_rows(b_out, 1),
            packed_rows(b_out2, 1),
            packed_rows(b_qkv, 2),
            packed_rows(b_in, 2),
            jnp.stack([doc_start // 256, doc_start % 256, live]).astype(BF),
            jnp.zeros((3, 128), BF),
        ]
    )

    def over_z(value):
        return [from_peer(value, mask) for mask in masks_z]

    def halves(pieces):
        one = jnp.concatenate([value[: r.chunk] for value in pieces])
        two = jnp.concatenate([value[r.chunk :] for value in pieces])
        return one, two

    my_tokens = lax.dynamic_slice_in_dim(tokens, core * part, part, 0)
    my_cotangent = lax.dynamic_slice_in_dim(cotangent, core * part, part, 0)
    triple = w_qkv.reshape(3, cores, cut, own_heads, 128).transpose(1, 3, 0, 2, 4)
    triple = triple.reshape(cores, own_heads, 3 * cut, 128)
    outward = w_out.reshape(own_heads, cores, cut, 128).transpose(1, 0, 2, 3)
    dealt = jnp.concatenate([triple, outward], axis=2)
    keep = lax.dynamic_index_in_dim(dealt, core, 0, keepdims=False)
    give = lax.dynamic_index_in_dim(dealt, 1 - core, 0, keepdims=False)
    feed_deal = run_kernel(
        lambda *refs: feed_deal_kernel(blocks, units, *refs),
        [((blocks, 2 * units, depth), BF)],
        ins=[VMEM, VMEM],
        name="feed_deal",
        moved=4e6,
    )(w_in, w_out2)
    tokens_z = join(my_tokens, *over_z(my_tokens))
    keep, got, feed_deal, my_cotangent, *tokens_z = join(keep, swap_cores(give), feed_deal, my_cotangent, *tokens_z)

    heads_low, heads_high = by_core(core, keep, got)
    deal = jnp.concatenate(
        [
            jnp.concatenate([heads_low, heads_high]),
            jnp.broadcast_to(small, (blocks,) + small.shape),
        ],
        axis=1,
    )
    here = lax.all_to_all(deal, "blk", 0, 0, tiled=True)
    one, two = halves(tokens_z)
    cotangent_z = over_z(my_cotangent)
    one, one_y, two, two_x = join(one, from_peer(one, 2), two, from_peer(two, 1))

    one, two = jnp.concatenate([one, one_y]), jnp.concatenate([two, two_x])
    mine_one, mine_two = halves(join(my_cotangent, *cotangent_z))
    here, feed_deal, one, one_x, two, two_y, mine_one, mine_y, mine_two, mine_x = join(
        here,
        feed_deal,
        one,
        from_peer(one, 1),
        two,
        from_peer(two, 2),
        mine_one,
        from_peer(mine_one, 2),
        mine_two,
        from_peer(mine_two, 1),
    )
    all_tokens = [one, one_x, two, two_y]

    one, two = jnp.concatenate([mine_one, mine_y]), jnp.concatenate([mine_two, mine_x])
    here, there, feed_deal = join(here, swap_cores(here), feed_deal)
    feed_mine = lax.all_to_all(feed_deal, "blk", 0, 0, tiled=True)
    steps = jnp.arange(ROT // 2, dtype=F32)
    speed = jnp.tile(10000.0 ** (-2.0 * steps / ROT), 4).reshape(1, 128)
    w_triple, w_near, marks, norms, shifts = run_kernel(
        lambda *refs: deal_kernel(cut, blocks, *refs),
        [
            ((width, 384), BF),
            ((128, width), BF),
            ((blocks * rows, 128), F32),
            ((8, width), F32),
            ((8, 512), F32),
        ],
        ins=[SMEM, VMEM, VMEM, VMEM],
        scratch=[pltpu.VMEM((2, 16, width), F32), pltpu.VMEM((128, 128), F32)],
        name="deal",
        moved=8e6,
    )(ids, speed, here, there)
    normed_feed, stats, mine = run_kernel(
        lambda *refs: norm_kernel(r, *refs),
        [((count, width), BF), ((count, 128), F32), ((count, 384), BF)],
        grid=(4,),
        ins=[SMEM] + [fixed(t) for t in all_tokens] + [fixed(norms), fixed(w_triple), fixed(shifts), fixed(marks)],
        out_specs=[tiled(width), tiled(128), tiled(384)],
        scratch=[pltpu.VMEM((quarter, width), BF), pltpu.VMEM((quarter, 128), F32), pltpu.VMEM((quarter, width), BF)],
        flops=2 * count * width * 384,
        name="norm",
        moved=22e6,
    )(ids, *all_tokens, norms, w_triple, shifts, marks)
    w_peer = from_peer(w_near, 1)
    mine, one, one_x, two, two_y = join(mine, one, from_peer(one, 1), two, from_peer(two, 2))

    peer, mine_there = from_peer(mine, 1), swap_cores(mine)
    all_cotangent = [one, one_x, two, two_y]
    feed_mine, *all_cotangent = join(feed_mine, *all_cotangent)

    feed_mine, feed_other = join(feed_mine, swap_cores(feed_mine))

    turned = pl.BlockSpec((2 * units, quarter), lambda i: (0, i))
    act, grad, act_turned, grad_turned, w_expand, w_shrink, unit_sums, grads, cotangent_sums = run_kernel(
        lambda *refs: feed_kernel(units, blocks, *refs),
        [((count, 2 * units), BF)] * 2
        + [((2 * units, count), BF)] * 2
        + [((2 * units, width), BF)] * 2
        + [((8, 2 * units), F32), ((count, 256), BF), ((8, width), F32)],
        grid=(4,),
        ins=[tiled(width)]
        + [fixed(t) for t in all_cotangent]
        + [fixed(feed_mine), fixed(feed_mine), fixed(shifts), fixed(w_near), fixed(w_peer)],
        out_specs=[tiled(2 * units)] * 2
        + [turned] * 2
        + [fixed_shape(2 * units, width)] * 2
        + [fixed_shape(8, 2 * units), tiled(256), fixed_shape(8, width)],
        scratch=[pltpu.VMEM((quarter, width), BF), pltpu.VMEM((width, 256), BF)],
        flops=8 * count * width * units,
        name="feed",
        moved=20e6,
    )(normed_feed, *all_cotangent, feed_mine, feed_other, shifts, w_near, w_peer)
    mine, peer, mine_there, act_turned, grad_turned = join(mine, peer, mine_there, act_turned, grad_turned)

    dealt_spec = pl.BlockSpec((WIDE // 128, 2 * units, 128), lambda j: (j, 0, 0))

    def outer(half, *extra):
        some = pl.BlockSpec((units, count), lambda j: (half, 0))
        return run_kernel(
            lambda *refs: outer_kernel(units, *refs),
            [((blocks, 2 * units, 128), BF)],
            grid=grid,
            ins=[some, some, across(count)] + [across(quarter)] * 4 + [dealt_spec] * len(extra),
            out_specs=[dealt_spec],
            flops=4 * count * width * units,
            name="outer",
            moved=12e6,
        )(grad_turned, act_turned, normed_feed, *all_cotangent, *extra)

    peer_there, feed_sent, grads = join(swap_cores(peer), outer(1), grads)

    tile = share // 2
    half_tile = lambda columns: pl.BlockSpec((tile, columns), lambda i: (i, 0))
    line_tile = pl.BlockSpec((8, tile), lambda i: (0, i))
    four = [mine, peer, mine_there, peer_there]
    common = [
        pltpu.VMEM((2 * count, 256), BF),
        pltpu.VMEM((2 * count, 256), BF),
        pltpu.VMEM((share, 256), BF),
        pltpu.VMEM((share, 256), BF),
        pltpu.VMEM((2 * count, 128), F32),
        pltpu.VMEM((8, 2 * count), F32),
        pltpu.VMEM((share, 128), F32),
    ]
    attended, keep1, send1, lines = run_kernel(
        lambda *refs: query_kernel(r, scale, *refs),
        [((share, 256), BF)] * 3 + [((8, share), F32)],
        grid=(2,),
        ins=[SMEM] + [fixed(mine)] * 4 + [fixed(grads), fixed(marks)],
        out_specs=[half_tile(256)] * 3 + [line_tile],
        scratch=common,
        flops=8 * share * 2 * count * 256,
        name="query",
        moved=6e6,
    )(ids, *four, grads, marks)
    feed_got, grads_there, attended, send1, lines = join(
        swap_cores(feed_sent), swap_cores(grads), attended, send1, lines
    )

    diagonal = [(2 * b + c, 2 * (b ^ 1) + 1 - c) for b in range(blocks) for c in (0, 1)]
    lines_peer, lines_there = from_peer(lines, 1), swap_cores(lines)
    lines_far = lax.ppermute(lines, ("blk", "tp"), diagonal)
    feed_grads = outer(0, feed_got)
    feed_grads, lines, lines_peer, lines_there, lines_far = join(feed_grads, lines, lines_peer, lines_there, lines_far)

    keep2, send2 = run_kernel(
        lambda *refs: key_kernel(r, scale, *refs),
        [((share, 256), BF)] * 2,
        grid=(2,),
        ins=[SMEM] + [fixed(mine)] * 4 + [fixed(grads)] * 2 + [fixed(lines)] * 4 + [fixed(marks)],
        out_specs=[half_tile(256)] * 2,
        scratch=common + [pltpu.VMEM((8, 2 * count), F32)],
        flops=8 * share * 2 * count * 256,
        name="key",
        moved=6e6,
    )(ids, *four, grads, grads_there, lines, lines_peer, lines_there, lines_far, marks)
    feed_grads, attended = join(feed_grads, attended)
    feed_dealt = lax.all_to_all(feed_grads, "blk", 0, 0, tiled=True)
    branches = run_kernel(
        lambda *refs: branch_kernel(r, *refs),
        [((quarter, width), BF)] * 4,
        grid=grid,
        ins=[fixed(act), fixed(attended), across(2 * units), across(128), across(128)],
        out_specs=[across(quarter)] * 4,
        flops=2 * count * width * (2 * units + 128),
        name="branch",
        moved=9e6,
    )(act, attended, w_shrink, w_near, w_peer)
    got1, got2, *branches = join(from_peer(send1, 1), from_peer(send2, 1), *branches)
    mixed_one, mixed_two = from_peer(branches[1], 1), from_peer(branches[3], 2)

    def fold(*refs):
        return run_kernel(
            fold_kernel,
            [((quarter // 2, width), BF)] * 4,
            grid=grid,
            ins=[across(quarter)] * 4,
            out_specs=[across(quarter // 2)] * 4,
            name="fold",
            moved=6e6,
        )(*refs)

    def by_z(*refs):
        return run_kernel(
            lambda *refs: by_z_kernel(r.chunk, *refs),
            [((part, width), BF)] * (1 + len(masks_z)),
            grid=grid,
            ins=[across(quarter // 2)] * 4,
            out_specs=[across(part)] * (1 + len(masks_z)),
            name="by_z",
            moved=3e6,
        )(*refs)

    def total(pieces, got):
        value = pieces[0].astype(F32)
        for piece in got:
            value = value + piece.astype(F32)
        return value

    def pieces_over_z(pieces):
        return [from_peer(piece, mask) for piece, mask in zip(pieces[1:], masks_z)]

    *combined, grad_linear, attended_near, sums, _ = run_kernel(
        lambda *refs: inputs_kernel(r, *refs),
        [((quarter, width), BF)] * 4 + [((count, 384), BF), ((count, 128), BF), ((8, width), F32), ((8, 512), F32)],
        grid=grid,
        ins=[fixed(keep1)] * 4
        + [fixed(grad)]
        + [across(quarter)] * 4
        + [fixed(stats), pl.BlockSpec((WIDE, 384), lambda j: (j, 0)), across(2 * units)]
        + [across(8), across(8), fixed(unit_sums)],
        out_specs=[across(quarter)] * 4
        + [fixed_shape(count, 384), fixed_shape(count, 128), across(8), fixed_shape(8, 512)],
        flops=2 * count * width * (384 + 2 * units),
        name="inputs",
        moved=16e6,
    )(keep1, keep2, got1, got2, grad, *all_tokens, stats, w_triple, w_expand, norms, cotangent_sums, unit_sums)
    grad_linear, sums, *combined = join(grad_linear, sums, *combined)

    got_one, got_two = from_peer(combined[1], 1), from_peer(combined[3], 2)
    line_spec = pl.BlockSpec((WIDE // 128, 4 * cut, 128), lambda j: (j, 0, 0))
    keep, give = run_kernel(
        lambda *refs: line_outer_kernel(cut, *refs),
        [((blocks, 4 * cut, 128), F32), ((blocks, 4 * cut, 128), BF)],
        grid=grid,
        ins=[SMEM, fixed(grad_linear), fixed(attended_near)]
        + [across(quarter)] * 4
        + [fixed(stats), across(8)]
        + [across(quarter)] * 4,
        out_specs=[line_spec] * 2,
        scratch=[
            pltpu.VMEM((384, count), BF),
            pltpu.VMEM((128, count), BF),
            pltpu.VMEM((count, WIDE), BF),
            pltpu.VMEM((512, WIDE), F32),
        ],
        flops=2 * count * width * 512,
        name="line_outer",
        moved=12e6,
    )(ids, grad_linear, attended_near, *all_tokens, stats, norms, *all_cotangent)
    mixed_one, mixed_two, keep, give, sums, sums_other = join(
        mixed_one, mixed_two, keep, give, sums, swap_cores(sums)
    )

    one, one_send, two, two_send = fold(branches[0], mixed_one, branches[2], mixed_two)
    small = run_kernel(
        lambda *refs: small_kernel(blocks, units, *refs),
        [((blocks, 32, 128), BF)],
        ins=[SMEM, VMEM, VMEM],
        scratch=[pltpu.VMEM((16, width), F32)],
        name="small",
        moved=1e6,
    )(ids, sums, sums_other)
    got, small, one, one_send, two, two_send = join(swap_cores(give), small, one, one_send, two, two_send)
    mixed_one, mixed_two = from_peer(one_send, 2), from_peer(two_send, 1)
    dealt = jnp.concatenate([(keep + got.astype(F32)).astype(BF), small], axis=1)
    dealt, feed_dealt = join(dealt, feed_dealt)
    dealt = lax.all_to_all(dealt, "blk", 0, 0, tiled=True)
    expand_grad, shrink_grad = run_kernel(
        lambda *refs: feed_unpack_kernel(units, *refs),
        [(w_in.shape, F32), (w_out2.shape, F32)],
        grid=(blocks,),
        ins=[pl.BlockSpec((1, 2 * units, 128), lambda k: (k, 0, 0))],
        out_specs=[pl.BlockSpec((depth, units), lambda k: (0, k)), pl.BlockSpec((units, depth), lambda k: (k, 0))],
        name="feed_unpack",
        moved=6e6,
    )(feed_dealt)
    got_one, got_two, mixed_one, mixed_two, expand_grad, shrink_grad = join(
        got_one, got_two, mixed_one, mixed_two, expand_grad, shrink_grad
    )
    mixed_pieces = by_z(one, mixed_one, two, mixed_two)
    one, one_send, two, two_send, *mixed_pieces = join(
        *fold(combined[0], got_one, combined[2], got_two), *mixed_pieces
    )
    got_one, got_two, *mixed_got = join(
        from_peer(one_send, 2), from_peer(two_send, 1), *pieces_over_z(mixed_pieces)
    )

    joined = join(*by_z(one, got_one, two, got_two), *mixed_got)
    pieces, mixed_got = joined[: 1 + len(masks_z)], joined[1 + len(masks_z) :]
    combined_got = pieces_over_z(pieces)

    def whole_block(value):
        return jnp.concatenate(by_core(core, value, swap_cores(value)))

    my_inputs = my_tokens.astype(F32)
    mixed = whole_block((my_inputs + total(mixed_pieces, mixed_got) + norms[4:5, :]).astype(BF))
    dealt, mixed = join(dealt, mixed)
    keep = lax.dynamic_slice_in_dim(dealt, core * own_heads, own_heads, 0)
    give = lax.dynamic_slice_in_dim(dealt, (1 - core) * own_heads, own_heads, 0)
    triple_grad, output_grad, small = run_kernel(
        lambda *refs: unpack_kernel(cut, own_heads, *refs),
        [((3, depth, own_heads * 128), F32), ((own_heads * 128, depth), F32), ((16, 128), F32)],
        ins=[SMEM, VMEM, VMEM, VMEM],
        scratch=[pltpu.VMEM((128, 128), F32)],
        name="unpack",
        moved=4e6,
    )(ids, keep, swap_cores(give), dealt)
    small = small.reshape(16, 16, -1)
    residual_grad = small[4]
    small, triple_grad, output_grad, *combined_got = join(small, triple_grad, output_grad, *combined_got)

    combined_sum = total(pieces, combined_got)
    my_center = my_inputs - jnp.mean(my_inputs, axis=-1, keepdims=True)
    my_inverse = lax.rsqrt(jnp.mean(my_center * my_center, axis=-1, keepdims=True) + EPSILON)
    my_normal = my_center * my_inverse
    my_grad = my_inverse * (
        combined_sum
        - jnp.mean(combined_sum, axis=-1, keepdims=True)
        - my_normal * jnp.mean(combined_sum * my_normal, axis=-1, keepdims=True)
    )
    tokens_grad = whole_block((my_cotangent.astype(F32) + my_grad).astype(BF))
    return (
        mixed,
        tokens_grad,
        triple_grad,
        small[6:8].reshape(32, -1)[:24].reshape(b_qkv.shape),
        output_grad,
        residual_grad,
        expand_grad,
        small[8:10].reshape(b_in.shape),
        shrink_grad,
        residual_grad,
        small[0:2],
        small[2:4],
    )


def solution(mesh):
    placed = (
        P("blk", None),
        P(None, "blk", "tp"),
        P(None, "tp", "blk"),
        P("tp", "blk"),
        P(None, "blk"),
        P("blk", "tp"),
        P("tp", "blk"),
        P("tp", "blk"),
        P(None, "blk"),
        P(None, None, "blk"),
        P(None, None, "blk"),
        P("blk"),
        P("blk"),
        P("blk", None),
    )
    two_to_a_head = mesh.shape["blk"] == 2 * HEADS
    return jax.shard_map(
        body if two_to_a_head else general_body,
        mesh=mesh,
        in_specs=placed,
        out_specs=(
            P("blk", None),
            P("blk", None),
            P(None, "blk", "tp"),
            P(None, "tp", "blk"),
            P("tp", "blk"),
            P(None, "blk"),
            P("blk", "tp"),
            P("tp", "blk"),
            P("tp", "blk"),
            P(None, "blk"),
            P(None, None, "blk"),
            P(None, None, "blk"),
        ),
        check_vma=False,
    )
```

```python
import math

import jax
import jax.numpy as jnp
from jax import lax
from jax.experimental import pallas as pl
from jax.experimental.pallas import tpu as pltpu
from jax.sharding import PartitionSpec as P

HEADS = 8
HEAD = 256
ROT = 64

EPSILON = 1e-05
NEGATIVE = -1e30
BF = jnp.bfloat16
F32 = jnp.float32


def dot(left, right, dims):
    return lax.dot_general(left, right, (dims, ((), ())), preferred_element_type=F32)


def swap_cores(value):
    return lax.ppermute(value, "tp", [(0, 1), (1, 0)])


def from_peer(value, mask):
    count = lax.axis_size("blk")
    return lax.ppermute(value, "blk", [(i, i ^ mask) for i in range(count)])


def spread(value, masks):
    return jnp.stack([value] + [from_peer(value, mask) for mask in masks])


def collect(parts, masks):
    total = parts[0].astype(F32)
    for at, mask in enumerate(masks):
        total = total + from_peer(parts[at + 1], mask).astype(F32)
    return total


def by_core(core, mine, other):
    first = core == 0
    return jnp.where(first, mine, other), jnp.where(first, other, mine)


def gelu_and_slope(values):
    cumulative = 0.5 * (1.0 + lax.erf(values * (1.0 / math.sqrt(2.0))))
    density = jnp.exp(-0.5 * values * values) * (1.0 / math.sqrt(2.0 * math.pi))
    return values * cumulative, cumulative + values * density


def turn(values, cosine, sine):
    half = ROT // 2
    first, second = values[:, :half], values[:, half:ROT]
    return jnp.concatenate(
        [first * cosine - second * sine, second * cosine + first * sine, values[:, ROT:]],
        axis=1,
    )


def general_body(
    tokens,
    w_qkv,
    b_qkv,
    w_out,
    b_out,
    w_in,
    b_in,
    w_out2,
    b_out2,
    norm_gain,
    norm_shift,
    doc_start,
    live,
    cotangent,
):
    blocks = lax.axis_size("blk")
    cores = lax.axis_size("tp")
    me, core = lax.axis_index("blk"), lax.axis_index("tp")
    rows, width = tokens.shape
    depth = w_in.shape[0]
    part = rows // cores
    quarter = part // 2
    group = blocks // HEADS
    columns = HEAD // group
    units = w_in.shape[1] // blocks
    cut = depth // cores
    near = columns // cores
    scale = 1.0 / math.sqrt(HEAD)

    masks_x = list(range(1, group))
    masks_y = [group]
    masks_z = [2 * group * i for i in range(1, blocks // (2 * group))]
    size_x, size_y, size_z = group, 2, len(masks_z) + 1

    def gather(value):
        over_z = spread(value, masks_z)
        one = spread(spread(over_z[:, :quarter], masks_y), masks_x)
        two = spread(spread(over_z[:, quarter:], masks_x), masks_y)
        return one.reshape(-1, value.shape[-1]), two.reshape(-1, value.shape[-1])

    def scatter(one, two):
        one = one.reshape(size_x, size_y, size_z, quarter, width)
        two = two.reshape(size_y, size_x, size_z, quarter, width)
        one = collect(collect(one, masks_x).astype(BF), masks_y)
        two = collect(collect(two, masks_y).astype(BF), masks_x)
        return collect(jnp.concatenate([one, two], axis=1).astype(BF), masks_z)

    small = jnp.concatenate(
        [
            norm_gain.reshape(-1),
            norm_shift.reshape(-1),
            b_out.reshape(-1),
            b_out2.reshape(-1),
            b_qkv.reshape(-1),
            b_in.reshape(-1),
            (doc_start // 256).astype(BF),
            (doc_start % 256).astype(BF),
            live.astype(BF),
        ]
    )
    small_rows = -(-small.size // 2048) * 16
    small = jnp.pad(small, (0, small_rows * 128 - small.size)).reshape(small_rows * 128 // columns, columns)
    lines = small.shape[0]

    own_heads = HEADS // cores * group
    triple = w_qkv.reshape(3, cores, cut, own_heads, columns).transpose(1, 3, 0, 2, 4)
    triple = triple.reshape(cores, own_heads, 3 * cut, columns)
    outward = w_out.reshape(own_heads, cores, near, depth).transpose(1, 0, 2, 3)
    outward = outward.reshape(cores, own_heads, near * depth // columns, columns)
    dealt = jnp.concatenate([triple, outward], axis=2)
    keep = lax.dynamic_index_in_dim(dealt, core, 0, keepdims=False)
    give = lax.dynamic_index_in_dim(dealt, 1 - core, 0, keepdims=False)
    got = swap_cores(give)
    heads_low, heads_high = by_core(core, keep, got)
    deal = jnp.concatenate(
        [
            jnp.concatenate([heads_low, heads_high]),
            jnp.broadcast_to(small, (blocks,) + small.shape),
        ],
        axis=1,
    )
    here = lax.all_to_all(deal, "blk", 0, 0, tiled=True)
    there = swap_cores(here)
    both = jnp.stack(by_core(core, here, there))

    expand_deal = w_in.reshape(depth, blocks, units).transpose(1, 0, 2)
    expand_mine = lax.all_to_all(expand_deal, "blk", 0, 0, tiled=True).reshape(width, units)
    expand_other = swap_cores(expand_mine)
    shrink_mine = lax.all_to_all(
        w_out2.reshape(blocks, units, depth), "blk", 0, 0, tiled=True
    )
    shrink_other = swap_cores(shrink_mine)
    w_expand = jnp.concatenate([expand_mine, expand_other], axis=1)
    w_shrink = jnp.concatenate([shrink_mine, shrink_other], axis=1)
    w_shrink = w_shrink.transpose(1, 0, 2).reshape(2 * units, width)

    my_tokens = lax.dynamic_slice_in_dim(tokens, core * part, part, 0)
    my_cotangent = lax.dynamic_slice_in_dim(cotangent, core * part, part, 0)
    all_tokens = jnp.concatenate(gather(my_tokens))
    all_cotangent = jnp.concatenate(gather(my_cotangent))
    count = all_tokens.shape[0]

    at = 3 * cut
    mid = at + near * depth // columns
    w_triple = both[:, :, :at].reshape(cores, blocks, 3, cut, columns)
    w_triple = w_triple.transpose(1, 0, 3, 2, 4).reshape(width, 3 * columns)
    w_near = both[:, :, at:mid].reshape(cores, blocks, near, depth)
    w_near = w_near.transpose(0, 2, 1, 3).reshape(columns, width)
    w_head = spread(w_near, masks_x).reshape(HEAD, width)
    flat = both[:, :, mid:].reshape(cores, blocks, -1)

    def take(offset, like):
        return flat[:, :, offset : offset + like.size].reshape((cores, blocks) + like.shape), offset + like.size

    offset = 0
    gain_all, offset = take(offset, norm_gain)
    shift_all, offset = take(offset, norm_shift)
    out_all, offset = take(offset, b_out)
    out2_all, offset = take(offset, b_out2)
    triple_all, offset = take(offset, b_qkv)
    expand_all, offset = take(offset, b_in)
    start_high, offset = take(offset, doc_start)
    start_low, offset = take(offset, doc_start)
    live_all, offset = take(offset, live)
    gains = gain_all[0].transpose(1, 2, 0, 3).reshape(2, width).astype(F32)
    shifts = shift_all[0].transpose(1, 2, 0, 3).reshape(2, width).astype(F32)
    residual_shift = (out_all[0].astype(F32) + out2_all[0].astype(F32)).transpose(1, 0, 2).reshape(width)
    triple_shift = triple_all.astype(F32).transpose(2, 0, 3, 1, 4).reshape(3, width)
    triple_shift = lax.dynamic_slice_in_dim(triple_shift, me * columns, columns, 1).reshape(-1)
    expand_shift = expand_all.astype(F32).transpose(0, 2, 1, 3).reshape(cores, -1)
    expand_shift = lax.dynamic_slice_in_dim(expand_shift, me * units, units, 1)
    expand_shift = jnp.concatenate(by_core(core, expand_shift[0], expand_shift[1]))
    starts = (start_high[0].astype(F32) * 256.0 + start_low[0].astype(F32)).astype(jnp.int32)
    lives = live_all[0].astype(jnp.int32)

    x_at = jnp.arange(size_x)[:, None, None]
    y_at = group * jnp.arange(size_y)[None, :, None]
    z_at = 2 * group * jnp.arange(size_z)[None, None, :]
    order = (x_at + y_at + z_at) ^ me
    inside = jnp.arange(quarter, dtype=jnp.int32)

    def index_of(which):
        base = order[..., None] * rows + which * part + inside
        one, two = base, base + quarter
        return jnp.concatenate(
            [one.reshape(size_x, -1), two.reshape(size_x, -1)], axis=1
        )

    def heads_order(value):
        tail = value.shape[1:]
        one = value[: count // 2].reshape((size_x, -1) + tail)
        two = value[count // 2 :].reshape((size_y, size_x, -1) + tail)
        two = jnp.swapaxes(two, 0, 1).reshape((size_x, -1) + tail)
        return jnp.concatenate([one, two], axis=1)

    def gathered_order(value):
        tail = value.shape[2:]
        middle = value.shape[1] // 2
        one = value[:, :middle].reshape((count // 2,) + tail)
        two = value[:, middle:].reshape((size_x, size_y, -1) + tail)
        two = jnp.swapaxes(two, 0, 1).reshape((count // 2,) + tail)
        return jnp.concatenate([one, two])

    index_mine, index_other = index_of(core), index_of(1 - core)
    index = jnp.concatenate([index_mine.reshape(-1), index_other.reshape(-1)])
    token_start = starts.reshape(-1)[index]
    token_live = lives.reshape(-1)[index]

    inputs = all_tokens.astype(F32)
    center = inputs - jnp.mean(inputs, axis=-1, keepdims=True)
    inverse = lax.rsqrt(jnp.mean(center * center, axis=-1, keepdims=True) + EPSILON)
    normal = center * inverse
    normed_attend = (normal * gains[0] + shifts[0]).astype(BF)
    normed_feed = (normal * gains[1] + shifts[1]).astype(BF)

    linear = dot(normed_attend, w_triple, ((1,), (0,))) + triple_shift
    linear = heads_order(linear).reshape(count, 3, columns)
    steps = jnp.arange(ROT // 2, dtype=F32)
    speed = 10000.0 ** (-2.0 * steps / ROT)
    place = (index - token_start).astype(F32)
    angle = place[:count, None] * speed[None, :]
    cosine, sine = jnp.cos(angle), jnp.sin(angle)
    slot = me % group

    def turn_pieces(pieces, cosine, sine):
        if columns >= ROT:
            return jnp.stack(
                [
                    turn(
                        pieces[r],
                        jnp.where(slot == r, cosine, 1.0),
                        jnp.where(slot == r, sine, 0.0),
                    )
                    for r in range(group)
                ]
            )
        place_of = jnp.arange(group) ^ slot
        whole = jnp.swapaxes(pieces[place_of], 0, 1).reshape(pieces.shape[1], HEAD)
        whole = turn(whole, cosine, sine).reshape(-1, group, columns)
        return jnp.swapaxes(whole, 0, 1)[place_of]

    if columns >= ROT:
        own_cosine = jnp.where(slot == 0, cosine, 1.0)
        own_sine = jnp.where(slot == 0, sine, 0.0)
        queries = turn(linear[:, 0], own_cosine, own_sine)
        keys = turn(linear[:, 1], own_cosine, own_sine)
    else:
        queries, keys = linear[:, 0], linear[:, 1]
    mine = jnp.concatenate([queries, keys, linear[:, 2]], axis=1).astype(BF)

    def align(value, r):
        slabs = value.reshape((size_x, -1) + value.shape[1:])
        return jnp.stack([slabs[x ^ r] for x in range(size_x)]).reshape(value.shape)

    pieces = [mine] + [align(from_peer(mine, r), r) for r in masks_x]
    pieces = jnp.stack(pieces).reshape(group, count, 3, columns)
    if columns < ROT:
        turned = [turn_pieces(pieces[:, :, s].astype(F32), cosine, sine).astype(BF) for s in (0, 1)]
        pieces = jnp.stack(turned + [pieces[:, :, 2]], axis=2)
    own_triple = pieces.transpose(2, 1, 0, 3).reshape(3, count, HEAD)
    other_triple = swap_cores(own_triple)
    queries, keys, values = jnp.concatenate([own_triple, other_triple], axis=1)

    cotangent_x = heads_order(all_cotangent)
    grad_attended = dot(all_cotangent, w_head, ((1,), (1,))).astype(BF)
    grad_attended = heads_order(grad_attended).reshape(count, HEAD)
    grad_attended = jnp.concatenate([grad_attended, swap_cores(grad_attended)])

    share = count // size_x
    mine_index, mine_start, mine_live = index[:share], token_start[:share], token_live[:share]

    def allowed(query_index, query_start, key_index, key_start, key_live):
        same = query_start == key_start
        causal = key_index <= query_index
        usable = (key_live == 1) | (key_index == query_index)
        return same & causal & usable

    mask = allowed(mine_index[:, None], mine_start[:, None], index[None], token_start[None], token_live[None])
    scores = dot(queries[:share], keys, ((1,), (1,))) * scale
    masked = jnp.where(mask, scores, NEGATIVE)
    top = jnp.max(masked, axis=-1, keepdims=True)
    weight = jnp.where(mask, jnp.exp(masked - top), 0.0)
    total = jnp.sum(weight, axis=-1, keepdims=True)
    prob = weight / total
    attended = dot(prob.astype(BF), values, ((1,), (0,)))
    log_total = top + jnp.log(total)
    delta = jnp.sum(grad_attended[:share].astype(F32) * attended, axis=-1, keepdims=True)
    push = dot(grad_attended[:share], values, ((1,), (1,)))
    slope = (prob * (push - delta)).astype(BF)
    grad_queries = dot(slope, keys, ((1,), (0,))) * scale
    attended = attended.astype(BF)

    marks = jnp.concatenate([log_total, delta], axis=1).T
    marks = spread(marks, masks_x).transpose(1, 0, 2).reshape(2, count)
    marks = jnp.concatenate([marks, swap_cores(marks)], axis=1)
    mask = allowed(index[None], token_start[None], mine_index[:, None], mine_start[:, None], mine_live[:, None])
    scores = dot(keys[:share], queries, ((1,), (1,))) * scale
    prob = jnp.where(mask, jnp.exp(jnp.where(mask, scores, NEGATIVE) - marks[0][None]), 0.0)
    grad_values = dot(prob.astype(BF), grad_attended, ((1,), (0,)))
    push = dot(values[:share], grad_attended, ((1,), (1,)))
    slope = (prob * (push - marks[1][None])).astype(BF)
    grad_keys = dot(slope, queries, ((1,), (0,))) * scale

    expanded = dot(normed_feed, w_expand, ((1,), (0,))) + expand_shift
    activated, bend = gelu_and_slope(expanded)
    activated = activated.astype(BF)
    grad_activated = dot(all_cotangent, w_shrink, ((1,), (1,)))
    grad_expanded = (bend * grad_activated).astype(BF)

    branch = dot(activated, w_shrink, ((1,), (0,)))
    attend_part = dot(attended, w_head, ((1,), (0,)))
    rest = jnp.zeros((size_x - 1,) + attend_part.shape, F32)
    attend_part = gathered_order(jnp.concatenate([attend_part[None], rest]))
    branch = (branch + attend_part).astype(BF)
    branch = scatter(branch[: count // 2], branch[count // 2 :])
    my_inputs = my_tokens.astype(F32)
    my_mixed = (my_inputs + branch.reshape(part, width) + residual_shift).astype(BF)

    def whole_block(value):
        low, high = by_core(core, value, swap_cores(value))
        return jnp.concatenate([low, high])

    mixed = whole_block(my_mixed)

    grad_shrink = dot(activated, all_cotangent, ((0,), (0,)))
    grad_expand = dot(normed_feed, grad_expanded, ((0,), (0,)))
    grad_shrink = grad_shrink[:units] + swap_cores(grad_shrink[units:].astype(BF)).astype(F32)
    grad_expand = grad_expand[:, :units] + swap_cores(grad_expand[:, units:].astype(BF)).astype(F32)
    shrink_deal = grad_shrink.astype(BF).reshape(units, blocks, depth).transpose(1, 0, 2)
    expand_deal = grad_expand.astype(BF).reshape(blocks, depth, units)
    shrink_grad = lax.all_to_all(shrink_deal, "blk", 0, 0, tiled=True)
    shrink_grad = shrink_grad.reshape(-1, depth).astype(F32)
    expand_grad = lax.all_to_all(expand_deal, "blk", 0, 0, tiled=True)
    expand_grad = expand_grad.transpose(1, 0, 2).reshape(depth, -1).astype(F32)

    def by_pieces(value):
        return value.reshape(share, group, columns).transpose(1, 0, 2)

    own_cosine, own_sine = cosine[:share], -sine[:share]
    back = [
        turn_pieces(by_pieces(grad_queries), own_cosine, own_sine),
        turn_pieces(by_pieces(grad_keys), own_cosine, own_sine),
        by_pieces(grad_values),
    ]
    back = jnp.concatenate(back, axis=2).astype(BF)
    back = jnp.concatenate([back, by_pieces(attended)], axis=2)
    back = jnp.stack([back[0]] + [from_peer(back[r], r) for r in masks_x])
    back = gathered_order(back)
    grad_linear, attended_near = back[:, : 3 * columns], back[:, 3 * columns :]
    grad_triple = dot(normed_attend, grad_linear, ((0,), (0,)))
    grad_out = dot(attended_near, all_cotangent, ((0,), (0,)))
    grad_triple = grad_triple.reshape(blocks, cores, cut, 3, columns).transpose(1, 0, 3, 2, 4)
    grad_triple = grad_triple.reshape(cores, blocks, 3 * cut, columns)
    grad_out = grad_out.reshape(cores, near, blocks, depth).transpose(0, 2, 1, 3)
    grad_out = grad_out.reshape(cores, blocks, near * depth // columns, columns)
    dealt = jnp.concatenate([grad_triple, grad_out], axis=2)
    keep = lax.dynamic_index_in_dim(dealt, core, 0, keepdims=False)
    give = lax.dynamic_index_in_dim(dealt, 1 - core, 0, keepdims=False)
    dealt = (keep + swap_cores(give.astype(BF)).astype(F32)).astype(BF)
    dealt = lax.all_to_all(dealt, "blk", 0, 0, tiled=True)
    dealt = dealt.reshape((cores, own_heads) + dealt.shape[1:])
    keep = lax.dynamic_index_in_dim(dealt, core, 0, keepdims=False)
    give = lax.dynamic_index_in_dim(dealt, 1 - core, 0, keepdims=False)
    dealt = jnp.stack(by_core(core, keep, swap_cores(give)))
    triple_grad = dealt[:, :, :at].reshape(cores, own_heads, 3, cut, columns)
    triple_grad = triple_grad.transpose(2, 0, 3, 1, 4).reshape(3, depth, -1).astype(F32)
    output_grad = dealt[:, :, at:].reshape(cores, own_heads, near, depth)
    output_grad = output_grad.transpose(1, 0, 2, 3).reshape(-1, depth).astype(F32)

    grad_attend_norm = dot(grad_linear, w_triple, ((1,), (1,)))
    grad_feed_norm = dot(grad_expanded, w_expand, ((1,), (1,)))
    combined = (gains[0] * grad_attend_norm + gains[1] * grad_feed_norm).astype(BF)
    combined = scatter(combined[: count // 2], combined[count // 2 :]).reshape(part, width)
    my_center = my_inputs - jnp.mean(my_inputs, axis=-1, keepdims=True)
    my_inverse = lax.rsqrt(jnp.mean(my_center * my_center, axis=-1, keepdims=True) + EPSILON)
    my_normal = my_center * my_inverse
    my_grad = my_inverse * (
        combined
        - jnp.mean(combined, axis=-1, keepdims=True)
        - my_normal * jnp.mean(combined * my_normal, axis=-1, keepdims=True)
    )
    tokens_grad = whole_block((my_cotangent.astype(F32) + my_grad).astype(BF))

    sums = [
        jnp.sum(normal * grad_attend_norm, axis=0),
        jnp.sum(normal * grad_feed_norm, axis=0),
        jnp.sum(grad_attend_norm, axis=0),
        jnp.sum(grad_feed_norm, axis=0),
        jnp.sum(all_cotangent.astype(F32), axis=0),
        jnp.sum(grad_expanded.astype(F32), axis=0),
        jnp.sum(grad_linear.astype(F32), axis=0),
    ]
    sums = jnp.concatenate(sums)
    other = swap_cores(sums)
    added = sums + other
    norm_sums = added[: 4 * width].reshape(4, width // 128, blocks, -1).transpose(2, 0, 1, 3)
    residual_sum = added[4 * width : 5 * width].reshape(width // 128, 128)
    lanes = 128 // blocks
    residual_grad = lax.dynamic_slice_in_dim(residual_sum, me * lanes, lanes, 1)
    unit_sum = sums[5 * width : 5 * width + units] + other[5 * width + units : 5 * width + 2 * units]
    unit_sums = lax.dynamic_update_slice_in_dim(
        jnp.zeros((w_in.shape[1],), F32), unit_sum, me * units, 0
    )
    unit_sums = unit_sums.reshape(-1, blocks, lanes).transpose(1, 0, 2)
    line_sum = added[5 * width + 2 * units :].reshape(3, columns)
    line_sums = lax.dynamic_update_slice_in_dim(
        jnp.zeros((3, width), F32), line_sum, me * columns, 1
    )
    line_sums = lax.dynamic_slice_in_dim(line_sums, core * (width // cores), width // cores, 1)
    line_sums = line_sums.reshape(3, -1, blocks, lanes).transpose(2, 0, 1, 3)
    tiny = jnp.concatenate(
        [norm_sums.reshape(blocks, -1), unit_sums.reshape(blocks, -1), line_sums.reshape(blocks, -1)],
        axis=1,
    )
    tiny = jnp.sum(lax.all_to_all(tiny, "blk", 0, 0, tiled=True), axis=0)
    first = norm_gain.size
    gain_grad = tiny[:first].reshape(norm_gain.shape)
    shift_grad = tiny[first : 2 * first].reshape(norm_shift.shape)
    expand_bias_grad = tiny[2 * first : 2 * first + b_in.size].reshape(b_in.shape)
    triple_bias_grad = tiny[2 * first + b_in.size :].reshape(b_qkv.shape)
    return (
        mixed,
        tokens_grad,
        triple_grad,
        triple_bias_grad,
        output_grad,
        residual_grad,
        expand_grad,
        expand_bias_grad,
        shrink_grad,
        residual_grad,
        gain_grad,
        shift_grad,
    )


VMEM = pl.BlockSpec(memory_space=pltpu.VMEM)
SMEM = pl.BlockSpec(memory_space=pltpu.SMEM)
GRANT = 28 * 1024 * 1024
MARK_COS, MARK_SIN = 32, 64
WEIGHTS = {"deal": 10, "norm": 10, "feed": 10, "query": 10, "key": 3, "by_z": 3, "fold": 100}
WIDE = 256


def run_kernel(kernel, outs, grid=None, ins=None, out_specs=None, scratch=(), flops=0, moved=0, name=None):
    weight = WEIGHTS.get(name, 1)
    outs = [jax.ShapeDtypeStruct(shape, kind) for shape, kind in outs]
    single = len(outs) == 1
    out_specs = out_specs or [VMEM] * len(outs)
    extra = {} if grid is None else {"grid": grid}
    return pl.pallas_call(
        kernel,
        out_shape=outs[0] if single else outs,
        in_specs=ins,
        out_specs=out_specs[0] if single else out_specs,
        scratch_shapes=list(scratch),
        compiler_params=pltpu.CompilerParams(vmem_limit_bytes=GRANT),
        cost_estimate=pl.CostEstimate(flops=int(flops * weight), bytes_accessed=int(moved * weight), transcendentals=0),
        name=name,
        **extra,
    )


def chunk_bits(half, at, lanes):
    z = at % lanes
    low, high = (at // lanes) % 2, at // (2 * lanes)
    x, y = (high, low) if half == 0 else (low, high)
    return x + 2 * y + 4 * z


class Rows:
    def __init__(self, blocks, cores, rows):
        self.blocks, self.rows = blocks, rows
        self.part = rows // cores
        self.chunk = self.part // 2
        self.half = blocks * self.chunk
        self.count = 2 * self.half
        self.share = self.half
        self.sizes_z = blocks // 4

    def natural(self, me, core, half, at):
        block = me ^ chunk_bits(half, at, self.sizes_z)
        return block * self.rows + core * self.part + half * self.chunk

    def x_rows(self, x):
        h, q = self.half // 2, self.half // 4
        return [
            (x * h, 0, h),
            (self.half + x * q, h, q),
            (self.half + 2 * q + x * q, h + q, q),
        ]

    def pairs(self):
        mine, peer = self.x_rows(0), self.x_rows(1)
        both = [(a[0], b[0], a[2]) for a, b in zip(mine, peer)]
        return both + [(b, a, n) for a, b, n in both]


def nn(left, right):
    return lax.dot_general(left, right, (((1,), (0,)), ((), ())), preferred_element_type=F32)


def nt(left, right):
    return lax.dot_general(left, right, (((1,), (1,)), ((), ())), preferred_element_type=F32)


def lane_of(shape):
    return lax.broadcasted_iota(jnp.int32, shape, len(shape) - 1)


def turn_lanes(values, table, active, sign):
    lane = lane_of(values.shape)
    first, second = lane < ROT // 2, lane < ROT
    cosine = jnp.where(first, pltpu.roll(table, 128 - MARK_COS, 1), table)
    sine_first = pltpu.roll(table, 128 - MARK_SIN, 1)
    sine_second = pltpu.roll(table, 128 - MARK_SIN + ROT // 2, 1)
    sine = jnp.where(first, -sine_first, sine_second) * sign
    cosine = jnp.where(second & active, cosine, 1.0)
    sine = jnp.where(second & active, sine, 0.0)
    partner = jnp.where(first, pltpu.roll(values, 128 - ROT // 2, 1), pltpu.roll(values, ROT // 2, 1))
    return values * cosine + partner * sine


def deal_kernel(cut, blocks, ids, speed, here, there, triple, near, marks, norms, shifts, lines, flip):
    me, core = ids[0], ids[1]
    width = lines.shape[2]
    for source in range(blocks):
        for who, ref in ((core, here), (1 - core, there)):
            at = pl.multiple_of(source * 2 * cut + who * cut, cut)
            for s in range(3):
                triple[pl.ds(at, cut), s * 128 : (s + 1) * 128] = ref[source, s * cut : (s + 1) * cut, :]
            at = pl.multiple_of(who * cut, cut)
            near[pl.ds(at, cut), source * 128 : (source + 1) * 128] = ref[source, 3 * cut : 4 * cut, :]

    lanes = 128 // blocks
    row = lax.broadcasted_iota(jnp.int32, (128, width), 0)
    lane = lane_of((128, width))
    deal = ((row // lanes == lane // 128) & (row % lanes == lane % lanes)).astype(BF)
    lane = lane_of((16, width)) % 128 // lanes
    flip[...] = jnp.zeros_like(flip)
    for which, ref in enumerate((here, there)):
        total = jnp.zeros((16, width), F32)
        for source in range(blocks):
            small = ref[source, 4 * cut : 4 * cut + 16, :]
            total = total + jnp.where(lane == source, nn(small, deal), 0.0)
            if which == 0:
                small = small.astype(F32)
                flip[source : source + 1, :] = small[10:11] * 256.0 + small[11:12]
                flip[blocks + source : blocks + source + 1, :] = small[12:13]
        lines[which] = total
    norms[:4, :] = lines[0, :4, :]
    norms[4:5, :] = lines[0, 4:5, :] + lines[0, 5:6, :]
    norms[5:, :] = jnp.zeros((3, width), F32)
    shifts[...] = jnp.zeros_like(shifts)
    heads = blocks // 2
    ours = me // heads == core
    for s in range(3):
        at = pl.multiple_of((me % heads + s % 2 * heads) * 128, 128)
        both = [lines[k, 6 + s // 2 : 7 + s // 2, pl.ds(at, 128)] for k in (0, 1)]
        shifts[0:1, s * 128 : (s + 1) * 128] = jnp.where(ours, both[0], both[1])
    units = 2 * width // blocks
    at = pl.multiple_of(me % heads * units, units)
    for k in (0, 1):
        shifts[1:2, k * units : (k + 1) * units] = lines[k, pl.ds(8 + me // heads, 1), pl.ds(at, units)]

    turned = flip[...].T
    lane = lane_of((128, 128))
    row = lax.broadcasted_iota(jnp.int32, (128, 128), 0).astype(F32)
    for q in range(blocks // 4):
        place = jnp.zeros((128, 128), F32)
        for g in range(4):
            b = 4 * q + g
            place = jnp.where(lane // 32 == g, row + b * 128.0 - turned[:, b : b + 1], place)
        angle = place * speed[0:1, :]
        cosine, sine = jnp.cos(angle), jnp.sin(angle)
        for g in range(4):
            b = 4 * q + g
            index = row + b * 128.0
            table = jnp.where(lane == 0, index, 0.0)
            table = jnp.where(lane == 1, jnp.where(turned[:, blocks + b : blocks + b + 1] == 1.0, index, -1.0), table)
            table = jnp.where(lane == 2, turned[:, b : b + 1], table)
            table = jnp.where(lane // 32 == 1, pltpu.roll(cosine, (MARK_COS - g * 32) % 128, 1), table)
            table = jnp.where(lane // 32 == 2, pltpu.roll(sine, (MARK_SIN - g * 32) % 128, 1), table)
            marks[b * 128 : (b + 1) * 128, :] = table


def feed_deal_kernel(blocks, units, expand, shrink, out):
    for k in range(blocks):
        out[k, :units, :] = expand[:, k * units : (k + 1) * units].T
        out[k, units:, :] = shrink[k * units : (k + 1) * units, :]


def pick(i, refs, tile):
    for k, ref in enumerate(refs):

        @pl.when(i == k)
        def _(ref=ref):
            tile[...] = ref[...]


def norm_kernel(r, ids, t0, t1, t2, t3, norms, weight, shifts, marks, feed, stats, mine, tile, table, attend):
    i = pl.program_id(0)
    me, core = ids[0], ids[1]
    pick(i, (t0, t1, t2, t3), tile)
    for half in (0, 1):

        @pl.when(i // 2 == half)
        def _(half=half):
            for q in range(8):
                at = r.natural(me, core, half, (i % 2) * 8 + q)
                table[q * r.chunk : (q + 1) * r.chunk, :] = marks[pl.ds(pl.multiple_of(at, r.chunk), r.chunk), :]

    step = 16
    lane = lane_of((step, 128))

    @pl.loop(0, tile.shape[0] // step, unroll=4)
    def _(j):
        rows = pl.ds(pl.multiple_of(j * step, step), step)
        values = tile[rows, :].astype(F32)
        mean = jnp.mean(values, axis=-1, keepdims=True)
        center = values - mean
        inverse = lax.rsqrt(jnp.mean(center * center, axis=-1, keepdims=True) + EPSILON)
        value = center * inverse
        attend[rows, :] = (value * norms[0:1, :] + norms[2:3, :]).astype(BF)
        feed[rows, :] = (value * norms[1:2, :] + norms[3:4, :]).astype(BF)
        stats[rows, :] = jnp.where(lane == 0, mean, inverse)

    linear = nn(attend[...], weight[...]) + shifts[0:1, :384]
    active = me % 2 == 0
    for s in (0, 1):
        cols = slice(s * 128, (s + 1) * 128)
        mine[:, cols] = turn_lanes(linear[:, cols], table[...], active, 1.0).astype(BF)
    mine[:, 256:] = linear[:, 256:].astype(BF)


def normal_of(tile, stats):
    return (tile.astype(F32) - stats[:, 0:1]) * stats[:, 1:2]


def gather_columns(r, out, low, high, column):
    cols = slice(column * 128, (column + 1) * 128)
    out[:, :128] = low[:, cols]
    for here, there, size in r.pairs():
        out[here : here + size, 128:] = high[there : there + size, cols]


def gather_marks(r, ids, marks, table, line):
    me, core = ids[0], ids[1]
    for w in (0, 1):
        who = core if w == 0 else 1 - core
        for half in (0, 1):
            for q in range(16):
                at = r.natural(me, who, half, q)
                to = w * r.count + half * r.half + q * r.chunk
                table[to : to + r.chunk, :] = marks[pl.ds(pl.multiple_of(at, r.chunk), r.chunk), :]
    for b in range(2 * r.count // 128):
        line[:, b * 128 : (b + 1) * 128] = table[b * 128 : (b + 1) * 128, :].T[:8, :]


def own_rows(r, out, ref, columns=slice(None)):
    for row, place, size in r.x_rows(0):
        out[place : place + size, :] = ref[row : row + size, columns]


def query_kernel(r, scale, ids, a00, a01, a10, a11, grads, marks, attended, keep, send, lines,
                 keys, values, queries, pushes, table, line, mine):
    i = pl.program_id(0)
    me = ids[0]
    count, tile = r.count, r.share // 2

    @pl.when(i == 0)
    def _():
        gather_columns(r, keys.at[:count], a00, a01, 1)
        gather_columns(r, keys.at[count:], a10, a11, 1)
        gather_columns(r, values.at[:count], a00, a01, 2)
        gather_columns(r, values.at[count:], a10, a11, 2)
        for row, place, size in r.x_rows(0):
            queries[place : place + size, :128] = a00[row : row + size, :128]
        for (row, place, size), (there, _, _) in zip(r.x_rows(0), r.x_rows(1)):
            queries[place : place + size, 128:] = a01[there : there + size, :128]
        own_rows(r, pushes, grads)
        gather_marks(r, ids, marks, table, line)
        own_rows(r, mine, table.at[:count])

    rows = pl.ds(pl.multiple_of(i * tile, tile), tile)
    mark = mine[rows, :]
    q_at, q_start = mark[:, 0:1], mark[:, 2:3]
    k_at, k_live = line[0:1, :], line[1:2, :]
    mask = ((k_live >= q_start) & (k_at <= q_at)) | (k_at == q_at)
    scores = jnp.where(mask, nt(queries[rows, :], keys[...]) * scale, NEGATIVE)
    top = jnp.max(scores, axis=-1, keepdims=True)
    weight = jnp.where(mask, jnp.exp(scores - top), 0.0)
    total = jnp.sum(weight, axis=-1, keepdims=True)
    prob = weight * (1.0 / total)
    result = nn(prob.astype(BF), values[...])
    grad = pushes[rows, :]
    delta = jnp.sum(grad.astype(F32) * result, axis=-1, keepdims=True)
    slope = (prob * (nt(grad, values[...]) - delta)).astype(BF)
    back = nn(slope, keys[...]) * scale
    result = result.astype(BF)
    attended[...] = result
    for k, ref in enumerate((keep, send)):
        cols = slice(k * 128, (k + 1) * 128)
        ref[:, :128] = turn_lanes(back[:, cols], mark, me % 2 == k, -1.0).astype(BF)
        ref[:, 128:] = result[:, cols]
    lane = lane_of((tile, 128))
    both = jnp.where(lane == 0, top + jnp.log(total), jnp.where(lane == 1, delta, 0.0))
    for b in range(tile // 128):
        lines[:, b * 128 : (b + 1) * 128] = both[b * 128 : (b + 1) * 128, :].T[:8, :]


def key_kernel(r, scale, ids, a00, a01, a10, a11, grads, other_grads, l00, l01, l10, l11, marks, keep, send,
               queries, pushes, keys, values, table, line, mine, tops):
    i = pl.program_id(0)
    me = ids[0]
    count, tile = r.count, r.share // 2

    @pl.when(i == 0)
    def _():
        gather_columns(r, queries.at[:count], a00, a01, 0)
        gather_columns(r, queries.at[count:], a10, a11, 0)
        pushes[:count, :] = grads[...]
        pushes[count:, :] = other_grads[...]
        for k, out in ((1, keys), (2, values)):
            cols = slice(k * 128, (k + 1) * 128)
            for row, place, size in r.x_rows(0):
                out[place : place + size, :128] = a00[row : row + size, cols]
            for (row, place, size), (there, _, _) in zip(r.x_rows(0), r.x_rows(1)):
                out[place : place + size, 128:] = a01[there : there + size, cols]
        gather_marks(r, ids, marks, table, line)
        own_rows(r, mine, table.at[:count])
        for base, low, high in ((0, l00, l01), (count, l10, l11)):
            for x, ref in ((0, low), (1, high)):
                for row, place, size in r.x_rows(x):
                    tops[:, base + row : base + row + size] = ref[:, place : place + size]

    rows = pl.ds(pl.multiple_of(i * tile, tile), tile)
    mark = mine[rows, :]
    k_at, k_live = mark[:, 0:1], mark[:, 1:2]
    q_at, q_start = line[0:1, :], line[2:3, :]
    mask = ((k_live >= q_start) & (k_at <= q_at)) | (k_at == q_at)
    scores = nt(keys[rows, :], queries[...]) * scale
    prob = jnp.where(mask, jnp.exp(scores - tops[0:1, :]), 0.0)
    grad_values = nn(prob.astype(BF), pushes[...])
    slope = (prob * (nt(values[rows, :], pushes[...]) - tops[1:2, :])).astype(BF)
    back = nn(slope, queries[...]) * scale
    for k, ref in enumerate((keep, send)):
        cols = slice(k * 128, (k + 1) * 128)
        ref[:, :128] = turn_lanes(back[:, cols], mark, me % 2 == k, -1.0).astype(BF)
        ref[:, 128:] = grad_values[:, cols].astype(BF)


def feed_kernel(units, blocks, normed, c0, c1, c2, c3, mine, other, shifts, near, peer,
                act, grad, act_turned, grad_turned, expand, shrink, sums, pushes, push_sums, tile, turned):
    i = pl.program_id(0)

    @pl.when(i == 0)
    def _():
        sums[...] = jnp.zeros_like(sums)
        push_sums[...] = jnp.zeros_like(push_sums)
        turned[:, :128] = near[...].T
        turned[:, 128:] = peer[...].T
        for source in range(blocks):
            cols = slice(source * 128, (source + 1) * 128)
            for at, ref in ((0, mine), (units, other)):
                expand[at : at + units, cols] = ref[source, :units, :]
                shrink[at : at + units, cols] = ref[source, units:, :]

    pick(i, (c0, c1, c2, c3), tile)
    pushes[...] = nn(tile[...], turned[...]).astype(BF)
    expanded = nt(normed[...], expand[...]) + shifts[1:2, : 2 * units]
    activated, bend = gelu_and_slope(expanded)
    activated = activated.astype(BF)
    act[...] = activated
    act_turned[...] = activated.T
    slope = (bend * nt(tile[...], shrink[...])).astype(BF)
    grad[...] = slope
    grad_turned[...] = slope.T
    sums[0:1, :] += jnp.sum(slope.astype(F32), axis=0, keepdims=True)
    push_sums[0:1, :] += jnp.sum(tile[...].astype(F32), axis=0, keepdims=True)


def by_quarter(left, quarters):
    size = quarters[0].shape[0]
    total = nn(left[:, :size], quarters[0][...])
    for k in range(1, len(quarters)):
        total = total + nn(left[:, k * size : (k + 1) * size], quarters[k][...])
    return total


def outer_kernel(units, grad_turned, act_turned, normed, c0, c1, c2, c3, *rest):
    out = rest[-1]
    for k in (0, 1):
        result = by_quarter(act_turned, (c0, c1, c2, c3)) if k else nn(grad_turned[...], normed[...])
        for b in range(WIDE // 128):
            lanes = slice(b * 128, (b + 1) * 128)
            rows = slice(k * units, (k + 1) * units)
            part = result[:, lanes]
            if len(rest) > 1:
                part = part + rest[0][b, rows, :].astype(F32)
            out[b, rows, :] = part.astype(BF)


def branch_kernel(r, act, attended, shrink, near, peer, o0, o1, o2, o3):
    outs = (o0, o1, o2, o3)
    size = r.count // 4
    extra = nn(attended[:, :128], near[...]) + nn(attended[:, 128:], peer[...])
    for k in range(4):
        result = nn(act[k * size : (k + 1) * size, :], shrink[...])
        covered = False
        for row, place, length in r.x_rows(0):
            if row == k * size:
                outs[k][:length, :] = (result[:length] + extra[place : place + length]).astype(BF)
                if length < size:
                    outs[k][length:, :] = result[length:].astype(BF)
                covered = True
        if not covered:
            outs[k][...] = result.astype(BF)


def inputs_kernel(r, keep1, keep2, got1, got2, grad, t0, t1, t2, t3, stats, triple, expand, gains, cotangent_sums, unit_sums,
                  o0, o1, o2, o3, linear, near, sums, line_sums):
    j = pl.program_id(0)
    size = r.count // 4

    @pl.when(j == 0)
    def _():
        for x, one, two in ((0, keep1, keep2), (1, got1, got2)):
            for row, place, length in r.x_rows(x):
                linear[row : row + length, :128] = one[place : place + length, :128]
                linear[row : row + length, 128:] = two[place : place + length, :]
                near[row : row + length, :] = one[place : place + length, 128:]
        line_sums[...] = jnp.zeros_like(line_sums)
        line_sums[0:1, :384] = jnp.sum(linear[...].astype(F32), axis=0, keepdims=True)

    sums[...] = jnp.zeros_like(sums)
    for k, (ref, tokens) in enumerate(((o0, t0), (o1, t1), (o2, t2), (o3, t3))):
        rows = slice(k * size, (k + 1) * size)
        attend = nt(linear[rows, :], triple[...])
        feed = nn(grad[rows, :], expand[...])
        value = normal_of(tokens[...], stats[rows, :])
        sums[0:1, :] += jnp.sum(value * attend, axis=0, keepdims=True)
        sums[1:2, :] += jnp.sum(value * feed, axis=0, keepdims=True)
        sums[2:3, :] += jnp.sum(attend, axis=0, keepdims=True)
        sums[3:4, :] += jnp.sum(feed, axis=0, keepdims=True)
        ref[...] = (gains[0:1, :] * attend + gains[1:2, :] * feed).astype(BF)
    sums[4:5, :] = cotangent_sums[0:1, :]
    for k in (0, 1):

        @pl.when(j == k)
        def _(k=k):
            sums[5:6, :] = line_sums[0:1, k * WIDE : (k + 1) * WIDE]
            sums[6:7, :] = unit_sums[0:1, k * WIDE : (k + 1) * WIDE]


def small_kernel(blocks, units, ids, mine, other, out, lines):
    me, core = ids[0], ids[1]
    width = lines.shape[1]
    heads, lanes = blocks // 2, 128 // blocks
    lines[...] = jnp.zeros_like(lines)
    lines[0:5, :] = mine[0:5, :] + other[0:5, :]
    ours = jnp.where(me // heads == core, 1.0, 0.0)
    for s in range(3):
        at = pl.multiple_of((me % heads + s % 2 * heads) * 128, 128)
        cols = slice(s * 128, (s + 1) * 128)
        lines[6 + s // 2 : 7 + s // 2, pl.ds(at, 128)] = (mine[5:6, cols] + other[5:6, cols]) * ours
    at = pl.multiple_of(me % heads * units, units)
    total = mine[6:7, :units] + other[6:7, units : 2 * units]
    for k in (0, 1):

        @pl.when(me // heads == k)
        def _(k=k):
            lines[8 + k : 9 + k, pl.ds(at, units)] = total

    row = lax.broadcasted_iota(jnp.int32, (width, 128), 0)
    lane = lane_of((width, 128))
    deal = ((lane // lanes == row // 128) & (lane % lanes == row % lanes)).astype(BF)
    value = lines[...]
    high = value.astype(BF)
    low = (value - high.astype(F32)).astype(BF)
    lane = lane_of((16, width)) % 128 // lanes
    line = lax.broadcasted_iota(jnp.int32, (16, width), 0)
    for b in range(blocks):
        sent = (lane == b) & ((line != 4) | (me == b))
        for k, part in enumerate((high, low)):
            part = jnp.where(sent, part.astype(F32), 0.0).astype(BF)
            out[b, k * 16 : (k + 1) * 16, :] = nn(part, deal).astype(BF)


def fold_kernel(keep1, got1, keep2, got2, one, one_send, two, two_send):
    for keep, got, outs in ((keep1, got1, (one, one_send)), (keep2, got2, (two, two_send))):
        half = outs[0].shape[0]
        for k, out in enumerate(outs):
            rows = slice(k * half, (k + 1) * half)
            out[...] = (keep[rows, :].astype(F32) + got[rows, :].astype(F32)).astype(BF)


def by_z_kernel(chunk, one, one_got, two, two_got, *outs):
    for half, (mine, got) in enumerate(((one, one_got), (two, two_got))):
        for z, out in enumerate(outs):
            rows = slice(z * chunk, (z + 1) * chunk)
            value = mine[rows, :].astype(F32) + got[rows, :].astype(F32)
            out[half * chunk : (half + 1) * chunk, :] = value.astype(BF)


def line_outer_kernel(cut, ids, linear, near, t0, t1, t2, t3, stats, norms, c0, c1, c2, c3,
                      keep, give, turned, near_turned, normed, result):
    core = ids[1]

    @pl.when(pl.program_id(0) == 0)
    def _():
        turned[...] = linear[...].T
        near_turned[...] = near[...].T

    size = t0.shape[0]
    for k, tokens in enumerate((t0, t1, t2, t3)):
        rows = slice(k * size, (k + 1) * size)
        value = normal_of(tokens[...], stats[rows, :])
        normed[rows, :] = (value * norms[0:1, :] + norms[2:3, :]).astype(BF)
    result[:384, :] = nn(turned[...], normed[...])
    result[384:, :] = by_quarter(near_turned, (c0, c1, c2, c3))
    for who, out in ((core, keep), (1 - core, give)):
        for s in range(4):
            at = pl.multiple_of(s * 2 * cut + who * cut, cut)
            for b in range(WIDE // 128):
                part = result[pl.ds(at, cut), b * 128 : (b + 1) * 128]
                out[b, s * cut : (s + 1) * cut, :] = part.astype(out.dtype)


def unpack_kernel(cut, heads, ids, mine, other, whole, triple, outward, small, pair):
    core = ids[1]
    for k in range(heads):
        for s in range(4):
            for who, ref in ((core, mine), (1 - core, other)):
                pair[pl.ds(pl.multiple_of(who * cut, cut), cut), :] = ref[k, s * cut : (s + 1) * cut, :].astype(F32)
            if s < 3:
                triple[s, :, k * 128 : (k + 1) * 128] = pair[...].T
            else:
                outward[k * 128 : (k + 1) * 128, :] = pair[...]
    total = jnp.zeros(small.shape, F32)
    for b in range(2 * heads):
        for k in (0, 1):
            at = 4 * cut + 16 * k
            total = total + whole[b, at : at + 16, :].astype(F32)
    small[...] = total


def feed_unpack_kernel(units, got, expand, shrink):
    for k in range(got.shape[0]):
        rows = slice(k * units, (k + 1) * units)
        expand[:, rows] = got[k, :units, :].astype(F32).T
        shrink[rows, :] = got[k, units:, :].astype(F32)


def join(*values):
    return lax.optimization_barrier(values)


def body(
    tokens,
    w_qkv,
    b_qkv,
    w_out,
    b_out,
    w_in,
    b_in,
    w_out2,
    b_out2,
    norm_gain,
    norm_shift,
    doc_start,
    live,
    cotangent,
):
    blocks = lax.axis_size("blk")
    cores = lax.axis_size("tp")
    me, core = lax.axis_index("blk"), lax.axis_index("tp")
    ids = jnp.stack([me, core]).astype(jnp.int32)
    rows, width = tokens.shape
    depth = w_in.shape[0]
    r = Rows(blocks, cores, rows)
    part, count, share = r.part, r.count, r.share
    quarter = count // 4
    units = w_in.shape[1] // blocks
    cut = depth // cores
    own_heads = HEADS // cores * 2
    scale = 1.0 / math.sqrt(HEAD)
    masks_z = [4 * i for i in range(1, blocks // 4)]
    grid = (width // WIDE,)

    once = pl.Buffered(1)

    def tiled(columns):
        return pl.BlockSpec((quarter, columns), lambda i: (i, 0))

    def across(lines):
        return pl.BlockSpec((lines, WIDE), lambda j: (0, j))

    def fixed(value):
        return pl.BlockSpec(value.shape, lambda i: (0,) * value.ndim, pipeline_mode=once)

    def fixed_shape(*shape):
        return pl.BlockSpec(shape, lambda i: (0,) * len(shape))

    def packed_rows(value, lines):
        flat = value.reshape(-1)
        return jnp.pad(flat, (0, lines * 128 - flat.size)).reshape(lines, 128)

    small = jnp.concatenate(
        [
            packed_rows(norm_gain, 2),
            packed_rows(norm_shift, 2),
            packed_rows(b_out, 1),
            packed_rows(b_out2, 1),
            packed_rows(b_qkv, 2),
            packed_rows(b_in, 2),
            jnp.stack([doc_start // 256, doc_start % 256, live]).astype(BF),
            jnp.zeros((3, 128), BF),
        ]
    )

    def over_z(value):
        return [from_peer(value, mask) for mask in masks_z]

    def halves(pieces):
        one = jnp.concatenate([value[: r.chunk] for value in pieces])
        two = jnp.concatenate([value[r.chunk :] for value in pieces])
        return one, two

    my_tokens = lax.dynamic_slice_in_dim(tokens, core * part, part, 0)
    my_cotangent = lax.dynamic_slice_in_dim(cotangent, core * part, part, 0)
    triple = w_qkv.reshape(3, cores, cut, own_heads, 128).transpose(1, 3, 0, 2, 4)
    triple = triple.reshape(cores, own_heads, 3 * cut, 128)
    outward = w_out.reshape(own_heads, cores, cut, 128).transpose(1, 0, 2, 3)
    dealt = jnp.concatenate([triple, outward], axis=2)
    keep = lax.dynamic_index_in_dim(dealt, core, 0, keepdims=False)
    give = lax.dynamic_index_in_dim(dealt, 1 - core, 0, keepdims=False)
    feed_deal = run_kernel(
        lambda *refs: feed_deal_kernel(blocks, units, *refs),
        [((blocks, 2 * units, depth), BF)],
        ins=[VMEM, VMEM],
        name="feed_deal",
        moved=4e6,
    )(w_in, w_out2)
    tokens_z = join(my_tokens, *over_z(my_tokens))
    keep, got, feed_deal, my_cotangent, *tokens_z = join(keep, swap_cores(give), feed_deal, my_cotangent, *tokens_z)

    heads_low, heads_high = by_core(core, keep, got)
    deal = jnp.concatenate(
        [
            jnp.concatenate([heads_low, heads_high]),
            jnp.broadcast_to(small, (blocks,) + small.shape),
        ],
        axis=1,
    )
    here = lax.all_to_all(deal, "blk", 0, 0, tiled=True)
    one, two = halves(tokens_z)
    cotangent_z = over_z(my_cotangent)
    one, one_y, two, two_x = join(one, from_peer(one, 2), two, from_peer(two, 1))

    one, two = jnp.concatenate([one, one_y]), jnp.concatenate([two, two_x])
    mine_one, mine_two = halves(join(my_cotangent, *cotangent_z))
    here, feed_deal, one, one_x, two, two_y, mine_one, mine_y, mine_two, mine_x = join(
        here,
        feed_deal,
        one,
        from_peer(one, 1),
        two,
        from_peer(two, 2),
        mine_one,
        from_peer(mine_one, 2),
        mine_two,
        from_peer(mine_two, 1),
    )
    all_tokens = [one, one_x, two, two_y]

    one, two = jnp.concatenate([mine_one, mine_y]), jnp.concatenate([mine_two, mine_x])
    here, there, feed_deal = join(here, swap_cores(here), feed_deal)
    feed_mine = lax.all_to_all(feed_deal, "blk", 0, 0, tiled=True)
    steps = jnp.arange(ROT // 2, dtype=F32)
    speed = jnp.tile(10000.0 ** (-2.0 * steps / ROT), 4).reshape(1, 128)
    w_triple, w_near, marks, norms, shifts = run_kernel(
        lambda *refs: deal_kernel(cut, blocks, *refs),
        [
            ((width, 384), BF),
            ((128, width), BF),
            ((blocks * rows, 128), F32),
            ((8, width), F32),
            ((8, 512), F32),
        ],
        ins=[SMEM, VMEM, VMEM, VMEM],
        scratch=[pltpu.VMEM((2, 16, width), F32), pltpu.VMEM((128, 128), F32)],
        name="deal",
        moved=8e6,
    )(ids, speed, here, there)
    normed_feed, stats, mine = run_kernel(
        lambda *refs: norm_kernel(r, *refs),
        [((count, width), BF), ((count, 128), F32), ((count, 384), BF)],
        grid=(4,),
        ins=[SMEM] + [fixed(t) for t in all_tokens] + [fixed(norms), fixed(w_triple), fixed(shifts), fixed(marks)],
        out_specs=[tiled(width), tiled(128), tiled(384)],
        scratch=[pltpu.VMEM((quarter, width), BF), pltpu.VMEM((quarter, 128), F32), pltpu.VMEM((quarter, width), BF)],
        flops=2 * count * width * 384,
        name="norm",
        moved=22e6,
    )(ids, *all_tokens, norms, w_triple, shifts, marks)
    w_peer = from_peer(w_near, 1)
    mine, one, one_x, two, two_y = join(mine, one, from_peer(one, 1), two, from_peer(two, 2))

    peer, mine_there = from_peer(mine, 1), swap_cores(mine)
    all_cotangent = [one, one_x, two, two_y]
    feed_mine, *all_cotangent = join(feed_mine, *all_cotangent)

    feed_mine, feed_other = join(feed_mine, swap_cores(feed_mine))

    turned = pl.BlockSpec((2 * units, quarter), lambda i: (0, i))
    act, grad, act_turned, grad_turned, w_expand, w_shrink, unit_sums, grads, cotangent_sums = run_kernel(
        lambda *refs: feed_kernel(units, blocks, *refs),
        [((count, 2 * units), BF)] * 2
        + [((2 * units, count), BF)] * 2
        + [((2 * units, width), BF)] * 2
        + [((8, 2 * units), F32), ((count, 256), BF), ((8, width), F32)],
        grid=(4,),
        ins=[tiled(width)]
        + [fixed(t) for t in all_cotangent]
        + [fixed(feed_mine), fixed(feed_mine), fixed(shifts), fixed(w_near), fixed(w_peer)],
        out_specs=[tiled(2 * units)] * 2
        + [turned] * 2
        + [fixed_shape(2 * units, width)] * 2
        + [fixed_shape(8, 2 * units), tiled(256), fixed_shape(8, width)],
        scratch=[pltpu.VMEM((quarter, width), BF), pltpu.VMEM((width, 256), BF)],
        flops=8 * count * width * units,
        name="feed",
        moved=20e6,
    )(normed_feed, *all_cotangent, feed_mine, feed_other, shifts, w_near, w_peer)
    mine, peer, mine_there, act_turned, grad_turned = join(mine, peer, mine_there, act_turned, grad_turned)

    dealt_spec = pl.BlockSpec((WIDE // 128, 2 * units, 128), lambda j: (j, 0, 0))

    def outer(half, *extra):
        some = pl.BlockSpec((units, count), lambda j: (half, 0))
        return run_kernel(
            lambda *refs: outer_kernel(units, *refs),
            [((blocks, 2 * units, 128), BF)],
            grid=grid,
            ins=[some, some, across(count)] + [across(quarter)] * 4 + [dealt_spec] * len(extra),
            out_specs=[dealt_spec],
            flops=4 * count * width * units,
            name="outer",
            moved=12e6,
        )(grad_turned, act_turned, normed_feed, *all_cotangent, *extra)

    peer_there, feed_sent, grads = join(swap_cores(peer), outer(1), grads)

    tile = share // 2
    half_tile = lambda columns: pl.BlockSpec((tile, columns), lambda i: (i, 0))
    line_tile = pl.BlockSpec((8, tile), lambda i: (0, i))
    four = [mine, peer, mine_there, peer_there]
    common = [
        pltpu.VMEM((2 * count, 256), BF),
        pltpu.VMEM((2 * count, 256), BF),
        pltpu.VMEM((share, 256), BF),
        pltpu.VMEM((share, 256), BF),
        pltpu.VMEM((2 * count, 128), F32),
        pltpu.VMEM((8, 2 * count), F32),
        pltpu.VMEM((share, 128), F32),
    ]
    attended, keep1, send1, lines = run_kernel(
        lambda *refs: query_kernel(r, scale, *refs),
        [((share, 256), BF)] * 3 + [((8, share), F32)],
        grid=(2,),
        ins=[SMEM] + [fixed(mine)] * 4 + [fixed(grads), fixed(marks)],
        out_specs=[half_tile(256)] * 3 + [line_tile],
        scratch=common,
        flops=8 * share * 2 * count * 256,
        name="query",
        moved=6e6,
    )(ids, *four, grads, marks)
    grads_there, attended, send1, lines = join(swap_cores(grads), attended, send1, lines)
    feed_got = swap_cores(feed_sent)

    diagonal = [(2 * b + c, 2 * (b ^ 1) + 1 - c) for b in range(blocks) for c in (0, 1)]
    lines_peer, lines_there = from_peer(lines, 1), swap_cores(lines)
    lines_far = lax.ppermute(lines, ("blk", "tp"), diagonal)
    feed_grads = outer(0, feed_got)
    feed_grads, lines, lines_peer, lines_there, lines_far = join(feed_grads, lines, lines_peer, lines_there, lines_far)

    keep2, send2 = run_kernel(
        lambda *refs: key_kernel(r, scale, *refs),
        [((share, 256), BF)] * 2,
        grid=(2,),
        ins=[SMEM] + [fixed(mine)] * 4 + [fixed(grads)] * 2 + [fixed(lines)] * 4 + [fixed(marks)],
        out_specs=[half_tile(256)] * 2,
        scratch=common + [pltpu.VMEM((8, 2 * count), F32)],
        flops=8 * share * 2 * count * 256,
        name="key",
        moved=6e6,
    )(ids, *four, grads, grads_there, lines, lines_peer, lines_there, lines_far, marks)
    feed_grads, attended = join(feed_grads, attended)
    feed_dealt = lax.all_to_all(feed_grads, "blk", 0, 0, tiled=True)
    branches = run_kernel(
        lambda *refs: branch_kernel(r, *refs),
        [((quarter, width), BF)] * 4,
        grid=grid,
        ins=[fixed(act), fixed(attended), across(2 * units), across(128), across(128)],
        out_specs=[across(quarter)] * 4,
        flops=2 * count * width * (2 * units + 128),
        name="branch",
        moved=9e6,
    )(act, attended, w_shrink, w_near, w_peer)
    got1, got2, *branches = join(from_peer(send1, 1), from_peer(send2, 1), *branches)
    mixed_one, mixed_two = from_peer(branches[1], 1), from_peer(branches[3], 2)

    def fold(*refs):
        return run_kernel(
            fold_kernel,
            [((quarter // 2, width), BF)] * 4,
            grid=grid,
            ins=[across(quarter)] * 4,
            out_specs=[across(quarter // 2)] * 4,
            name="fold",
            moved=6e6,
        )(*refs)

    def by_z(*refs):
        return run_kernel(
            lambda *refs: by_z_kernel(r.chunk, *refs),
            [((part, width), BF)] * (1 + len(masks_z)),
            grid=grid,
            ins=[across(quarter // 2)] * 4,
            out_specs=[across(part)] * (1 + len(masks_z)),
            name="by_z",
            moved=3e6,
        )(*refs)

    def total(pieces, got):
        value = pieces[0].astype(F32)
        for piece in got:
            value = value + piece.astype(F32)
        return value

    def pieces_over_z(pieces):
        return [from_peer(piece, mask) for piece, mask in zip(pieces[1:], masks_z)]

    *combined, grad_linear, attended_near, sums, _ = run_kernel(
        lambda *refs: inputs_kernel(r, *refs),
        [((quarter, width), BF)] * 4 + [((count, 384), BF), ((count, 128), BF), ((8, width), F32), ((8, 512), F32)],
        grid=grid,
        ins=[fixed(keep1)] * 4
        + [fixed(grad)]
        + [across(quarter)] * 4
        + [fixed(stats), pl.BlockSpec((WIDE, 384), lambda j: (j, 0)), across(2 * units)]
        + [across(8), across(8), fixed(unit_sums)],
        out_specs=[across(quarter)] * 4
        + [fixed_shape(count, 384), fixed_shape(count, 128), across(8), fixed_shape(8, 512)],
        flops=2 * count * width * (384 + 2 * units),
        name="inputs",
        moved=16e6,
    )(keep1, keep2, got1, got2, grad, *all_tokens, stats, w_triple, w_expand, norms, cotangent_sums, unit_sums)
    grad_linear, sums, *combined = join(grad_linear, sums, *combined)

    got_one, got_two = from_peer(combined[1], 1), from_peer(combined[3], 2)
    line_spec = pl.BlockSpec((WIDE // 128, 4 * cut, 128), lambda j: (j, 0, 0))
    keep, give = run_kernel(
        lambda *refs: line_outer_kernel(cut, *refs),
        [((blocks, 4 * cut, 128), F32), ((blocks, 4 * cut, 128), BF)],
        grid=grid,
        ins=[SMEM, fixed(grad_linear), fixed(attended_near)]
        + [across(quarter)] * 4
        + [fixed(stats), across(8)]
        + [across(quarter)] * 4,
        out_specs=[line_spec] * 2,
        scratch=[
            pltpu.VMEM((384, count), BF),
            pltpu.VMEM((128, count), BF),
            pltpu.VMEM((count, WIDE), BF),
            pltpu.VMEM((512, WIDE), F32),
        ],
        flops=2 * count * width * 512,
        name="line_outer",
        moved=12e6,
    )(ids, grad_linear, attended_near, *all_tokens, stats, norms, *all_cotangent)
    mixed_one, mixed_two, keep, give, sums, sums_other = join(
        mixed_one, mixed_two, keep, give, sums, swap_cores(sums)
    )

    one, one_send, two, two_send = fold(branches[0], mixed_one, branches[2], mixed_two)
    small = run_kernel(
        lambda *refs: small_kernel(blocks, units, *refs),
        [((blocks, 32, 128), BF)],
        ins=[SMEM, VMEM, VMEM],
        scratch=[pltpu.VMEM((16, width), F32)],
        name="small",
        moved=1e6,
    )(ids, sums, sums_other)
    got, small, one, one_send, two, two_send = join(swap_cores(give), small, one, one_send, two, two_send)
    mixed_one, mixed_two = from_peer(one_send, 2), from_peer(two_send, 1)
    dealt = jnp.concatenate([(keep + got.astype(F32)).astype(BF), small], axis=1)
    dealt, feed_dealt = join(dealt, feed_dealt)
    dealt = lax.all_to_all(dealt, "blk", 0, 0, tiled=True)
    expand_grad, shrink_grad = run_kernel(
        lambda *refs: feed_unpack_kernel(units, *refs),
        [(w_in.shape, F32), (w_out2.shape, F32)],
        grid=(4,),
        ins=[pl.BlockSpec((blocks // 4, 2 * units, 128), lambda k: (k, 0, 0))],
        out_specs=[
            pl.BlockSpec((depth, units * blocks // 4), lambda k: (0, k)),
            pl.BlockSpec((units * blocks // 4, depth), lambda k: (k, 0)),
        ],
        name="feed_unpack",
        moved=6e6,
    )(feed_dealt)
    got_one, got_two, mixed_one, mixed_two, expand_grad, shrink_grad = join(
        got_one, got_two, mixed_one, mixed_two, expand_grad, shrink_grad
    )
    mixed_pieces = by_z(one, mixed_one, two, mixed_two)
    one, one_send, two, two_send, *mixed_pieces = join(
        *fold(combined[0], got_one, combined[2], got_two), *mixed_pieces
    )
    mixed_got = pieces_over_z(mixed_pieces)
    got_one, got_two = join(from_peer(one_send, 2), from_peer(two_send, 1))

    joined = join(*by_z(one, got_one, two, got_two), *mixed_got)
    pieces, mixed_got = joined[: 1 + len(masks_z)], joined[1 + len(masks_z) :]
    combined_got = pieces_over_z(pieces)

    def whole_block(value):
        return jnp.concatenate(by_core(core, value, swap_cores(value)))

    my_inputs = my_tokens.astype(F32)
    mixed = whole_block((my_inputs + total(mixed_pieces, mixed_got) + norms[4:5, :]).astype(BF))
    dealt, mixed = join(dealt, mixed)
    keep = lax.dynamic_slice_in_dim(dealt, core * own_heads, own_heads, 0)
    give = lax.dynamic_slice_in_dim(dealt, (1 - core) * own_heads, own_heads, 0)
    triple_grad, output_grad, small = run_kernel(
        lambda *refs: unpack_kernel(cut, own_heads, *refs),
        [((3, depth, own_heads * 128), F32), ((own_heads * 128, depth), F32), ((16, 128), F32)],
        ins=[SMEM, VMEM, VMEM, VMEM],
        scratch=[pltpu.VMEM((128, 128), F32)],
        name="unpack",
        moved=4e6,
    )(ids, keep, swap_cores(give), dealt)
    small = small.reshape(16, 16, -1)
    residual_grad = small[4]
    small, triple_grad, output_grad, *combined_got = join(small, triple_grad, output_grad, *combined_got)

    combined_sum = total(pieces, combined_got)
    my_center = my_inputs - jnp.mean(my_inputs, axis=-1, keepdims=True)
    my_inverse = lax.rsqrt(jnp.mean(my_center * my_center, axis=-1, keepdims=True) + EPSILON)
    my_normal = my_center * my_inverse
    my_grad = my_inverse * (
        combined_sum
        - jnp.mean(combined_sum, axis=-1, keepdims=True)
        - my_normal * jnp.mean(combined_sum * my_normal, axis=-1, keepdims=True)
    )
    tokens_grad = whole_block((my_cotangent.astype(F32) + my_grad).astype(BF))
    return (
        mixed,
        tokens_grad,
        triple_grad,
        small[6:8].reshape(32, -1)[:24].reshape(b_qkv.shape),
        output_grad,
        residual_grad,
        expand_grad,
        small[8:10].reshape(b_in.shape),
        shrink_grad,
        residual_grad,
        small[0:2],
        small[2:4],
    )


def solution(mesh):
    placed = (
        P("blk", None),
        P(None, "blk", "tp"),
        P(None, "tp", "blk"),
        P("tp", "blk"),
        P(None, "blk"),
        P("blk", "tp"),
        P("tp", "blk"),
        P("tp", "blk"),
        P(None, "blk"),
        P(None, None, "blk"),
        P(None, None, "blk"),
        P("blk"),
        P("blk"),
        P("blk", None),
    )
    two_to_a_head = mesh.shape["blk"] == 2 * HEADS
    return jax.shard_map(
        body if two_to_a_head else general_body,
        mesh=mesh,
        in_specs=placed,
        out_specs=(
            P("blk", None),
            P("blk", None),
            P(None, "blk", "tp"),
            P(None, "tp", "blk"),
            P("tp", "blk"),
            P(None, "blk"),
            P("blk", "tp"),
            P("tp", "blk"),
            P("tp", "blk"),
            P(None, "blk"),
            P(None, None, "blk"),
            P(None, None, "blk"),
        ),
        check_vma=False,
    )
```

```python
import math

import jax
import jax.numpy as jnp
from jax import lax
from jax.experimental import pallas as pl
from jax.experimental.pallas import tpu as pltpu
from jax.sharding import PartitionSpec as P

HEADS = 8
HEAD = 256
ROT = 64

EPSILON = 1e-05
NEGATIVE = -1e30
BF = jnp.bfloat16
F32 = jnp.float32


def dot(left, right, dims):
    return lax.dot_general(left, right, (dims, ((), ())), preferred_element_type=F32)


def swap_cores(value):
    return lax.ppermute(value, "tp", [(0, 1), (1, 0)])


def from_peer(value, mask):
    count = lax.axis_size("blk")
    return lax.ppermute(value, "blk", [(i, i ^ mask) for i in range(count)])


def spread(value, masks):
    return jnp.stack([value] + [from_peer(value, mask) for mask in masks])


def collect(parts, masks):
    total = parts[0].astype(F32)
    for at, mask in enumerate(masks):
        total = total + from_peer(parts[at + 1], mask).astype(F32)
    return total


def by_core(core, mine, other):
    first = core == 0
    return jnp.where(first, mine, other), jnp.where(first, other, mine)


def gelu_and_slope(values):
    cumulative = 0.5 * (1.0 + lax.erf(values * (1.0 / math.sqrt(2.0))))
    density = jnp.exp(-0.5 * values * values) * (1.0 / math.sqrt(2.0 * math.pi))
    return values * cumulative, cumulative + values * density


def turn(values, cosine, sine):
    half = ROT // 2
    first, second = values[:, :half], values[:, half:ROT]
    return jnp.concatenate(
        [first * cosine - second * sine, second * cosine + first * sine, values[:, ROT:]],
        axis=1,
    )


def general_body(
    tokens,
    w_qkv,
    b_qkv,
    w_out,
    b_out,
    w_in,
    b_in,
    w_out2,
    b_out2,
    norm_gain,
    norm_shift,
    doc_start,
    live,
    cotangent,
):
    blocks = lax.axis_size("blk")
    cores = lax.axis_size("tp")
    me, core = lax.axis_index("blk"), lax.axis_index("tp")
    rows, width = tokens.shape
    depth = w_in.shape[0]
    part = rows // cores
    quarter = part // 2
    group = blocks // HEADS
    columns = HEAD // group
    units = w_in.shape[1] // blocks
    cut = depth // cores
    near = columns // cores
    scale = 1.0 / math.sqrt(HEAD)

    masks_x = list(range(1, group))
    masks_y = [group]
    masks_z = [2 * group * i for i in range(1, blocks // (2 * group))]
    size_x, size_y, size_z = group, 2, len(masks_z) + 1

    def gather(value):
        over_z = spread(value, masks_z)
        one = spread(spread(over_z[:, :quarter], masks_y), masks_x)
        two = spread(spread(over_z[:, quarter:], masks_x), masks_y)
        return one.reshape(-1, value.shape[-1]), two.reshape(-1, value.shape[-1])

    def scatter(one, two):
        one = one.reshape(size_x, size_y, size_z, quarter, width)
        two = two.reshape(size_y, size_x, size_z, quarter, width)
        one = collect(collect(one, masks_x).astype(BF), masks_y)
        two = collect(collect(two, masks_y).astype(BF), masks_x)
        return collect(jnp.concatenate([one, two], axis=1).astype(BF), masks_z)

    small = jnp.concatenate(
        [
            norm_gain.reshape(-1),
            norm_shift.reshape(-1),
            b_out.reshape(-1),
            b_out2.reshape(-1),
            b_qkv.reshape(-1),
            b_in.reshape(-1),
            (doc_start // 256).astype(BF),
            (doc_start % 256).astype(BF),
            live.astype(BF),
        ]
    )
    small_rows = -(-small.size // 2048) * 16
    small = jnp.pad(small, (0, small_rows * 128 - small.size)).reshape(small_rows * 128 // columns, columns)
    lines = small.shape[0]

    own_heads = HEADS // cores * group
    triple = w_qkv.reshape(3, cores, cut, own_heads, columns).transpose(1, 3, 0, 2, 4)
    triple = triple.reshape(cores, own_heads, 3 * cut, columns)
    outward = w_out.reshape(own_heads, cores, near, depth).transpose(1, 0, 2, 3)
    outward = outward.reshape(cores, own_heads, near * depth // columns, columns)
    dealt = jnp.concatenate([triple, outward], axis=2)
    keep = lax.dynamic_index_in_dim(dealt, core, 0, keepdims=False)
    give = lax.dynamic_index_in_dim(dealt, 1 - core, 0, keepdims=False)
    got = swap_cores(give)
    heads_low, heads_high = by_core(core, keep, got)
    deal = jnp.concatenate(
        [
            jnp.concatenate([heads_low, heads_high]),
            jnp.broadcast_to(small, (blocks,) + small.shape),
        ],
        axis=1,
    )
    here = lax.all_to_all(deal, "blk", 0, 0, tiled=True)
    there = swap_cores(here)
    both = jnp.stack(by_core(core, here, there))

    expand_deal = w_in.reshape(depth, blocks, units).transpose(1, 0, 2)
    expand_mine = lax.all_to_all(expand_deal, "blk", 0, 0, tiled=True).reshape(width, units)
    expand_other = swap_cores(expand_mine)
    shrink_mine = lax.all_to_all(
        w_out2.reshape(blocks, units, depth), "blk", 0, 0, tiled=True
    )
    shrink_other = swap_cores(shrink_mine)
    w_expand = jnp.concatenate([expand_mine, expand_other], axis=1)
    w_shrink = jnp.concatenate([shrink_mine, shrink_other], axis=1)
    w_shrink = w_shrink.transpose(1, 0, 2).reshape(2 * units, width)

    my_tokens = lax.dynamic_slice_in_dim(tokens, core * part, part, 0)
    my_cotangent = lax.dynamic_slice_in_dim(cotangent, core * part, part, 0)
    all_tokens = jnp.concatenate(gather(my_tokens))
    all_cotangent = jnp.concatenate(gather(my_cotangent))
    count = all_tokens.shape[0]

    at = 3 * cut
    mid = at + near * depth // columns
    w_triple = both[:, :, :at].reshape(cores, blocks, 3, cut, columns)
    w_triple = w_triple.transpose(1, 0, 3, 2, 4).reshape(width, 3 * columns)
    w_near = both[:, :, at:mid].reshape(cores, blocks, near, depth)
    w_near = w_near.transpose(0, 2, 1, 3).reshape(columns, width)
    w_head = spread(w_near, masks_x).reshape(HEAD, width)
    flat = both[:, :, mid:].reshape(cores, blocks, -1)

    def take(offset, like):
        return flat[:, :, offset : offset + like.size].reshape((cores, blocks) + like.shape), offset + like.size

    offset = 0
    gain_all, offset = take(offset, norm_gain)
    shift_all, offset = take(offset, norm_shift)
    out_all, offset = take(offset, b_out)
    out2_all, offset = take(offset, b_out2)
    triple_all, offset = take(offset, b_qkv)
    expand_all, offset = take(offset, b_in)
    start_high, offset = take(offset, doc_start)
    start_low, offset = take(offset, doc_start)
    live_all, offset = take(offset, live)
    gains = gain_all[0].transpose(1, 2, 0, 3).reshape(2, width).astype(F32)
    shifts = shift_all[0].transpose(1, 2, 0, 3).reshape(2, width).astype(F32)
    residual_shift = (out_all[0].astype(F32) + out2_all[0].astype(F32)).transpose(1, 0, 2).reshape(width)
    triple_shift = triple_all.astype(F32).transpose(2, 0, 3, 1, 4).reshape(3, width)
    triple_shift = lax.dynamic_slice_in_dim(triple_shift, me * columns, columns, 1).reshape(-1)
    expand_shift = expand_all.astype(F32).transpose(0, 2, 1, 3).reshape(cores, -1)
    expand_shift = lax.dynamic_slice_in_dim(expand_shift, me * units, units, 1)
    expand_shift = jnp.concatenate(by_core(core, expand_shift[0], expand_shift[1]))
    starts = (start_high[0].astype(F32) * 256.0 + start_low[0].astype(F32)).astype(jnp.int32)
    lives = live_all[0].astype(jnp.int32)

    x_at = jnp.arange(size_x)[:, None, None]
    y_at = group * jnp.arange(size_y)[None, :, None]
    z_at = 2 * group * jnp.arange(size_z)[None, None, :]
    order = (x_at + y_at + z_at) ^ me
    inside = jnp.arange(quarter, dtype=jnp.int32)

    def index_of(which):
        base = order[..., None] * rows + which * part + inside
        one, two = base, base + quarter
        return jnp.concatenate(
            [one.reshape(size_x, -1), two.reshape(size_x, -1)], axis=1
        )

    def heads_order(value):
        tail = value.shape[1:]
        one = value[: count // 2].reshape((size_x, -1) + tail)
        two = value[count // 2 :].reshape((size_y, size_x, -1) + tail)
        two = jnp.swapaxes(two, 0, 1).reshape((size_x, -1) + tail)
        return jnp.concatenate([one, two], axis=1)

    def gathered_order(value):
        tail = value.shape[2:]
        middle = value.shape[1] // 2
        one = value[:, :middle].reshape((count // 2,) + tail)
        two = value[:, middle:].reshape((size_x, size_y, -1) + tail)
        two = jnp.swapaxes(two, 0, 1).reshape((count // 2,) + tail)
        return jnp.concatenate([one, two])

    index_mine, index_other = index_of(core), index_of(1 - core)
    index = jnp.concatenate([index_mine.reshape(-1), index_other.reshape(-1)])
    token_start = starts.reshape(-1)[index]
    token_live = lives.reshape(-1)[index]

    inputs = all_tokens.astype(F32)
    center = inputs - jnp.mean(inputs, axis=-1, keepdims=True)
    inverse = lax.rsqrt(jnp.mean(center * center, axis=-1, keepdims=True) + EPSILON)
    normal = center * inverse
    normed_attend = (normal * gains[0] + shifts[0]).astype(BF)
    normed_feed = (normal * gains[1] + shifts[1]).astype(BF)

    linear = dot(normed_attend, w_triple, ((1,), (0,))) + triple_shift
    linear = heads_order(linear).reshape(count, 3, columns)
    steps = jnp.arange(ROT // 2, dtype=F32)
    speed = 10000.0 ** (-2.0 * steps / ROT)
    place = (index - token_start).astype(F32)
    angle = place[:count, None] * speed[None, :]
    cosine, sine = jnp.cos(angle), jnp.sin(angle)
    slot = me % group

    def turn_pieces(pieces, cosine, sine):
        if columns >= ROT:
            return jnp.stack(
                [
                    turn(
                        pieces[r],
                        jnp.where(slot == r, cosine, 1.0),
                        jnp.where(slot == r, sine, 0.0),
                    )
                    for r in range(group)
                ]
            )
        place_of = jnp.arange(group) ^ slot
        whole = jnp.swapaxes(pieces[place_of], 0, 1).reshape(pieces.shape[1], HEAD)
        whole = turn(whole, cosine, sine).reshape(-1, group, columns)
        return jnp.swapaxes(whole, 0, 1)[place_of]

    if columns >= ROT:
        own_cosine = jnp.where(slot == 0, cosine, 1.0)
        own_sine = jnp.where(slot == 0, sine, 0.0)
        queries = turn(linear[:, 0], own_cosine, own_sine)
        keys = turn(linear[:, 1], own_cosine, own_sine)
    else:
        queries, keys = linear[:, 0], linear[:, 1]
    mine = jnp.concatenate([queries, keys, linear[:, 2]], axis=1).astype(BF)

    def align(value, r):
        slabs = value.reshape((size_x, -1) + value.shape[1:])
        return jnp.stack([slabs[x ^ r] for x in range(size_x)]).reshape(value.shape)

    pieces = [mine] + [align(from_peer(mine, r), r) for r in masks_x]
    pieces = jnp.stack(pieces).reshape(group, count, 3, columns)
    if columns < ROT:
        turned = [turn_pieces(pieces[:, :, s].astype(F32), cosine, sine).astype(BF) for s in (0, 1)]
        pieces = jnp.stack(turned + [pieces[:, :, 2]], axis=2)
    own_triple = pieces.transpose(2, 1, 0, 3).reshape(3, count, HEAD)
    other_triple = swap_cores(own_triple)
    queries, keys, values = jnp.concatenate([own_triple, other_triple], axis=1)

    cotangent_x = heads_order(all_cotangent)
    grad_attended = dot(all_cotangent, w_head, ((1,), (1,))).astype(BF)
    grad_attended = heads_order(grad_attended).reshape(count, HEAD)
    grad_attended = jnp.concatenate([grad_attended, swap_cores(grad_attended)])

    share = count // size_x
    mine_index, mine_start, mine_live = index[:share], token_start[:share], token_live[:share]

    def allowed(query_index, query_start, key_index, key_start, key_live):
        same = query_start == key_start
        causal = key_index <= query_index
        usable = (key_live == 1) | (key_index == query_index)
        return same & causal & usable

    mask = allowed(mine_index[:, None], mine_start[:, None], index[None], token_start[None], token_live[None])
    scores = dot(queries[:share], keys, ((1,), (1,))) * scale
    masked = jnp.where(mask, scores, NEGATIVE)
    top = jnp.max(masked, axis=-1, keepdims=True)
    weight = jnp.where(mask, jnp.exp(masked - top), 0.0)
    total = jnp.sum(weight, axis=-1, keepdims=True)
    prob = weight / total
    attended = dot(prob.astype(BF), values, ((1,), (0,)))
    log_total = top + jnp.log(total)
    delta = jnp.sum(grad_attended[:share].astype(F32) * attended, axis=-1, keepdims=True)
    push = dot(grad_attended[:share], values, ((1,), (1,)))
    slope = (prob * (push - delta)).astype(BF)
    grad_queries = dot(slope, keys, ((1,), (0,))) * scale
    attended = attended.astype(BF)

    marks = jnp.concatenate([log_total, delta], axis=1).T
    marks = spread(marks, masks_x).transpose(1, 0, 2).reshape(2, count)
    marks = jnp.concatenate([marks, swap_cores(marks)], axis=1)
    mask = allowed(index[None], token_start[None], mine_index[:, None], mine_start[:, None], mine_live[:, None])
    scores = dot(keys[:share], queries, ((1,), (1,))) * scale
    prob = jnp.where(mask, jnp.exp(jnp.where(mask, scores, NEGATIVE) - marks[0][None]), 0.0)
    grad_values = dot(prob.astype(BF), grad_attended, ((1,), (0,)))
    push = dot(values[:share], grad_attended, ((1,), (1,)))
    slope = (prob * (push - marks[1][None])).astype(BF)
    grad_keys = dot(slope, queries, ((1,), (0,))) * scale

    expanded = dot(normed_feed, w_expand, ((1,), (0,))) + expand_shift
    activated, bend = gelu_and_slope(expanded)
    activated = activated.astype(BF)
    grad_activated = dot(all_cotangent, w_shrink, ((1,), (1,)))
    grad_expanded = (bend * grad_activated).astype(BF)

    branch = dot(activated, w_shrink, ((1,), (0,)))
    attend_part = dot(attended, w_head, ((1,), (0,)))
    rest = jnp.zeros((size_x - 1,) + attend_part.shape, F32)
    attend_part = gathered_order(jnp.concatenate([attend_part[None], rest]))
    branch = (branch + attend_part).astype(BF)
    branch = scatter(branch[: count // 2], branch[count // 2 :])
    my_inputs = my_tokens.astype(F32)
    my_mixed = (my_inputs + branch.reshape(part, width) + residual_shift).astype(BF)

    def whole_block(value):
        low, high = by_core(core, value, swap_cores(value))
        return jnp.concatenate([low, high])

    mixed = whole_block(my_mixed)

    grad_shrink = dot(activated, all_cotangent, ((0,), (0,)))
    grad_expand = dot(normed_feed, grad_expanded, ((0,), (0,)))
    grad_shrink = grad_shrink[:units] + swap_cores(grad_shrink[units:].astype(BF)).astype(F32)
    grad_expand = grad_expand[:, :units] + swap_cores(grad_expand[:, units:].astype(BF)).astype(F32)
    shrink_deal = grad_shrink.astype(BF).reshape(units, blocks, depth).transpose(1, 0, 2)
    expand_deal = grad_expand.astype(BF).reshape(blocks, depth, units)
    shrink_grad = lax.all_to_all(shrink_deal, "blk", 0, 0, tiled=True)
    shrink_grad = shrink_grad.reshape(-1, depth).astype(F32)
    expand_grad = lax.all_to_all(expand_deal, "blk", 0, 0, tiled=True)
    expand_grad = expand_grad.transpose(1, 0, 2).reshape(depth, -1).astype(F32)

    def by_pieces(value):
        return value.reshape(share, group, columns).transpose(1, 0, 2)

    own_cosine, own_sine = cosine[:share], -sine[:share]
    back = [
        turn_pieces(by_pieces(grad_queries), own_cosine, own_sine),
        turn_pieces(by_pieces(grad_keys), own_cosine, own_sine),
        by_pieces(grad_values),
    ]
    back = jnp.concatenate(back, axis=2).astype(BF)
    back = jnp.concatenate([back, by_pieces(attended)], axis=2)
    back = jnp.stack([back[0]] + [from_peer(back[r], r) for r in masks_x])
    back = gathered_order(back)
    grad_linear, attended_near = back[:, : 3 * columns], back[:, 3 * columns :]
    grad_triple = dot(normed_attend, grad_linear, ((0,), (0,)))
    grad_out = dot(attended_near, all_cotangent, ((0,), (0,)))
    grad_triple = grad_triple.reshape(blocks, cores, cut, 3, columns).transpose(1, 0, 3, 2, 4)
    grad_triple = grad_triple.reshape(cores, blocks, 3 * cut, columns)
    grad_out = grad_out.reshape(cores, near, blocks, depth).transpose(0, 2, 1, 3)
    grad_out = grad_out.reshape(cores, blocks, near * depth // columns, columns)
    dealt = jnp.concatenate([grad_triple, grad_out], axis=2)
    keep = lax.dynamic_index_in_dim(dealt, core, 0, keepdims=False)
    give = lax.dynamic_index_in_dim(dealt, 1 - core, 0, keepdims=False)
    dealt = (keep + swap_cores(give.astype(BF)).astype(F32)).astype(BF)
    dealt = lax.all_to_all(dealt, "blk", 0, 0, tiled=True)
    dealt = dealt.reshape((cores, own_heads) + dealt.shape[1:])
    keep = lax.dynamic_index_in_dim(dealt, core, 0, keepdims=False)
    give = lax.dynamic_index_in_dim(dealt, 1 - core, 0, keepdims=False)
    dealt = jnp.stack(by_core(core, keep, swap_cores(give)))
    triple_grad = dealt[:, :, :at].reshape(cores, own_heads, 3, cut, columns)
    triple_grad = triple_grad.transpose(2, 0, 3, 1, 4).reshape(3, depth, -1).astype(F32)
    output_grad = dealt[:, :, at:].reshape(cores, own_heads, near, depth)
    output_grad = output_grad.transpose(1, 0, 2, 3).reshape(-1, depth).astype(F32)

    grad_attend_norm = dot(grad_linear, w_triple, ((1,), (1,)))
    grad_feed_norm = dot(grad_expanded, w_expand, ((1,), (1,)))
    combined = (gains[0] * grad_attend_norm + gains[1] * grad_feed_norm).astype(BF)
    combined = scatter(combined[: count // 2], combined[count // 2 :]).reshape(part, width)
    my_center = my_inputs - jnp.mean(my_inputs, axis=-1, keepdims=True)
    my_inverse = lax.rsqrt(jnp.mean(my_center * my_center, axis=-1, keepdims=True) + EPSILON)
    my_normal = my_center * my_inverse
    my_grad = my_inverse * (
        combined
        - jnp.mean(combined, axis=-1, keepdims=True)
        - my_normal * jnp.mean(combined * my_normal, axis=-1, keepdims=True)
    )
    tokens_grad = whole_block((my_cotangent.astype(F32) + my_grad).astype(BF))

    sums = [
        jnp.sum(normal * grad_attend_norm, axis=0),
        jnp.sum(normal * grad_feed_norm, axis=0),
        jnp.sum(grad_attend_norm, axis=0),
        jnp.sum(grad_feed_norm, axis=0),
        jnp.sum(all_cotangent.astype(F32), axis=0),
        jnp.sum(grad_expanded.astype(F32), axis=0),
        jnp.sum(grad_linear.astype(F32), axis=0),
    ]
    sums = jnp.concatenate(sums)
    other = swap_cores(sums)
    added = sums + other
    norm_sums = added[: 4 * width].reshape(4, width // 128, blocks, -1).transpose(2, 0, 1, 3)
    residual_sum = added[4 * width : 5 * width].reshape(width // 128, 128)
    lanes = 128 // blocks
    residual_grad = lax.dynamic_slice_in_dim(residual_sum, me * lanes, lanes, 1)
    unit_sum = sums[5 * width : 5 * width + units] + other[5 * width + units : 5 * width + 2 * units]
    unit_sums = lax.dynamic_update_slice_in_dim(
        jnp.zeros((w_in.shape[1],), F32), unit_sum, me * units, 0
    )
    unit_sums = unit_sums.reshape(-1, blocks, lanes).transpose(1, 0, 2)
    line_sum = added[5 * width + 2 * units :].reshape(3, columns)
    line_sums = lax.dynamic_update_slice_in_dim(
        jnp.zeros((3, width), F32), line_sum, me * columns, 1
    )
    line_sums = lax.dynamic_slice_in_dim(line_sums, core * (width // cores), width // cores, 1)
    line_sums = line_sums.reshape(3, -1, blocks, lanes).transpose(2, 0, 1, 3)
    tiny = jnp.concatenate(
        [norm_sums.reshape(blocks, -1), unit_sums.reshape(blocks, -1), line_sums.reshape(blocks, -1)],
        axis=1,
    )
    tiny = jnp.sum(lax.all_to_all(tiny, "blk", 0, 0, tiled=True), axis=0)
    first = norm_gain.size
    gain_grad = tiny[:first].reshape(norm_gain.shape)
    shift_grad = tiny[first : 2 * first].reshape(norm_shift.shape)
    expand_bias_grad = tiny[2 * first : 2 * first + b_in.size].reshape(b_in.shape)
    triple_bias_grad = tiny[2 * first + b_in.size :].reshape(b_qkv.shape)
    return (
        mixed,
        tokens_grad,
        triple_grad,
        triple_bias_grad,
        output_grad,
        residual_grad,
        expand_grad,
        expand_bias_grad,
        shrink_grad,
        residual_grad,
        gain_grad,
        shift_grad,
    )


VMEM = pl.BlockSpec(memory_space=pltpu.VMEM)
SMEM = pl.BlockSpec(memory_space=pltpu.SMEM)
GRANT = 28 * 1024 * 1024
MARK_COS, MARK_SIN = 32, 64
WEIGHTS = {
    "deal": 10, "norm": 10, "feed": 10, "query": 10, "key": 3, "by_z": 3, "fold": 100, "small": 100, "inputs": 0.3, "feed_unpack": 30
}
WIDE = 256


def run_kernel(kernel, outs, grid=None, ins=None, out_specs=None, scratch=(), flops=0, moved=0, name=None):
    weight = WEIGHTS.get(name, 1)
    outs = [jax.ShapeDtypeStruct(shape, kind) for shape, kind in outs]
    single = len(outs) == 1
    out_specs = out_specs or [VMEM] * len(outs)
    extra = {} if grid is None else {"grid": grid}
    return pl.pallas_call(
        kernel,
        out_shape=outs[0] if single else outs,
        in_specs=ins,
        out_specs=out_specs[0] if single else out_specs,
        scratch_shapes=list(scratch),
        compiler_params=pltpu.CompilerParams(vmem_limit_bytes=GRANT),
        cost_estimate=pl.CostEstimate(flops=int(flops * weight), bytes_accessed=int(moved * weight), transcendentals=0),
        name=name,
        **extra,
    )


def chunk_bits(half, at, lanes):
    z = at % lanes
    low, high = (at // lanes) % 2, at // (2 * lanes)
    x, y = (high, low) if half == 0 else (low, high)
    return x + 2 * y + 4 * z


class Rows:
    def __init__(self, blocks, cores, rows):
        self.blocks, self.rows = blocks, rows
        self.part = rows // cores
        self.chunk = self.part // 2
        self.half = blocks * self.chunk
        self.count = 2 * self.half
        self.share = self.half
        self.sizes_z = blocks // 4

    def natural(self, me, core, half, at):
        block = me ^ chunk_bits(half, at, self.sizes_z)
        return block * self.rows + core * self.part + half * self.chunk

    def x_rows(self, x):
        h, q = self.half // 2, self.half // 4
        return [
            (x * h, 0, h),
            (self.half + x * q, h, q),
            (self.half + 2 * q + x * q, h + q, q),
        ]

    def pairs(self):
        mine, peer = self.x_rows(0), self.x_rows(1)
        both = [(a[0], b[0], a[2]) for a, b in zip(mine, peer)]
        return both + [(b, a, n) for a, b, n in both]


def nn(left, right):
    return lax.dot_general(left, right, (((1,), (0,)), ((), ())), preferred_element_type=F32)


def nt(left, right):
    return lax.dot_general(left, right, (((1,), (1,)), ((), ())), preferred_element_type=F32)


def lane_of(shape):
    return lax.broadcasted_iota(jnp.int32, shape, len(shape) - 1)


def turn_lanes(values, table, active, sign):
    lane = lane_of(values.shape)
    first, second = lane < ROT // 2, lane < ROT
    cosine = jnp.where(first, pltpu.roll(table, 128 - MARK_COS, 1), table)
    sine_first = pltpu.roll(table, 128 - MARK_SIN, 1)
    sine_second = pltpu.roll(table, 128 - MARK_SIN + ROT // 2, 1)
    sine = jnp.where(first, -sine_first, sine_second) * sign
    cosine = jnp.where(second & active, cosine, 1.0)
    sine = jnp.where(second & active, sine, 0.0)
    partner = jnp.where(first, pltpu.roll(values, 128 - ROT // 2, 1), pltpu.roll(values, ROT // 2, 1))
    return values * cosine + partner * sine


def deal_kernel(cut, blocks, ids, speed, here, there, triple, near, marks, norms, shifts, lines, flip):
    me, core = ids[0], ids[1]
    width = lines.shape[2]
    for source in range(blocks):
        for who, ref in ((core, here), (1 - core, there)):
            at = pl.multiple_of(source * 2 * cut + who * cut, cut)
            for s in range(3):
                triple[pl.ds(at, cut), s * 128 : (s + 1) * 128] = ref[source, s * cut : (s + 1) * cut, :]
            at = pl.multiple_of(who * cut, cut)
            near[pl.ds(at, cut), source * 128 : (source + 1) * 128] = ref[source, 3 * cut : 4 * cut, :]

    lanes = 128 // blocks
    row = lax.broadcasted_iota(jnp.int32, (128, width), 0)
    lane = lane_of((128, width))
    deal = ((row // lanes == lane // 128) & (row % lanes == lane % lanes)).astype(BF)
    lane = lane_of((16, width)) % 128 // lanes
    flip[...] = jnp.zeros_like(flip)
    for which, ref in enumerate((here, there)):
        total = jnp.zeros((16, width), F32)
        for source in range(blocks):
            small = ref[source, 4 * cut : 4 * cut + 16, :]
            total = total + jnp.where(lane == source, nn(small, deal), 0.0)
            if which == 0:
                small = small.astype(F32)
                flip[source : source + 1, :] = small[10:11] * 256.0 + small[11:12]
                flip[blocks + source : blocks + source + 1, :] = small[12:13]
        lines[which] = total
    norms[:4, :] = lines[0, :4, :]
    norms[4:5, :] = lines[0, 4:5, :] + lines[0, 5:6, :]
    norms[5:, :] = jnp.zeros((3, width), F32)
    shifts[...] = jnp.zeros_like(shifts)
    heads = blocks // 2
    ours = me // heads == core
    for s in range(3):
        at = pl.multiple_of((me % heads + s % 2 * heads) * 128, 128)
        both = [lines[k, 6 + s // 2 : 7 + s // 2, pl.ds(at, 128)] for k in (0, 1)]
        shifts[0:1, s * 128 : (s + 1) * 128] = jnp.where(ours, both[0], both[1])
    units = 2 * width // blocks
    at = pl.multiple_of(me % heads * units, units)
    for k in (0, 1):
        shifts[1:2, k * units : (k + 1) * units] = lines[k, pl.ds(8 + me // heads, 1), pl.ds(at, units)]

    turned = flip[...].T
    lane = lane_of((128, 128))
    row = lax.broadcasted_iota(jnp.int32, (128, 128), 0).astype(F32)
    for q in range(blocks // 4):
        place = jnp.zeros((128, 128), F32)
        for g in range(4):
            b = 4 * q + g
            place = jnp.where(lane // 32 == g, row + b * 128.0 - turned[:, b : b + 1], place)
        angle = place * speed[0:1, :]
        cosine, sine = jnp.cos(angle), jnp.sin(angle)
        for g in range(4):
            b = 4 * q + g
            index = row + b * 128.0
            table = jnp.where(lane == 0, index, 0.0)
            table = jnp.where(lane == 1, jnp.where(turned[:, blocks + b : blocks + b + 1] == 1.0, index, -1.0), table)
            table = jnp.where(lane == 2, turned[:, b : b + 1], table)
            table = jnp.where(lane // 32 == 1, pltpu.roll(cosine, (MARK_COS - g * 32) % 128, 1), table)
            table = jnp.where(lane // 32 == 2, pltpu.roll(sine, (MARK_SIN - g * 32) % 128, 1), table)
            marks[b * 128 : (b + 1) * 128, :] = table


def feed_deal_kernel(blocks, units, expand, shrink, out):
    for k in range(blocks):
        out[k, :units, :] = expand[:, k * units : (k + 1) * units].T
        out[k, units:, :] = shrink[k * units : (k + 1) * units, :]


def pick(i, refs, tile):
    for k, ref in enumerate(refs):

        @pl.when(i == k)
        def _(ref=ref):
            tile[...] = ref[...]


def norm_kernel(r, ids, t0, t1, t2, t3, norms, weight, shifts, marks, feed, stats, mine, tile, table, attend):
    i = pl.program_id(0)
    me, core = ids[0], ids[1]
    pick(i, (t0, t1, t2, t3), tile)
    for half in (0, 1):

        @pl.when(i // 2 == half)
        def _(half=half):
            for q in range(8):
                at = r.natural(me, core, half, (i % 2) * 8 + q)
                table[q * r.chunk : (q + 1) * r.chunk, :] = marks[pl.ds(pl.multiple_of(at, r.chunk), r.chunk), :]

    step = 16
    lane = lane_of((step, 128))

    @pl.loop(0, tile.shape[0] // step, unroll=4)
    def _(j):
        rows = pl.ds(pl.multiple_of(j * step, step), step)
        values = tile[rows, :].astype(F32)
        mean = jnp.mean(values, axis=-1, keepdims=True)
        center = values - mean
        inverse = lax.rsqrt(jnp.mean(center * center, axis=-1, keepdims=True) + EPSILON)
        value = center * inverse
        attend[rows, :] = (value * norms[0:1, :] + norms[2:3, :]).astype(BF)
        feed[rows, :] = (value * norms[1:2, :] + norms[3:4, :]).astype(BF)
        stats[rows, :] = jnp.where(lane == 0, mean, inverse)

    linear = nn(attend[...], weight[...]) + shifts[0:1, :384]
    active = me % 2 == 0
    for s in (0, 1):
        cols = slice(s * 128, (s + 1) * 128)
        mine[:, cols] = turn_lanes(linear[:, cols], table[...], active, 1.0).astype(BF)
    mine[:, 256:] = linear[:, 256:].astype(BF)


def normal_of(tile, stats):
    return (tile.astype(F32) - stats[:, 0:1]) * stats[:, 1:2]


def gather_columns(r, out, low, high, column):
    cols = slice(column * 128, (column + 1) * 128)
    out[:, :128] = low[:, cols]
    for here, there, size in r.pairs():
        out[here : here + size, 128:] = high[there : there + size, cols]


def gather_marks(r, ids, marks, table, line):
    me, core = ids[0], ids[1]
    for w in (0, 1):
        who = core if w == 0 else 1 - core
        for half in (0, 1):
            for q in range(16):
                at = r.natural(me, who, half, q)
                to = w * r.count + half * r.half + q * r.chunk
                table[to : to + r.chunk, :] = marks[pl.ds(pl.multiple_of(at, r.chunk), r.chunk), :]
    for b in range(2 * r.count // 128):
        line[:, b * 128 : (b + 1) * 128] = table[b * 128 : (b + 1) * 128, :].T[:8, :]


def own_rows(r, out, ref, columns=slice(None)):
    for row, place, size in r.x_rows(0):
        out[place : place + size, :] = ref[row : row + size, columns]


def query_kernel(r, scale, ids, a00, a01, a10, a11, grads, marks, attended, keep, send, lines,
                 keys, values, queries, pushes, table, line, mine):
    i = pl.program_id(0)
    me = ids[0]
    count, tile = r.count, r.share // 2

    @pl.when(i == 0)
    def _():
        gather_columns(r, keys.at[:count], a00, a01, 1)
        gather_columns(r, keys.at[count:], a10, a11, 1)
        gather_columns(r, values.at[:count], a00, a01, 2)
        gather_columns(r, values.at[count:], a10, a11, 2)
        for row, place, size in r.x_rows(0):
            queries[place : place + size, :128] = a00[row : row + size, :128]
        for (row, place, size), (there, _, _) in zip(r.x_rows(0), r.x_rows(1)):
            queries[place : place + size, 128:] = a01[there : there + size, :128]
        own_rows(r, pushes, grads)
        gather_marks(r, ids, marks, table, line)
        own_rows(r, mine, table.at[:count])

    rows = pl.ds(pl.multiple_of(i * tile, tile), tile)
    mark = mine[rows, :]
    q_at, q_start = mark[:, 0:1], mark[:, 2:3]
    k_at, k_live = line[0:1, :], line[1:2, :]
    mask = ((k_live >= q_start) & (k_at <= q_at)) | (k_at == q_at)
    scores = jnp.where(mask, nt(queries[rows, :], keys[...]) * scale, NEGATIVE)
    top = jnp.max(scores, axis=-1, keepdims=True)
    weight = jnp.where(mask, jnp.exp(scores - top), 0.0)
    total = jnp.sum(weight, axis=-1, keepdims=True)
    prob = weight * (1.0 / total)
    result = nn(prob.astype(BF), values[...])
    grad = pushes[rows, :]
    delta = jnp.sum(grad.astype(F32) * result, axis=-1, keepdims=True)
    slope = (prob * (nt(grad, values[...]) - delta)).astype(BF)
    back = nn(slope, keys[...]) * scale
    result = result.astype(BF)
    attended[...] = result
    for k, ref in enumerate((keep, send)):
        cols = slice(k * 128, (k + 1) * 128)
        ref[:, :128] = turn_lanes(back[:, cols], mark, me % 2 == k, -1.0).astype(BF)
        ref[:, 128:] = result[:, cols]
    lane = lane_of((tile, 128))
    both = jnp.where(lane == 0, top + jnp.log(total), jnp.where(lane == 1, delta, 0.0))
    for b in range(tile // 128):
        lines[:, b * 128 : (b + 1) * 128] = both[b * 128 : (b + 1) * 128, :].T[:8, :]


def key_kernel(r, scale, ids, a00, a01, a10, a11, grads, other_grads, l00, l01, l10, l11, marks, keep, send,
               queries, pushes, keys, values, table, line, mine, tops):
    i = pl.program_id(0)
    me = ids[0]
    count, tile = r.count, r.share // 2

    @pl.when(i == 0)
    def _():
        gather_columns(r, queries.at[:count], a00, a01, 0)
        gather_columns(r, queries.at[count:], a10, a11, 0)
        pushes[:count, :] = grads[...]
        pushes[count:, :] = other_grads[...]
        for k, out in ((1, keys), (2, values)):
            cols = slice(k * 128, (k + 1) * 128)
            for row, place, size in r.x_rows(0):
                out[place : place + size, :128] = a00[row : row + size, cols]
            for (row, place, size), (there, _, _) in zip(r.x_rows(0), r.x_rows(1)):
                out[place : place + size, 128:] = a01[there : there + size, cols]
        gather_marks(r, ids, marks, table, line)
        own_rows(r, mine, table.at[:count])
        for base, low, high in ((0, l00, l01), (count, l10, l11)):
            for x, ref in ((0, low), (1, high)):
                for row, place, size in r.x_rows(x):
                    tops[:, base + row : base + row + size] = ref[:, place : place + size]

    rows = pl.ds(pl.multiple_of(i * tile, tile), tile)
    mark = mine[rows, :]
    k_at, k_live = mark[:, 0:1], mark[:, 1:2]
    q_at, q_start = line[0:1, :], line[2:3, :]
    mask = ((k_live >= q_start) & (k_at <= q_at)) | (k_at == q_at)
    scores = nt(keys[rows, :], queries[...]) * scale
    prob = jnp.where(mask, jnp.exp(scores - tops[0:1, :]), 0.0)
    grad_values = nn(prob.astype(BF), pushes[...])
    slope = (prob * (nt(values[rows, :], pushes[...]) - tops[1:2, :])).astype(BF)
    back = nn(slope, queries[...]) * scale
    for k, ref in enumerate((keep, send)):
        cols = slice(k * 128, (k + 1) * 128)
        ref[:, :128] = turn_lanes(back[:, cols], mark, me % 2 == k, -1.0).astype(BF)
        ref[:, 128:] = grad_values[:, cols].astype(BF)


def feed_kernel(units, blocks, normed, c0, c1, c2, c3, mine, other, shifts, near, peer,
                act, grad, act_turned, grad_turned, expand, shrink, sums, pushes, push_sums, tile, turned):
    i = pl.program_id(0)

    @pl.when(i == 0)
    def _():
        sums[...] = jnp.zeros_like(sums)
        push_sums[...] = jnp.zeros_like(push_sums)
        turned[:, :128] = near[...].T
        turned[:, 128:] = peer[...].T
        for source in range(blocks):
            cols = slice(source * 128, (source + 1) * 128)
            for at, ref in ((0, mine), (units, other)):
                expand[at : at + units, cols] = ref[source, :units, :]
                shrink[at : at + units, cols] = ref[source, units:, :]

    pick(i, (c0, c1, c2, c3), tile)
    pushes[...] = nn(tile[...], turned[...]).astype(BF)
    expanded = nt(normed[...], expand[...]) + shifts[1:2, : 2 * units]
    activated, bend = gelu_and_slope(expanded)
    activated = activated.astype(BF)
    act[...] = activated
    act_turned[...] = activated.T
    slope = (bend * nt(tile[...], shrink[...])).astype(BF)
    grad[...] = slope
    grad_turned[...] = slope.T
    sums[0:1, :] += jnp.sum(slope.astype(F32), axis=0, keepdims=True)
    push_sums[0:1, :] += jnp.sum(tile[...].astype(F32), axis=0, keepdims=True)


def by_quarter(left, quarters):
    size = quarters[0].shape[0]
    total = nn(left[:, :size], quarters[0][...])
    for k in range(1, len(quarters)):
        total = total + nn(left[:, k * size : (k + 1) * size], quarters[k][...])
    return total


def outer_kernel(units, grad_turned, act_turned, normed, c0, c1, c2, c3, *rest):
    out = rest[-1]
    for k in (0, 1):
        result = by_quarter(act_turned, (c0, c1, c2, c3)) if k else nn(grad_turned[...], normed[...])
        for b in range(WIDE // 128):
            lanes = slice(b * 128, (b + 1) * 128)
            rows = slice(k * units, (k + 1) * units)
            part = result[:, lanes]
            if len(rest) > 1:
                part = part + rest[0][b, rows, :].astype(F32)
            out[b, rows, :] = part.astype(BF)


def branch_kernel(r, act, attended, shrink, near, peer, o0, o1, o2, o3):
    outs = (o0, o1, o2, o3)
    size = r.count // 4
    extra = nn(attended[:, :128], near[...]) + nn(attended[:, 128:], peer[...])
    for k in range(4):
        result = nn(act[k * size : (k + 1) * size, :], shrink[...])
        covered = False
        for row, place, length in r.x_rows(0):
            if row == k * size:
                outs[k][:length, :] = (result[:length] + extra[place : place + length]).astype(BF)
                if length < size:
                    outs[k][length:, :] = result[length:].astype(BF)
                covered = True
        if not covered:
            outs[k][...] = result.astype(BF)


def inputs_kernel(r, keep1, keep2, got1, got2, grad, t0, t1, t2, t3, stats, triple, expand, gains, cotangent_sums, unit_sums,
                  o0, o1, o2, o3, linear, near, sums, line_sums):
    j = pl.program_id(0)
    size = r.count // 4

    @pl.when(j == 0)
    def _():
        for x, one, two in ((0, keep1, keep2), (1, got1, got2)):
            for row, place, length in r.x_rows(x):
                linear[row : row + length, :128] = one[place : place + length, :128]
                linear[row : row + length, 128:] = two[place : place + length, :]
                near[row : row + length, :] = one[place : place + length, 128:]
        line_sums[...] = jnp.zeros_like(line_sums)
        line_sums[0:1, :384] = jnp.sum(linear[...].astype(F32), axis=0, keepdims=True)

    sums[...] = jnp.zeros_like(sums)
    for k, (ref, tokens) in enumerate(((o0, t0), (o1, t1), (o2, t2), (o3, t3))):
        rows = slice(k * size, (k + 1) * size)
        attend = nt(linear[rows, :], triple[...])
        feed = nn(grad[rows, :], expand[...])
        value = normal_of(tokens[...], stats[rows, :])
        sums[0:1, :] += jnp.sum(value * attend, axis=0, keepdims=True)
        sums[1:2, :] += jnp.sum(value * feed, axis=0, keepdims=True)
        sums[2:3, :] += jnp.sum(attend, axis=0, keepdims=True)
        sums[3:4, :] += jnp.sum(feed, axis=0, keepdims=True)
        ref[...] = (gains[0:1, :] * attend + gains[1:2, :] * feed).astype(BF)
    sums[4:5, :] = cotangent_sums[0:1, :]
    for k in (0, 1):

        @pl.when(j == k)
        def _(k=k):
            sums[5:6, :] = line_sums[0:1, k * WIDE : (k + 1) * WIDE]
            sums[6:7, :] = unit_sums[0:1, k * WIDE : (k + 1) * WIDE]


def small_kernel(blocks, units, ids, mine, other, out, lines):
    me, core = ids[0], ids[1]
    width = lines.shape[1]
    heads, lanes = blocks // 2, 128 // blocks
    lines[...] = jnp.zeros_like(lines)
    lines[0:5, :] = mine[0:5, :] + other[0:5, :]
    ours = jnp.where(me // heads == core, 1.0, 0.0)
    for s in range(3):
        at = pl.multiple_of((me % heads + s % 2 * heads) * 128, 128)
        cols = slice(s * 128, (s + 1) * 128)
        lines[6 + s // 2 : 7 + s // 2, pl.ds(at, 128)] = (mine[5:6, cols] + other[5:6, cols]) * ours
    at = pl.multiple_of(me % heads * units, units)
    total = mine[6:7, :units] + other[6:7, units : 2 * units]
    for k in (0, 1):

        @pl.when(me // heads == k)
        def _(k=k):
            lines[8 + k : 9 + k, pl.ds(at, units)] = total

    row = lax.broadcasted_iota(jnp.int32, (width, 128), 0)
    lane = lane_of((width, 128))
    deal = ((lane // lanes == row // 128) & (lane % lanes == row % lanes)).astype(BF)
    value = lines[...]
    high = value.astype(BF)
    low = (value - high.astype(F32)).astype(BF)
    lane = lane_of((16, width)) % 128 // lanes
    line = lax.broadcasted_iota(jnp.int32, (16, width), 0)
    for b in range(blocks):
        sent = (lane == b) & ((line != 4) | (me == b))
        for k, part in enumerate((high, low)):
            part = jnp.where(sent, part.astype(F32), 0.0).astype(BF)
            out[b, k * 16 : (k + 1) * 16, :] = nn(part, deal).astype(BF)


def fold_kernel(keep1, got1, keep2, got2, one, one_send, two, two_send):
    for keep, got, outs in ((keep1, got1, (one, one_send)), (keep2, got2, (two, two_send))):
        half = outs[0].shape[0]
        for k, out in enumerate(outs):
            rows = slice(k * half, (k + 1) * half)
            out[...] = (keep[rows, :].astype(F32) + got[rows, :].astype(F32)).astype(BF)


def by_z_kernel(chunk, one, one_got, two, two_got, *outs):
    for half, (mine, got) in enumerate(((one, one_got), (two, two_got))):
        for z, out in enumerate(outs):
            rows = slice(z * chunk, (z + 1) * chunk)
            value = mine[rows, :].astype(F32) + got[rows, :].astype(F32)
            out[half * chunk : (half + 1) * chunk, :] = value.astype(BF)


def line_outer_kernel(cut, ids, linear, near, t0, t1, t2, t3, stats, norms, c0, c1, c2, c3,
                      keep, give, turned, near_turned, normed, result):
    core = ids[1]

    @pl.when(pl.program_id(0) == 0)
    def _():
        turned[...] = linear[...].T
        near_turned[...] = near[...].T

    size = t0.shape[0]
    for k, tokens in enumerate((t0, t1, t2, t3)):
        rows = slice(k * size, (k + 1) * size)
        value = normal_of(tokens[...], stats[rows, :])
        normed[rows, :] = (value * norms[0:1, :] + norms[2:3, :]).astype(BF)
    result[:384, :] = nn(turned[...], normed[...])
    result[384:, :] = by_quarter(near_turned, (c0, c1, c2, c3))
    for who, out in ((core, keep), (1 - core, give)):
        for s in range(4):
            at = pl.multiple_of(s * 2 * cut + who * cut, cut)
            for b in range(WIDE // 128):
                part = result[pl.ds(at, cut), b * 128 : (b + 1) * 128]
                out[b, s * cut : (s + 1) * cut, :] = part.astype(out.dtype)


def unpack_kernel(cut, heads, ids, mine, other, whole, triple, outward, small, pair):
    core = ids[1]
    for k in range(heads):
        for s in range(4):
            for who, ref in ((core, mine), (1 - core, other)):
                pair[pl.ds(pl.multiple_of(who * cut, cut), cut), :] = ref[k, s * cut : (s + 1) * cut, :].astype(F32)
            if s < 3:
                triple[s, :, k * 128 : (k + 1) * 128] = pair[...].T
            else:
                outward[k * 128 : (k + 1) * 128, :] = pair[...]
    total = jnp.zeros(small.shape, F32)
    for b in range(2 * heads):
        for k in (0, 1):
            at = 4 * cut + 16 * k
            total = total + whole[b, at : at + 16, :].astype(F32)
    small[...] = total


def feed_unpack_kernel(units, got, expand, shrink):
    for k in range(got.shape[0]):
        rows = slice(k * units, (k + 1) * units)
        expand[:, rows] = got[k, :units, :].astype(F32).T
        shrink[rows, :] = got[k, units:, :].astype(F32)


def join(*values):
    return lax.optimization_barrier(values)


def body(
    tokens,
    w_qkv,
    b_qkv,
    w_out,
    b_out,
    w_in,
    b_in,
    w_out2,
    b_out2,
    norm_gain,
    norm_shift,
    doc_start,
    live,
    cotangent,
):
    blocks = lax.axis_size("blk")
    cores = lax.axis_size("tp")
    me, core = lax.axis_index("blk"), lax.axis_index("tp")
    ids = jnp.stack([me, core]).astype(jnp.int32)
    rows, width = tokens.shape
    depth = w_in.shape[0]
    r = Rows(blocks, cores, rows)
    part, count, share = r.part, r.count, r.share
    quarter = count // 4
    units = w_in.shape[1] // blocks
    cut = depth // cores
    own_heads = HEADS // cores * 2
    scale = 1.0 / math.sqrt(HEAD)
    masks_z = [4 * i for i in range(1, blocks // 4)]
    grid = (width // WIDE,)

    once = pl.Buffered(1)

    def tiled(columns):
        return pl.BlockSpec((quarter, columns), lambda i: (i, 0))

    def across(lines):
        return pl.BlockSpec((lines, WIDE), lambda j: (0, j))

    def fixed(value):
        return pl.BlockSpec(value.shape, lambda i: (0,) * value.ndim, pipeline_mode=once)

    def fixed_shape(*shape):
        return pl.BlockSpec(shape, lambda i: (0,) * len(shape))

    def packed_rows(value, lines):
        flat = value.reshape(-1)
        return jnp.pad(flat, (0, lines * 128 - flat.size)).reshape(lines, 128)

    small = jnp.concatenate(
        [
            packed_rows(norm_gain, 2),
            packed_rows(norm_shift, 2),
            packed_rows(b_out, 1),
            packed_rows(b_out2, 1),
            packed_rows(b_qkv, 2),
            packed_rows(b_in, 2),
            jnp.stack([doc_start // 256, doc_start % 256, live]).astype(BF),
            jnp.zeros((3, 128), BF),
        ]
    )

    def over_z(value):
        return [from_peer(value, mask) for mask in masks_z]

    def halves(pieces):
        one = jnp.concatenate([value[: r.chunk] for value in pieces])
        two = jnp.concatenate([value[r.chunk :] for value in pieces])
        return one, two

    my_tokens = lax.dynamic_slice_in_dim(tokens, core * part, part, 0)
    my_cotangent = lax.dynamic_slice_in_dim(cotangent, core * part, part, 0)
    triple = w_qkv.reshape(3, cores, cut, own_heads, 128).transpose(1, 3, 0, 2, 4)
    triple = triple.reshape(cores, own_heads, 3 * cut, 128)
    outward = w_out.reshape(own_heads, cores, cut, 128).transpose(1, 0, 2, 3)
    dealt = jnp.concatenate([triple, outward], axis=2)
    keep = lax.dynamic_index_in_dim(dealt, core, 0, keepdims=False)
    give = lax.dynamic_index_in_dim(dealt, 1 - core, 0, keepdims=False)
    feed_deal = run_kernel(
        lambda *refs: feed_deal_kernel(blocks, units, *refs),
        [((blocks, 2 * units, depth), BF)],
        ins=[VMEM, VMEM],
        name="feed_deal",
        moved=4e6,
    )(w_in, w_out2)
    tokens_z = join(my_tokens, *over_z(my_tokens))
    keep, got, feed_deal, my_cotangent, *tokens_z = join(keep, swap_cores(give), feed_deal, my_cotangent, *tokens_z)

    heads_low, heads_high = by_core(core, keep, got)
    deal = jnp.concatenate(
        [
            jnp.concatenate([heads_low, heads_high]),
            jnp.broadcast_to(small, (blocks,) + small.shape),
        ],
        axis=1,
    )
    here = lax.all_to_all(deal, "blk", 0, 0, tiled=True)
    one, two = halves(tokens_z)
    cotangent_z = over_z(my_cotangent)
    one, one_y, two, two_x = join(one, from_peer(one, 2), two, from_peer(two, 1))

    one, two = jnp.concatenate([one, one_y]), jnp.concatenate([two, two_x])
    mine_one, mine_two = halves(join(my_cotangent, *cotangent_z))
    here, feed_deal, one, one_x, two, two_y, mine_one, mine_y, mine_two, mine_x = join(
        here,
        feed_deal,
        one,
        from_peer(one, 1),
        two,
        from_peer(two, 2),
        mine_one,
        from_peer(mine_one, 2),
        mine_two,
        from_peer(mine_two, 1),
    )
    all_tokens = [one, one_x, two, two_y]

    one, two = jnp.concatenate([mine_one, mine_y]), jnp.concatenate([mine_two, mine_x])
    here, there, feed_deal = join(here, swap_cores(here), feed_deal)
    feed_mine = lax.all_to_all(feed_deal, "blk", 0, 0, tiled=True)
    steps = jnp.arange(ROT // 2, dtype=F32)
    speed = jnp.tile(10000.0 ** (-2.0 * steps / ROT), 4).reshape(1, 128)
    w_triple, w_near, marks, norms, shifts = run_kernel(
        lambda *refs: deal_kernel(cut, blocks, *refs),
        [
            ((width, 384), BF),
            ((128, width), BF),
            ((blocks * rows, 128), F32),
            ((8, width), F32),
            ((8, 512), F32),
        ],
        ins=[SMEM, VMEM, VMEM, VMEM],
        scratch=[pltpu.VMEM((2, 16, width), F32), pltpu.VMEM((128, 128), F32)],
        name="deal",
        moved=8e6,
    )(ids, speed, here, there)
    normed_feed, stats, mine = run_kernel(
        lambda *refs: norm_kernel(r, *refs),
        [((count, width), BF), ((count, 128), F32), ((count, 384), BF)],
        grid=(4,),
        ins=[SMEM] + [fixed(t) for t in all_tokens] + [fixed(norms), fixed(w_triple), fixed(shifts), fixed(marks)],
        out_specs=[tiled(width), tiled(128), tiled(384)],
        scratch=[pltpu.VMEM((quarter, width), BF), pltpu.VMEM((quarter, 128), F32), pltpu.VMEM((quarter, width), BF)],
        flops=2 * count * width * 384,
        name="norm",
        moved=22e6,
    )(ids, *all_tokens, norms, w_triple, shifts, marks)
    w_peer = from_peer(w_near, 1)
    mine, one, one_x, two, two_y = join(mine, one, from_peer(one, 1), two, from_peer(two, 2))

    peer, mine_there = from_peer(mine, 1), swap_cores(mine)
    all_cotangent = [one, one_x, two, two_y]
    feed_mine, *all_cotangent = join(feed_mine, *all_cotangent)

    feed_mine, feed_other = join(feed_mine, swap_cores(feed_mine))

    turned = pl.BlockSpec((2 * units, quarter), lambda i: (0, i))
    act, grad, act_turned, grad_turned, w_expand, w_shrink, unit_sums, grads, cotangent_sums = run_kernel(
        lambda *refs: feed_kernel(units, blocks, *refs),
        [((count, 2 * units), BF)] * 2
        + [((2 * units, count), BF)] * 2
        + [((2 * units, width), BF)] * 2
        + [((8, 2 * units), F32), ((count, 256), BF), ((8, width), F32)],
        grid=(4,),
        ins=[tiled(width)]
        + [fixed(t) for t in all_cotangent]
        + [fixed(feed_mine), fixed(feed_mine), fixed(shifts), fixed(w_near), fixed(w_peer)],
        out_specs=[tiled(2 * units)] * 2
        + [turned] * 2
        + [fixed_shape(2 * units, width)] * 2
        + [fixed_shape(8, 2 * units), tiled(256), fixed_shape(8, width)],
        scratch=[pltpu.VMEM((quarter, width), BF), pltpu.VMEM((width, 256), BF)],
        flops=8 * count * width * units,
        name="feed",
        moved=20e6,
    )(normed_feed, *all_cotangent, feed_mine, feed_other, shifts, w_near, w_peer)
    mine, peer, mine_there, act_turned, grad_turned = join(mine, peer, mine_there, act_turned, grad_turned)

    dealt_spec = pl.BlockSpec((WIDE // 128, 2 * units, 128), lambda j: (j, 0, 0))

    def outer(half, *extra):
        some = pl.BlockSpec((units, count), lambda j: (half, 0))
        return run_kernel(
            lambda *refs: outer_kernel(units, *refs),
            [((blocks, 2 * units, 128), BF)],
            grid=grid,
            ins=[some, some, across(count)] + [across(quarter)] * 4 + [dealt_spec] * len(extra),
            out_specs=[dealt_spec],
            flops=4 * count * width * units,
            name="outer",
            moved=12e6,
        )(grad_turned, act_turned, normed_feed, *all_cotangent, *extra)

    peer_there, feed_sent, grads = join(swap_cores(peer), outer(1), grads)

    tile = share // 2
    half_tile = lambda columns: pl.BlockSpec((tile, columns), lambda i: (i, 0))
    line_tile = pl.BlockSpec((8, tile), lambda i: (0, i))
    four = [mine, peer, mine_there, peer_there]
    common = [
        pltpu.VMEM((2 * count, 256), BF),
        pltpu.VMEM((2 * count, 256), BF),
        pltpu.VMEM((share, 256), BF),
        pltpu.VMEM((share, 256), BF),
        pltpu.VMEM((2 * count, 128), F32),
        pltpu.VMEM((8, 2 * count), F32),
        pltpu.VMEM((share, 128), F32),
    ]
    attended, keep1, send1, lines = run_kernel(
        lambda *refs: query_kernel(r, scale, *refs),
        [((share, 256), BF)] * 3 + [((8, share), F32)],
        grid=(2,),
        ins=[SMEM] + [fixed(mine)] * 4 + [fixed(grads), fixed(marks)],
        out_specs=[half_tile(256)] * 3 + [line_tile],
        scratch=common,
        flops=8 * share * 2 * count * 256,
        name="query",
        moved=6e6,
    )(ids, *four, grads, marks)
    grads_there, attended, send1, lines = join(swap_cores(grads), attended, send1, lines)
    feed_got = swap_cores(feed_sent)

    diagonal = [(2 * b + c, 2 * (b ^ 1) + 1 - c) for b in range(blocks) for c in (0, 1)]
    lines_peer, lines_there = from_peer(lines, 1), swap_cores(lines)
    lines_far = lax.ppermute(lines, ("blk", "tp"), diagonal)
    feed_grads = outer(0, feed_got)
    feed_grads, lines, lines_peer, lines_there, lines_far = join(feed_grads, lines, lines_peer, lines_there, lines_far)

    keep2, send2 = run_kernel(
        lambda *refs: key_kernel(r, scale, *refs),
        [((share, 256), BF)] * 2,
        grid=(2,),
        ins=[SMEM] + [fixed(mine)] * 4 + [fixed(grads)] * 2 + [fixed(lines)] * 4 + [fixed(marks)],
        out_specs=[half_tile(256)] * 2,
        scratch=common + [pltpu.VMEM((8, 2 * count), F32)],
        flops=8 * share * 2 * count * 256,
        name="key",
        moved=6e6,
    )(ids, *four, grads, grads_there, lines, lines_peer, lines_there, lines_far, marks)
    feed_grads, attended = join(feed_grads, attended)
    feed_dealt = lax.all_to_all(feed_grads, "blk", 0, 0, tiled=True)
    branches = run_kernel(
        lambda *refs: branch_kernel(r, *refs),
        [((quarter, width), BF)] * 4,
        grid=grid,
        ins=[fixed(act), fixed(attended), across(2 * units), across(128), across(128)],
        out_specs=[across(quarter)] * 4,
        flops=2 * count * width * (2 * units + 128),
        name="branch",
        moved=9e6,
    )(act, attended, w_shrink, w_near, w_peer)
    got1, got2, *branches = join(from_peer(send1, 1), from_peer(send2, 1), *branches)
    mixed_one, mixed_two = from_peer(branches[1], 1), from_peer(branches[3], 2)

    def fold(*refs):
        return run_kernel(
            fold_kernel,
            [((quarter // 2, width), BF)] * 4,
            grid=grid,
            ins=[across(quarter)] * 4,
            out_specs=[across(quarter // 2)] * 4,
            name="fold",
            moved=6e6,
        )(*refs)

    def by_z(*refs):
        return run_kernel(
            lambda *refs: by_z_kernel(r.chunk, *refs),
            [((part, width), BF)] * (1 + len(masks_z)),
            grid=grid,
            ins=[across(quarter // 2)] * 4,
            out_specs=[across(part)] * (1 + len(masks_z)),
            name="by_z",
            moved=3e6,
        )(*refs)

    def total(pieces, got):
        value = pieces[0].astype(F32)
        for piece in got:
            value = value + piece.astype(F32)
        return value

    def pieces_over_z(pieces):
        return [from_peer(piece, mask) for piece, mask in zip(pieces[1:], masks_z)]

    *combined, grad_linear, attended_near, sums, _ = run_kernel(
        lambda *refs: inputs_kernel(r, *refs),
        [((quarter, width), BF)] * 4 + [((count, 384), BF), ((count, 128), BF), ((8, width), F32), ((8, 512), F32)],
        grid=grid,
        ins=[fixed(keep1)] * 4
        + [fixed(grad)]
        + [across(quarter)] * 4
        + [fixed(stats), pl.BlockSpec((WIDE, 384), lambda j: (j, 0)), across(2 * units)]
        + [across(8), across(8), fixed(unit_sums)],
        out_specs=[across(quarter)] * 4
        + [fixed_shape(count, 384), fixed_shape(count, 128), across(8), fixed_shape(8, 512)],
        flops=2 * count * width * (384 + 2 * units),
        name="inputs",
        moved=16e6,
    )(keep1, keep2, got1, got2, grad, *all_tokens, stats, w_triple, w_expand, norms, cotangent_sums, unit_sums)
    grad_linear, sums, *combined = join(grad_linear, sums, *combined)

    got_one, got_two = from_peer(combined[1], 1), from_peer(combined[3], 2)
    line_spec = pl.BlockSpec((WIDE // 128, 4 * cut, 128), lambda j: (j, 0, 0))
    keep, give = run_kernel(
        lambda *refs: line_outer_kernel(cut, *refs),
        [((blocks, 4 * cut, 128), F32), ((blocks, 4 * cut, 128), BF)],
        grid=grid,
        ins=[SMEM, fixed(grad_linear), fixed(attended_near)]
        + [across(quarter)] * 4
        + [fixed(stats), across(8)]
        + [across(quarter)] * 4,
        out_specs=[line_spec] * 2,
        scratch=[
            pltpu.VMEM((384, count), BF),
            pltpu.VMEM((128, count), BF),
            pltpu.VMEM((count, WIDE), BF),
            pltpu.VMEM((512, WIDE), F32),
        ],
        flops=2 * count * width * 512,
        name="line_outer",
        moved=12e6,
    )(ids, grad_linear, attended_near, *all_tokens, stats, norms, *all_cotangent)
    mixed_one, mixed_two, keep, give, sums, sums_other = join(
        mixed_one, mixed_two, keep, give, sums, swap_cores(sums)
    )

    one, one_send, two, two_send = fold(branches[0], mixed_one, branches[2], mixed_two)
    small = run_kernel(
        lambda *refs: small_kernel(blocks, units, *refs),
        [((blocks, 32, 128), BF)],
        ins=[SMEM, VMEM, VMEM],
        scratch=[pltpu.VMEM((16, width), F32)],
        name="small",
        moved=1e6,
    )(ids, sums, sums_other)
    got, small, one, one_send, two, two_send = join(swap_cores(give), small, one, one_send, two, two_send)
    mixed_one, mixed_two = from_peer(one_send, 2), from_peer(two_send, 1)
    dealt = jnp.concatenate([(keep + got.astype(F32)).astype(BF), small], axis=1)
    dealt, feed_dealt = join(dealt, feed_dealt)
    dealt = lax.all_to_all(dealt, "blk", 0, 0, tiled=True)
    expand_grad, shrink_grad = run_kernel(
        lambda *refs: feed_unpack_kernel(units, *refs),
        [(w_in.shape, F32), (w_out2.shape, F32)],
        grid=(4,),
        ins=[pl.BlockSpec((blocks // 4, 2 * units, 128), lambda k: (k, 0, 0))],
        out_specs=[
            pl.BlockSpec((depth, units * blocks // 4), lambda k: (0, k)),
            pl.BlockSpec((units * blocks // 4, depth), lambda k: (k, 0)),
        ],
        name="feed_unpack",
        moved=6e6,
    )(feed_dealt)
    got_one, got_two, mixed_one, mixed_two, expand_grad, shrink_grad = join(
        got_one, got_two, mixed_one, mixed_two, expand_grad, shrink_grad
    )
    mixed_pieces = by_z(one, mixed_one, two, mixed_two)
    one, one_send, two, two_send, *mixed_pieces = join(
        *fold(combined[0], got_one, combined[2], got_two), *mixed_pieces
    )
    mixed_got = pieces_over_z(mixed_pieces)
    got_one, got_two = join(from_peer(one_send, 2), from_peer(two_send, 1))

    joined = join(*by_z(one, got_one, two, got_two), *mixed_got)
    pieces, mixed_got = joined[: 1 + len(masks_z)], joined[1 + len(masks_z) :]
    combined_got = pieces_over_z(pieces)

    def whole_block(value):
        return jnp.concatenate(by_core(core, value, swap_cores(value)))

    my_inputs = my_tokens.astype(F32)
    mixed = whole_block((my_inputs + total(mixed_pieces, mixed_got) + norms[4:5, :]).astype(BF))
    dealt, mixed = join(dealt, mixed)
    keep = lax.dynamic_slice_in_dim(dealt, core * own_heads, own_heads, 0)
    give = lax.dynamic_slice_in_dim(dealt, (1 - core) * own_heads, own_heads, 0)
    triple_grad, output_grad, small = run_kernel(
        lambda *refs: unpack_kernel(cut, own_heads, *refs),
        [((3, depth, own_heads * 128), F32), ((own_heads * 128, depth), F32), ((16, 128), F32)],
        ins=[SMEM, VMEM, VMEM, VMEM],
        scratch=[pltpu.VMEM((128, 128), F32)],
        name="unpack",
        moved=4e6,
    )(ids, keep, swap_cores(give), dealt)
    small = small.reshape(16, 16, -1)
    residual_grad = small[4]
    small, triple_grad, output_grad, *combined_got = join(small, triple_grad, output_grad, *combined_got)

    combined_sum = total(pieces, combined_got)
    my_center = my_inputs - jnp.mean(my_inputs, axis=-1, keepdims=True)
    my_inverse = lax.rsqrt(jnp.mean(my_center * my_center, axis=-1, keepdims=True) + EPSILON)
    my_normal = my_center * my_inverse
    my_grad = my_inverse * (
        combined_sum
        - jnp.mean(combined_sum, axis=-1, keepdims=True)
        - my_normal * jnp.mean(combined_sum * my_normal, axis=-1, keepdims=True)
    )
    tokens_grad = whole_block((my_cotangent.astype(F32) + my_grad).astype(BF))
    return (
        mixed,
        tokens_grad,
        triple_grad,
        small[6:8].reshape(32, -1)[:24].reshape(b_qkv.shape),
        output_grad,
        residual_grad,
        expand_grad,
        small[8:10].reshape(b_in.shape),
        shrink_grad,
        residual_grad,
        small[0:2],
        small[2:4],
    )


def solution(mesh):
    placed = (
        P("blk", None),
        P(None, "blk", "tp"),
        P(None, "tp", "blk"),
        P("tp", "blk"),
        P(None, "blk"),
        P("blk", "tp"),
        P("tp", "blk"),
        P("tp", "blk"),
        P(None, "blk"),
        P(None, None, "blk"),
        P(None, None, "blk"),
        P("blk"),
        P("blk"),
        P("blk", None),
    )
    two_to_a_head = mesh.shape["blk"] == 2 * HEADS
    return jax.shard_map(
        body if two_to_a_head else general_body,
        mesh=mesh,
        in_specs=placed,
        out_specs=(
            P("blk", None),
            P("blk", None),
            P(None, "blk", "tp"),
            P(None, "tp", "blk"),
            P("tp", "blk"),
            P(None, "blk"),
            P("blk", "tp"),
            P("tp", "blk"),
            P("tp", "blk"),
            P(None, "blk"),
            P(None, None, "blk"),
            P(None, None, "blk"),
        ),
        check_vma=False,
    )
```
